32 devices in a mesh: dp: 4 (over x, core), chan: 8 (over z, y).
Axes of the slice: x: 2, y: 2, z: 4, core: 2. Of those that a mesh axis runs over, the one named last changes fastest.
Arguments:
- patches: float32 [4, 93312, 144], P('dp', 'chan'), may hold values from -6 to 6
- class_in: float32 [4, 128, 144], P('dp', 'chan'), may hold values from -6 to 6
- conv_weight: float32 [288, 9], P('chan')
- conv_bias: float32 [288], P('chan')
- head_weight: float32 [144, 288], P(None, 'chan')
- head_bias: float32 [288], P('chan')
- first_conv_w: float32 [288, 9], P('chan'), may hold values from -224 to 224
- first_conv_b: float32 [288], P('chan'), may hold values from -224 to 224
- first_head_w: float32 [144, 288], P(None, 'chan'), may hold values from -16 to 16
- first_head_b: float32 [288], P('chan'), may hold values from -16 to 16
- second_conv_w: float32 [288, 9], P('chan'), may hold values from 100.352 to 401.408
- second_conv_b: float32 [288], P('chan'), may hold values from 100.352 to 401.408
- second_head_w: float32 [144, 288], P(None, 'chan'), may hold values from 0.512 to 2.048
- second_head_b: float32 [288], P('chan'), may hold values from 0.512 to 2.048
- average_conv_w: float32 [288, 9], P('chan'), may hold values from -5 to 5
- average_conv_b: float32 [288], P('chan'), may hold values from -6 to 6
- average_head_w: float32 [144, 288], P(None, 'chan'), may hold values from -3 to 3
- average_head_b: float32 [288], P('chan'), may hold values from -6 to 6
- pooled_cot: float32 [4, 25088, 288], P('dp', 'chan'), may hold values from -6 to 6
- class_cot: float32 [4, 128, 288], P('dp', 'chan'), may hold values from -6 to 6
Outputs:
- pooled: float32 [4, 25088, 288], P('dp', 'chan')
- class_out: float32 [4, 128, 288], P('dp', 'chan')
- patches_grad: float32 [4, 93312, 144], P('dp', 'chan')
- class_grad: float32 [4, 128, 144], P('dp', 'chan')
- new_first_conv_w: float32 [288, 9], P('chan')
- new_second_conv_w: float32 [288, 9], P('chan')
- new_conv_w: float32 [288, 9], P('chan')
- new_average_conv_w: float32 [288, 9], P('chan')
- new_first_conv_b: float32 [288], P('chan')
- new_second_conv_b: float32 [288], P('chan')
- new_conv_b: float32 [288], P('chan')
- new_average_conv_b: float32 [288], P('chan')
- new_first_head_w: float32 [144, 288], P(None, 'chan')
- new_second_head_w: float32 [144, 288], P(None, 'chan')
- new_head_w: float32 [144, 288], P(None, 'chan')
- new_average_head_w: float32 [144, 288], P(None, 'chan')
- new_first_head_b: float32 [288], P('chan')
- new_second_head_b: float32 [288], P('chan')
- new_head_b: float32 [288], P('chan')
- new_average_head_b: float32 [288], P('chan')
- trust_ratios: float32 [4], replicated
The draws below stay inside these ranges and needn't reach their ends.
All inputs are finite; a program needn't handle non-finite values.
Results may differ from the reference program's by a relative error of at most 0.0003.
Values sent between devices are 32-bit elements; how exact they have to be, the bound alone decides.
No kernel may reach another device: no remote copies, remote signals or barrier semaphores. Data moves between devices by JAX's collectives and lax.ppermute only.
A program may use at most 512 MiB of HBM per device.

```python
import math
import jax
import jax.numpy as jnp
from jax import lax

CIN = 144
COUT = 288
GRID = 27
TAPS = 9
OUTG = 14
IMG_GRP = 128
N_DP = 4


def rising_draw(key, outer, count, scale):
    base = jnp.clip(jax.random.normal(key, (outer, count), jnp.float32), -4.0, 4.0)
    spread = 3.0
    steps = jnp.arange(count, dtype=jnp.float32) / float(max(count - 1, 1))
    return base * scale * (1.0 + (spread - 1.0) * steps)


def draw_conv_weight(key, part):
    return rising_draw(jax.random.fold_in(key, 11), TAPS, COUT, 0.17).T


def draw_conv_bias(key, part):
    return rising_draw(jax.random.fold_in(key, 12), 1, COUT, 0.25).reshape(COUT)


def draw_head_weight(key, part):
    return rising_draw(jax.random.fold_in(key, 13), CIN, COUT, 0.045)


def draw_head_bias(key, part):
    return rising_draw(jax.random.fold_in(key, 14), 1, COUT, 0.25).reshape(COUT)


def steps_of(stream_key, extent, cuts, low, top_value):
    factor_of = 1.0
    for dim, shards_of in cuts:
        heights = jax.random.uniform(jax.random.fold_in(jax.random.fold_in(stream_key, 6), dim), (shards_of,), jnp.float32, low / len(cuts), top_value / len(cuts))
        factor_of = factor_of * jnp.repeat(jnp.exp(heights), extent[dim] // shards_of).reshape((-1,) + (1,) * (len(extent) - 1 - dim))
    return factor_of


def noise(key, shape, scale, limit, shards=(), kind=jnp.bfloat16):
    entries = scale * jax.random.normal(key, shape, jnp.float32)
    if shards:
        entries = entries * steps_of(key, shape, shards, -0.22, 0.18)
    return jnp.clip(entries, -limit, limit).astype(kind)


def setup_inputs(seed: int = 0) -> dict:
    arg_keys = jax.random.split(jax.random.key(seed), 21)
    return {
        "patches": noise(arg_keys[0], (N_DP, GRID * GRID * IMG_GRP, CIN), 1.0, 6.0, ((0, 4), (1, 8)), jnp.float32),
        "class_in": noise(arg_keys[1], (N_DP, IMG_GRP, CIN), 1.0, 6.0, ((0, 4), (1, 8)), jnp.float32),
        "conv_weight": draw_conv_weight(jax.random.fold_in(arg_keys[20], 71), 0),
        "conv_bias": draw_conv_bias(jax.random.fold_in(arg_keys[20], 71), 0),
        "head_weight": draw_head_weight(jax.random.fold_in(arg_keys[20], 71), 0),
        "head_bias": draw_head_bias(jax.random.fold_in(arg_keys[20], 71), 0),
        "first_conv_w": noise(arg_keys[6], (COUT, TAPS), (0.11 * (N_DP * IMG_GRP * OUTG * OUTG) ** 0.5), 224.0, ((0, 8),), jnp.float32),
        "first_conv_b": noise(arg_keys[7], (COUT,), (0.11 * (N_DP * IMG_GRP * OUTG * OUTG) ** 0.5), 224.0, ((0, 8),), jnp.float32),
        "first_head_w": noise(arg_keys[8], (CIN, COUT), (0.11 * (N_DP * IMG_GRP) ** 0.5), 16.0, ((1, 8),), jnp.float32),
        "first_head_b": noise(arg_keys[9], (COUT,), (0.11 * (N_DP * IMG_GRP) ** 0.5), 16.0, ((0, 8),), jnp.float32),
        "second_conv_w": jnp.clip(jnp.exp(math.log(401.408) - 1.3862944 * jax.random.uniform(arg_keys[10], (COUT, TAPS), jnp.float32) ** steps_of(arg_keys[10], (COUT, TAPS), ((0, 8),), -0.2, 0.2)), 100.352, 401.408),
        "second_conv_b": jnp.clip(jnp.exp(math.log(401.408) - 1.3862944 * jax.random.uniform(arg_keys[11], (COUT,), jnp.float32) ** steps_of(arg_keys[11], (COUT,), ((0, 8),), -0.2, 0.2)), 100.352, 401.408),
        "second_head_w": jnp.clip(jnp.exp(math.log(2.048) - 1.3862944 * jax.random.uniform(arg_keys[12], (CIN, COUT), jnp.float32) ** steps_of(arg_keys[12], (CIN, COUT), ((1, 8),), -0.2, 0.2)), 0.512, 2.048),
        "second_head_b": jnp.clip(jnp.exp(math.log(2.048) - 1.3862944 * jax.random.uniform(arg_keys[13], (COUT,), jnp.float32) ** steps_of(arg_keys[13], (COUT,), ((0, 8),), -0.2, 0.2)), 0.512, 2.048),
        "average_conv_w": noise(arg_keys[14], (COUT, TAPS), 0.33, 5.0, ((0, 8),), jnp.float32),
        "average_conv_b": noise(arg_keys[15], (COUT,), 0.5, 6.0, ((0, 8),), jnp.float32),
        "average_head_w": noise(arg_keys[16], (CIN, COUT), 0.2, 3.0, ((1, 8),), jnp.float32),
        "average_head_b": noise(arg_keys[17], (COUT,), 0.5, 6.0, ((0, 8),), jnp.float32),
        "pooled_cot": noise(arg_keys[18], (N_DP, OUTG * OUTG * IMG_GRP, COUT), 1.0, 6.0, ((0, 4), (1, 8)), jnp.float32),
        "class_cot": noise(arg_keys[19], (N_DP, IMG_GRP, COUT), 1.0, 6.0, ((0, 4), (1, 8)), jnp.float32),
    }


@jax.custom_vjp
def low(v):
    return lax.optimization_barrier(v.astype(jnp.bfloat16)).astype(jnp.float32)

@jax.custom_vjp
def low_back(v):
    return v

def low_keep(v):
    return (low(v), None)

def low_pass(kept, grad):
    return (grad,)

def back_keep(v):
    return (v, None)

def back_low(kept, grad):
    return (low(grad),)
low.defvjp(low_keep, low_pass)
low_back.defvjp(back_keep, back_low)
beta_one = 0.9
beta_two = 0.999
fix_first = 1.0 - 0.9 ** 10
fix_second = 1.0 - 0.999 ** 10
small_eps = 1e-06
learn_rate = 0.5
keep_rate = 0.9

def forward(patches, class_in, conv_weight, conv_bias, head_weight, head_bias):
    groups = patches.shape[0]
    grid = patches.reshape(groups, GRID, GRID, IMG_GRP, CIN)
    doubled = jnp.repeat(grid, 2, axis=4)
    padded = jnp.pad(doubled, ((0, 0), (1, 1), (1, 1), (0, 0), (0, 0)))
    total = jnp.zeros((groups, OUTG, OUTG, IMG_GRP, COUT), jnp.float32) + conv_bias
    for row_tap in range(3):
        for col_tap in range(3):
            window = padded[:, row_tap:row_tap + 2 * OUTG - 1:2, col_tap:col_tap + 2 * OUTG - 1:2]
            total = total + window * conv_weight[:, 3 * row_tap + col_tap]
    pooled = total.reshape(groups, OUTG * OUTG * IMG_GRP, COUT)
    class_out = jnp.einsum('dbi,io->dbo', class_in, head_weight, precision=lax.Precision.HIGHEST) + head_bias
    return (pooled, class_out)

def lamb(weight, grad, first, second, average, decay):
    first_new = beta_one * first + (1.0 - beta_one) * grad
    second_new = beta_two * second + (1.0 - beta_two) * grad * grad
    update = first_new / fix_first / (jnp.sqrt(second_new / fix_second) + small_eps) + decay * weight
    ratio = jnp.sqrt(jnp.sum(weight * weight)) / jnp.sqrt(jnp.sum(update * update))
    weight_new = weight - learn_rate * ratio * update
    average_new = keep_rate * average + (1.0 - keep_rate) * weight_new
    return (first_new, second_new, weight_new, average_new, ratio)

def reference(patches, class_in, conv_weight, conv_bias, head_weight, head_bias, first_conv_w, first_conv_b, first_head_w, first_head_b, second_conv_w, second_conv_b, second_head_w, second_head_b, average_conv_w, average_conv_b, average_head_w, average_head_b, pooled_cot, class_cot):
    outputs, pullback = jax.vjp(forward, patches, class_in, conv_weight, conv_bias, head_weight, head_bias)
    pooled, class_out = outputs
    grads = pullback((pooled_cot, class_cot))
    patches_grad, class_grad, grad_cw, grad_cb, grad_hw, grad_hb = grads
    conv_w_set = lamb(conv_weight, grad_cw, first_conv_w, second_conv_w, average_conv_w, 0.05)
    conv_b_set = lamb(conv_bias, grad_cb, first_conv_b, second_conv_b, average_conv_b, 0.0)
    head_w_set = lamb(head_weight, grad_hw, first_head_w, second_head_w, average_head_w, 0.05)
    head_b_set = lamb(head_bias, grad_hb, first_head_b, second_head_b, average_head_b, 0.0)
    ratios = jnp.stack([conv_w_set[4], conv_b_set[4], head_w_set[4], head_b_set[4]]).astype(jnp.float32)
    return (pooled, class_out, patches_grad, class_grad, conv_w_set[0], conv_w_set[1], conv_w_set[2], conv_w_set[3], conv_b_set[0], conv_b_set[1], conv_b_set[2], conv_b_set[3], head_w_set[0], head_w_set[1], head_w_set[2], head_w_set[3], head_b_set[0], head_b_set[1], head_b_set[2], head_b_set[3], ratios)
```

```python
import functools

import jax
import jax.numpy as jnp
import numpy as np
from jax import lax
from jax.experimental import pallas as pl
from jax.experimental.pallas import tpu as pltpu
from jax.sharding import PartitionSpec as P

GRID = 27
TAPS = 9
OUTG = 14
LANES = 128
SUBL = 8

beta_one = 0.9
beta_two = 0.999
fix_first = 1.0 - 0.9**10
fix_second = 1.0 - 0.999**10
small_eps = 1e-06
learn_rate = 0.5
keep_rate = 0.9
highest = lax.Precision.HIGHEST


def make_plan(groups, images, n_in, n_out):
    tiles_img = images // LANES
    n_tiles = OUTG * OUTG * tiles_img
    tap_tile = np.full((n_tiles, TAPS), -1, np.int64)
    for i in range(OUTG):
        for j in range(OUTG):
            for it in range(tiles_img):
                for a in range(3):
                    for e in range(3):
                        r, s = 2 * i + a - 1, 2 * j + e - 1
                        if 0 <= r < GRID and 0 <= s < GRID:
                            tap_tile[(i * OUTG + j) * tiles_img + it, 3 * a + e] = (
                                r * GRID + s
                            ) * tiles_img + it
    step = int(np.gcd(np.gcd(n_in, n_out), LANES))
    wanted = {}
    for lane in range(0, LANES, step):
        p_owner = (np.arange(n_tiles) * LANES + lane) // n_out
        t_owner = (tap_tile * LANES + lane) // n_in
        for p in range(n_tiles):
            k = int(p_owner[p])
            for t in range(TAPS):
                if tap_tile[p, t] >= 0 and t_owner[p, t] != k:
                    wanted.setdefault((k, int(t_owner[p, t])), set()).add(p)
    messages = sorted(wanted.items(), key=lambda kv: (-len(kv[1]), kv[0]))
    ops = []
    for (src, dst), tiles in messages:
        for op in ops:
            if (
                op["size"] - len(tiles) <= 1
                and all(src != s and dst != d for s, d in op["pairs"])
            ):
                break
        else:
            op = {"size": len(tiles), "pairs": [], "tiles": []}
            ops.append(op)
        op["pairs"].append((src, dst))
        op["tiles"].append(sorted(tiles))
    in_base = np.arange(groups) * n_in // LANES
    in_shift = np.arange(groups) * n_in % LANES
    out_base = np.arange(groups) * n_out // LANES
    out_shift = np.arange(groups) * n_out % LANES
    in_tiles = int(max(-(-(in_shift + n_in) // LANES)))
    out_tiles = int(max(-(-(out_shift + n_out) // LANES)))
    sizes = [op["size"] for op in ops]
    halo = sum(sizes)
    own_slot = np.full((groups, halo), out_tiles, np.int64)
    taps = np.full((groups, out_tiles + halo, TAPS), in_tiles, np.int64)

    def tap_rows(device, p):
        local = tap_tile[p] - in_base[device]
        first, last = device * n_in, (device + 1) * n_in
        held = (
            (tap_tile[p] >= 0)
            & (tap_tile[p] * LANES < last)
            & ((tap_tile[p] + 1) * LANES > first)
        )
        return np.where(held, local, in_tiles)

    for k in range(groups):
        for j in range(out_tiles):
            if out_base[k] + j < n_tiles:
                taps[k, j] = tap_rows(k, out_base[k] + j)
    start = 0
    for op in ops:
        for (src, dst), tiles in zip(op["pairs"], op["tiles"]):
            for j, p in enumerate(tiles):
                own_slot[src, start + j] = p - out_base[src]
                taps[dst, out_tiles + start + j] = tap_rows(dst, p)
        start += op["size"]
    table = np.concatenate(
        [
            in_shift[:, None],
            out_shift[:, None],
            own_slot,
            taps.reshape(groups, -1),
        ],
        axis=1,
    ).astype(np.int32)
    return {
        "ops": ops,
        "sizes": sizes,
        "halo": halo,
        "in_tiles": in_tiles,
        "out_tiles": out_tiles,
        "n_in": n_in,
        "n_out": n_out,
        "table": table,
        "slot_at": 2,
        "taps_at": 2 + halo,
    }


def lane_ids():
    return lax.broadcasted_iota(jnp.int32, (SUBL, LANES), 1)


def align_into(load, store, n_local, tiles, shift):
    lane = lane_ids()
    zero = jnp.zeros((SUBL, LANES), jnp.float32)
    local_tiles = -(-n_local // LANES)
    before = zero
    for t in range(tiles):
        if t < local_tiles:
            now = load(t)
            if (t + 1) * LANES > n_local:
                now = jnp.where(lane < n_local - t * LANES, now, 0.0)
            now = pltpu.roll(now, shift, 1)
        else:
            now = zero
        store(t, jnp.where(lane < shift, before, now))
        before = now
    store(tiles, zero)


def unalign_from(load, store, n_local, tiles, shift):
    lane = lane_ids()
    local_tiles = -(-n_local // LANES)
    back = lax.rem(LANES - shift, LANES)
    now = pltpu.roll(load(0), back, 1)
    for t in range(local_tiles):
        later = pltpu.roll(load(t + 1), back, 1) if t + 1 < tiles else now
        store(t, jnp.where(lane < LANES - shift, now, later))
        now = later


def tile_lanes(t):
    return slice(t * LANES, (t + 1) * LANES)


def rows_of(part):
    return slice(part * SUBL, (part + 1) * SUBL)


def of_half(half):
    return pl.ds(half, SUBL, stride=2)


def align_cot(cot_ref, held, plan, shift):
    for part in range(2):
        align_into(
            lambda t: cot_ref[rows_of(part), tile_lanes(t)],
            lambda t, v: held.__setitem__((t, rows_of(part)), v),
            plan["n_out"],
            plan["out_tiles"],
            shift,
        )


def align_patches(x_ref, held, plan, shift):
    align_into(
        lambda t: x_ref[:, tile_lanes(t)],
        lambda t, v: held.__setitem__(t, v),
        plan["n_in"],
        plan["in_tiles"],
        shift,
    )


def tap_weights(w_ref, half, count):
    rows = w_ref[of_half(half), :]
    return [jnp.broadcast_to(rows[:, t : t + 1], (SUBL, LANES)) for t in range(count)]


def tap_slots(tab, plan, entry):
    at = plan["taps_at"] + entry * TAPS
    return [tab[at + t] for t in range(TAPS)]


def add_up(items):
    items = list(items)
    while len(items) > 1:
        items = [
            items[i] + items[i + 1] if i + 1 < len(items) else items[i]
            for i in range(0, len(items), 2)
        ]
    return items[0]


def pack_kernel(plan, tab, cot_ref, *refs):
    outs, held = refs[:-1], refs[-1]
    align_cot(cot_ref, held, plan, tab[1])
    at = plan["slot_at"]
    for out, size in zip(outs, plan["sizes"]):
        for j in range(size):
            slot = tab[at + j]
            out[j] = held[slot]
        at += size


def forward_kernel(plan, own, tab, x_ref, w_ref, *refs):
    outs, held = refs[:-1], refs[-1]
    align_patches(x_ref, held, plan, tab[0])
    count = TAPS + 1 if own else TAPS
    weights = [tap_weights(w_ref, half, count) for half in range(2)]

    def one(out, j, entry):
        slots = tap_slots(tab, plan, entry)
        tiles = [held[s] for s in slots]
        for half in range(2):
            total = add_up([tiles[t] * weights[half][t] for t in range(TAPS)])
            if own:
                total = total + weights[half][TAPS]
            out[j, of_half(half)] = total

    if own:
        for j in range(plan["out_tiles"]):
            one(outs[0], j, j)
    else:
        entry = plan["out_tiles"]
        for out, size in zip(outs, plan["sizes"]):
            for j in range(size):
                one(out, j, entry + j)
            entry += size


def backward_kernel(plan, tab, x_ref, cot_ref, w_ref, *refs):
    n_ops = len(plan["sizes"])
    halos = refs[:n_ops]
    grad_ref, sums_ref, held_x, held_c, back = refs[n_ops:]
    align_patches(x_ref, held_x, plan, tab[0])
    align_cot(cot_ref, held_c, plan, tab[1])
    zero = jnp.zeros((SUBL, LANES), jnp.float32)
    for t in range(plan["in_tiles"] + 1):
        back[t] = zero
    weights = [tap_weights(w_ref, half, TAPS) for half in range(2)]

    def one(source, j, entry, total, own):
        slots = tap_slots(tab, plan, entry)
        cots = [source[j, of_half(half)] for half in range(2)]
        total = list(total)
        for t in range(TAPS):
            tile = held_x[slots[t]]
            for half in range(2):
                total[2 * t + half] = total[2 * t + half] + cots[half] * tile
            back[slots[t]] = back[slots[t]] + (
                cots[0] * weights[0][t] + cots[1] * weights[1][t]
            )
        if own:
            for half in range(2):
                total[2 * TAPS + half] = total[2 * TAPS + half] + cots[half]
        return tuple(total)

    total = (zero,) * (2 * TAPS + 2)
    for j in range(plan["out_tiles"]):
        total = one(held_c, j, j, total, True)
    entry = plan["out_tiles"]
    for halo, size in zip(halos, plan["sizes"]):
        for j in range(size):
            total = one(halo, j, entry + j, total, False)
        entry += size
    unalign_from(
        lambda t: back[t],
        lambda t, v: grad_ref.__setitem__((slice(None), tile_lanes(t)), v),
        plan["n_in"],
        plan["in_tiles"],
        tab[0],
    )
    lane = lane_ids()
    for half in range(2):
        row = zero
        for t in range(TAPS + 1):
            row = jnp.where(lane == t, jnp.sum(total[2 * t + half], axis=1, keepdims=True), row)
        sums_ref[of_half(half), :] = row


def finish_kernel(plan, tab, own_ref, *refs):
    n_ops = len(plan["sizes"])
    halos = refs[:n_ops]
    out_ref, held = refs[n_ops:]
    tiles = plan["out_tiles"]
    for t in range(tiles):
        held[t] = own_ref[t]
    at = plan["slot_at"]
    for halo, size in zip(halos, plan["sizes"]):
        for j in range(size):
            slot = tab[at + j]
            held[slot] = held[slot] + halo[j]
        at += size
    for part in range(2):
        unalign_from(
            lambda t: held[t, rows_of(part)],
            lambda t, v: out_ref.__setitem__((rows_of(part), tile_lanes(t)), v),
            plan["n_out"],
            tiles,
            tab[1],
        )


def call(kernel, table, operands, in_specs, outs, out_specs, scratch, steps, flops):
    moved = sum(4 * int(np.prod(a.shape)) for a in operands) + sum(
        4 * int(np.prod(o.shape)) for o in outs
    )
    return pl.pallas_call(
        kernel,
        grid_spec=pltpu.PrefetchScalarGridSpec(
            num_scalar_prefetch=1,
            grid=(steps,),
            in_specs=in_specs,
            out_specs=out_specs,
            scratch_shapes=scratch,
        ),
        out_shape=outs,
        compiler_params=pltpu.CompilerParams(
            dimension_semantics=("arbitrary",), vmem_limit_bytes=32 * 1024 * 1024
        ),
        cost_estimate=pl.CostEstimate(flops=flops, bytes_accessed=moved, transcendentals=0),
    )(table, *operands)


def round_up(n, m):
    return -(-n // m) * m


def f32(*shape):
    return jax.ShapeDtypeStruct(shape, jnp.float32)


def swap(x, axis, bit):
    size = lax.axis_size(axis)
    return lax.ppermute(x, axis, [(k, k ^ bit) for k in range(size)])


def bits_of(axis):
    size = lax.axis_size(axis)
    assert size & (size - 1) == 0
    bits, b = [], 1
    while b < size:
        bits.append(b)
        b *= 2
    return bits


def sum_over(x, axis):
    for bit in reversed(bits_of(axis)):
        x = x + swap(x, axis, bit)
    return x


def gather_over(x, axis):
    me = lax.axis_index(axis)
    size = lax.axis_size(axis)
    every = jnp.zeros((size,) + x.shape, x.dtype)
    every = lax.dynamic_update_index_in_dim(every, x, me, 0)
    for bit in bits_of(axis):
        base = me // bit * bit
        block = lax.dynamic_slice_in_dim(every, base, bit, 0)
        block = swap(block, axis, bit)
        every = lax.dynamic_update_slice_in_dim(every, block, base ^ bit, 0)
    return every


def moments(weight, grad, first, second, decay):
    first_new = beta_one * first + (1.0 - beta_one) * grad
    second_new = beta_two * second + (1.0 - beta_two) * grad * grad
    update = (
        first_new / fix_first / (jnp.sqrt(second_new / fix_second) + small_eps) + decay * weight
    )
    return (first_new, second_new, update)


def per_device(
    patches,
    class_in,
    conv_weight,
    conv_bias,
    head_weight,
    head_bias,
    first_conv_w,
    first_conv_b,
    first_head_w,
    first_head_b,
    second_conv_w,
    second_conv_b,
    second_head_w,
    second_head_b,
    average_conv_w,
    average_conv_b,
    average_head_w,
    average_head_b,
    pooled_cot,
    class_cot,
):
    groups = lax.axis_size("chan")
    me = lax.axis_index("chan")
    per_dev = conv_weight.shape[0]
    n_in, channels_in = patches.shape[1:]
    n_out, channels = pooled_cot.shape[1:]
    local_images = class_in.shape[1]
    images = local_images * groups
    plan = make_plan(groups, images, n_in, n_out)
    sizes, tiles, in_tiles = plan["sizes"], plan["out_tiles"], plan["in_tiles"]
    table = lax.dynamic_index_in_dim(jnp.asarray(plan["table"]), me, 0, keepdims=False)
    steps = channels_in // SUBL
    x = patches[0].T
    cot = pooled_cot[0].T
    in_lanes, out_lanes = round_up(n_in, LANES), round_up(n_out, LANES)
    x_spec = pl.BlockSpec((SUBL, in_lanes), lambda g, tab: (g, 0))
    cot_spec = pl.BlockSpec((2 * SUBL, out_lanes), lambda g, tab: (g, 0))
    halo_specs = [
        pl.BlockSpec((n, 2 * SUBL, LANES), lambda g, tab: (0, g, 0)) for n in sizes
    ]
    halo_outs = [f32(n, channels, LANES) for n in sizes]
    own_spec = pl.BlockSpec((tiles, 2 * SUBL, LANES), lambda g, tab: (0, g, 0))
    w_spec = pl.BlockSpec((2 * SUBL, LANES), lambda g, tab: (g, 0))
    macs = n_out * channels * TAPS

    sends = call(
        functools.partial(pack_kernel, plan),
        table,
        [cot],
        [cot_spec],
        halo_outs,
        halo_specs,
        [pltpu.VMEM((tiles + 1, 2 * SUBL, LANES), jnp.float32)],
        steps,
        1000,
    )
    cot_halo = [
        lax.ppermute(s, "chan", op["pairs"]) for s, op in zip(sends, plan["ops"])
    ]

    stack3 = [
        jnp.concatenate([w, b[:, None]], axis=1)
        for w, b in (
            (conv_weight, conv_bias),
            (first_conv_w, first_conv_b),
            (second_conv_w, second_conv_b),
        )
    ]
    pieces = [*stack3, head_weight, head_bias, class_in[0], class_cot[0]]
    flat = jnp.concatenate([p.reshape(-1) for p in pieces])
    rows = round_up(flat.shape[0], SUBL * LANES)
    flat = jnp.pad(flat, (0, rows - flat.shape[0])).reshape(-1, LANES)
    full = gather_over(flat, "chan").reshape(groups, -1)
    whole, at = [], 0
    for p in pieces:
        n = int(np.prod(p.shape))
        whole.append(full[:, at : at + n].reshape((groups,) + p.shape))
        at += n
    conv_all, first_all, second_all = [w.reshape(channels, TAPS + 1) for w in whole[:3]]
    head_all = jnp.moveaxis(whole[3], 0, 1).reshape(channels_in, channels)
    head_b_all = whole[4].reshape(channels)
    class_all = whole[5].reshape(images, channels_in)
    class_cot_all = whole[6].reshape(images, channels)

    conv_lanes = jnp.pad(conv_all, ((0, 0), (0, LANES - TAPS - 1)))
    partials = call(
        functools.partial(forward_kernel, plan, False),
        table,
        [x, conv_lanes],
        [x_spec, w_spec],
        halo_outs,
        halo_specs,
        [pltpu.VMEM((in_tiles + 1, SUBL, LANES), jnp.float32)],
        steps,
        2 * macs,
    )
    pooled_halo = [
        lax.ppermute(s, "chan", [(d, s_) for s_, d in op["pairs"]])
        for s, op in zip(partials, plan["ops"])
    ]
    pooled_own = call(
        functools.partial(forward_kernel, plan, True),
        table,
        [x, conv_lanes],
        [x_spec, w_spec],
        [f32(tiles, channels, LANES)],
        [own_spec],
        [pltpu.VMEM((in_tiles + 1, SUBL, LANES), jnp.float32)],
        steps,
        2 * macs,
    )[0]
    x_grad, sums = call(
        functools.partial(backward_kernel, plan),
        table,
        [x, cot, conv_lanes, *cot_halo],
        [x_spec, cot_spec, w_spec, *halo_specs],
        [f32(channels_in, n_in), f32(channels, LANES)],
        [x_spec, pl.BlockSpec((2 * SUBL, LANES), lambda g, tab: (g, 0))],
        [
            pltpu.VMEM((in_tiles + 1, SUBL, LANES), jnp.float32),
            pltpu.VMEM((tiles + 1, 2 * SUBL, LANES), jnp.float32),
            pltpu.VMEM((in_tiles + 1, SUBL, LANES), jnp.float32),
        ],
        steps,
        4 * macs,
    )
    pooled = call(
        functools.partial(finish_kernel, plan),
        table,
        [pooled_own, *pooled_halo],
        [own_spec, *halo_specs],
        [f32(channels, n_out)],
        [cot_spec],
        [pltpu.VMEM((tiles + 1, 2 * SUBL, LANES), jnp.float32)],
        steps,
        1000,
    )[0]

    local_class, local_class_cot = class_in[0], class_cot[0]
    class_out = jnp.dot(local_class, head_all, precision=highest) + head_b_all
    class_grad = jnp.dot(local_class_cot, head_all.T, precision=highest)
    my_cot = lax.dynamic_slice_in_dim(class_cot_all, me * per_dev, per_dev, 1)
    grad_h = jnp.concatenate(
        [jnp.dot(class_all.T, my_cot, precision=highest), jnp.sum(my_cot, axis=0)[None]], axis=0
    )
    grad_h = sum_over(grad_h, "dp")
    head_w_set = moments(head_weight, grad_h[:channels_in], first_head_w, second_head_w, 0.05)
    head_b_set = moments(head_bias, grad_h[channels_in], first_head_b, second_head_b, 0.0)
    norms = jnp.stack([jnp.sum(head_w_set[2] ** 2), jnp.sum(head_b_set[2] ** 2)])
    norms = jnp.where(lax.axis_index("dp") == 0, norms, 0.0)

    mine = jnp.zeros((2 * SUBL, round_up(channels, LANES)), jnp.float32)
    mine = mine.at[: TAPS + 1, :channels].set(sums[:, : TAPS + 1].T)
    mine = mine.at[TAPS + 1, :2].set(norms)
    mine = sum_over(sum_over(mine, "dp"), "chan")
    grad_all = mine[: TAPS + 1, :channels].T
    head_norms = mine[TAPS + 1, :2]
    wide_w = moments(conv_all[:, :TAPS], grad_all[:, :TAPS], first_all[:, :TAPS], second_all[:, :TAPS], 0.05)
    wide_b = moments(conv_all[:, TAPS], grad_all[:, TAPS], first_all[:, TAPS], second_all[:, TAPS], 0.0)
    weight_sq = [
        jnp.sum(conv_all[:, :TAPS] ** 2),
        jnp.sum(conv_all[:, TAPS] ** 2),
        jnp.sum(head_all**2),
        jnp.sum(head_b_all**2),
    ]
    update_sq = [jnp.sum(wide_w[2] ** 2), jnp.sum(wide_b[2] ** 2), head_norms[0], head_norms[1]]
    ratios = [jnp.sqrt(weight_sq[k]) / jnp.sqrt(update_sq[k]) for k in range(4)]

    def cut(v):
        return lax.dynamic_slice_in_dim(v, me * per_dev, per_dev, 0)

    sets = (tuple(cut(v) for v in wide_w), tuple(cut(v) for v in wide_b), head_w_set, head_b_set)
    weights = (conv_weight, conv_bias, head_weight, head_bias)
    averages = (average_conv_w, average_conv_b, average_head_w, average_head_b)
    results = []
    for k in range(4):
        weight_new = weights[k] - learn_rate * ratios[k] * sets[k][2]
        average_new = keep_rate * averages[k] + (1.0 - keep_rate) * weight_new
        results.extend([sets[k][0], sets[k][1], weight_new, average_new])
    trust = jnp.stack(ratios)
    return tuple(
        [pooled.T[None], class_out[None], x_grad.T[None], class_grad[None]] + results + [trust]
    )


def solution(mesh):
    return jax.shard_map(
        per_device,
        mesh=mesh,
        in_specs=(
            P("dp", "chan", None),
            P("dp", "chan", None),
            P("chan", None),
            P("chan"),
            P(None, "chan"),
            P("chan"),
            P("chan", None),
            P("chan"),
            P(None, "chan"),
            P("chan"),
            P("chan", None),
            P("chan"),
            P(None, "chan"),
            P("chan"),
            P("chan", None),
            P("chan"),
            P(None, "chan"),
            P("chan"),
            P("dp", "chan", None),
            P("dp", "chan", None),
        ),
        out_specs=(
            P("dp", "chan", None),
            P("dp", "chan", None),
            P("dp", "chan", None),
            P("dp", "chan", None),
            P("chan", None),
            P("chan", None),
            P("chan", None),
            P("chan", None),
            P("chan"),
            P("chan"),
            P("chan"),
            P("chan"),
            P(None, "chan"),
            P(None, "chan"),
            P(None, "chan"),
            P(None, "chan"),
            P("chan"),
            P("chan"),
            P("chan"),
            P("chan"),
            P(),
        ),
        check_vma=False,
    )
```

```python
import functools

import jax
import jax.numpy as jnp
import numpy as np
from jax import lax
from jax.experimental import pallas as pl
from jax.experimental.pallas import tpu as pltpu
from jax.sharding import PartitionSpec as P

GRID = 27
TAPS = 9
OUTG = 14
LANES = 128
SUBL = 8
UNIT = 16

beta_one = 0.9
beta_two = 0.999
fix_first = 1.0 - 0.9**10
fix_second = 1.0 - 0.999**10
small_eps = 1e-06
learn_rate = 0.5
keep_rate = 0.9
highest = lax.Precision.HIGHEST


def grouped(messages, spare):
    ops = []
    for (src, dst), tiles in sorted(messages, key=lambda kv: (-len(kv[1]), kv[0])):
        for op in ops:
            if op["size"] - len(tiles) <= spare and all(
                src != s and dst != d for s, d in op["pairs"]
            ):
                break
        else:
            op = {"size": len(tiles), "pairs": [], "tiles": []}
            ops.append(op)
        op["pairs"].append((src, dst))
        op["tiles"].append(tiles)
    for op in ops:
        op["near"] = all(src ^ dst == 1 for src, dst in op["pairs"])
    return ops


def make_plan(groups, images, n_in, n_out):
    tiles_img = images // LANES
    n_tiles = OUTG * OUTG * tiles_img
    tap_tile = np.full((n_tiles, TAPS), -1, np.int64)
    for i in range(OUTG):
        for j in range(OUTG):
            for it in range(tiles_img):
                for a in range(3):
                    for e in range(3):
                        r, s = 2 * i + a - 1, 2 * j + e - 1
                        if 0 <= r < GRID and 0 <= s < GRID:
                            tap_tile[(i * OUTG + j) * tiles_img + it, 3 * a + e] = (
                                r * GRID + s
                            ) * tiles_img + it
    step = int(np.gcd(np.gcd(n_in, n_out), LANES))
    wanted = {}
    for lane in range(0, LANES, step):
        p_owner = (np.arange(n_tiles) * LANES + lane) // n_out
        t_owner = (tap_tile * LANES + lane) // n_in
        for p in range(n_tiles):
            k = int(p_owner[p])
            for t in range(TAPS):
                if tap_tile[p, t] >= 0 and t_owner[p, t] != k:
                    wanted.setdefault((k, int(t_owner[p, t])), set()).add(p)
    wanted = {pair: sorted(tiles) for pair, tiles in wanted.items()}
    near = {pair: tiles for pair, tiles in wanted.items() if pair[0] ^ pair[1] == 1}
    even = max([min(len(t), len(near.get(p[::-1], []))) for p, t in near.items()], default=0)
    ops = grouped([(p, t[:even]) for p, t in near.items() if even], even)
    ops += grouped([(p, t[even:]) for p, t in near.items() if len(t) > even], 2)
    ops += grouped([(p, t) for p, t in wanted.items() if p not in near], 2)
    back_ops = grouped([((d, s), t) for (s, d), t in wanted.items()], 2)
    longest = max(op["size"] for op in back_ops)
    for op in back_ops:
        op["early"] = op["near"] and 4 * op["size"] > 3 * longest
    in_base = np.arange(groups) * n_in // LANES
    in_shift = np.arange(groups) * n_in % LANES
    out_base = np.arange(groups) * n_out // LANES
    out_shift = np.arange(groups) * n_out % LANES
    in_tiles = int(max(-(-(in_shift + n_in) // LANES)))
    out_tiles = int(max(-(-(out_shift + n_out) // LANES)))
    sizes = [op["size"] for op in ops]
    halo = sum(sizes)
    back_sizes = [op["size"] for op in back_ops]
    back_halo = sum(back_sizes)
    owned = [
        range(int(out_base[k]), int(out_base[k]) - (-(int(out_shift[k]) + n_out) // LANES))
        for k in range(groups)
    ]
    none = out_tiles + halo
    own_slot = np.full((groups, halo), out_tiles, np.int64)
    got = [[] for _ in range(groups)]
    start = 0
    for op in ops:
        for (src, dst), tiles in zip(op["pairs"], op["tiles"]):
            for j, p in enumerate(tiles):
                own_slot[src, start + j] = p - out_base[src]
                got[dst].append((p, start + j))
        start += op["size"]
    most = max(len(v) for v in got)

    def tap_rows(device, p):
        local = tap_tile[p] - in_base[device]
        first, last = device * n_in, (device + 1) * n_in
        held = (
            (tap_tile[p] >= 0)
            & (tap_tile[p] * LANES < last)
            & ((tap_tile[p] + 1) * LANES > first)
        )
        return np.where(held, local, in_tiles)

    own_taps = np.full((groups, out_tiles, TAPS), in_tiles, np.int64)
    got_taps = np.full((groups, most, 1 + TAPS), in_tiles, np.int64)
    got_taps[:, :, 0] = none
    from_got = np.full((groups, back_halo), most, np.int64)
    adds = [[[] for _ in range(out_tiles)] for _ in range(groups)]
    merges, slot_of = [], []
    for k in range(groups):
        for j, p in enumerate(owned[k]):
            own_taps[k, j] = tap_rows(k, p)
        slot_of.append({p: j for j, p in enumerate(owned[k])})
        merges.append([])
        for n, (p, place) in enumerate(got[k]):
            got_taps[k, n, 0] = out_tiles + place
            got_taps[k, n, 1:] = tap_rows(k, p)
            if p in slot_of[k]:
                merges[k].append([slot_of[k][p], out_tiles + place])
            else:
                slot_of[k][p] = out_tiles + place
    start = 0
    for op in back_ops:
        for (src, dst), tiles in zip(op["pairs"], op["tiles"]):
            names = [p for p, _ in got[src]]
            for j, p in enumerate(tiles):
                from_got[src, start + j] = names.index(p)
                adds[dst][p - out_base[dst]].append(start + j)
        start += op["size"]
    n_merges = max(len(v) for v in merges)
    merges = np.array([v + [[none, none]] * (n_merges - len(v)) for v in merges], np.int64)
    n_adds = max(len(v) for per_dev in adds for v in per_dev)
    adds = np.array([[v + [back_halo] * (n_adds - len(v)) for v in per_dev] for per_dev in adds])
    kinds = [
        [(a, e) for a in ((1,), (0, 2))[row_odd] for e in ((1,), (0, 2))[col_odd]]
        for row_odd in range(2)
        for col_odd in range(2)
    ]
    lists = [[[] for _ in range(groups)] for _ in kinds]
    for k in range(groups):
        count = -(-(int(in_shift[k]) + n_in) // LANES)
        for t in range(count):
            position, it = divmod(int(in_base[k]) + t, tiles_img)
            r, s = divmod(position, GRID)
            kind = 2 * (r % 2) + s % 2
            entry = [t]
            for a, e in kinds[kind]:
                i, j = (r + 1 - a) // 2, (s + 1 - e) // 2
                entry.append(slot_of[k].get((i * OUTG + j) * tiles_img + it, none))
            lists[kind][k].append(entry)
    reach_tables, kind_sizes = [], []
    for kind, per_device_lists in enumerate(lists):
        width = 1 + len(kinds[kind])
        size = max(len(v) for v in per_device_lists)
        kind_sizes.append(size)
        filler = [in_tiles] + [none] * (width - 1)
        reach_tables.append(
            np.array([v + [filler] * (size - len(v)) for v in per_device_lists]).reshape(groups, -1)
        )
    parts = [
        ("shifts", np.stack([in_shift, out_shift], axis=1)),
        ("own_slot", own_slot),
        ("own_taps", own_taps.reshape(groups, -1)),
        ("got_taps", got_taps.reshape(groups, -1)),
        ("from_got", from_got),
        ("merges", merges.reshape(groups, -1)),
        ("adds", adds.reshape(groups, -1)),
        *((f"kind{q}", v) for q, v in enumerate(reach_tables)),
    ]
    at, total = {}, 0
    for name, v in parts:
        at[name] = total
        total += v.shape[1]
    return {
        "ops": ops,
        "sizes": sizes,
        "halo": halo,
        "back_ops": back_ops,
        "back_sizes": back_sizes,
        "back_halo": back_halo,
        "in_tiles": in_tiles,
        "out_tiles": out_tiles,
        "most": most,
        "n_merges": n_merges,
        "n_adds": n_adds,
        "n_in": n_in,
        "n_out": n_out,
        "kinds": [[3 * a + e for a, e in kind] for kind in kinds],
        "kind_sizes": kind_sizes,
        "at": at,
        "table": np.concatenate([v for _, v in parts], axis=1).astype(np.int32),
    }


def lane_ids():
    return lax.broadcasted_iota(jnp.int32, (UNIT, LANES), 1)


def align_into(load, store, n_local, tiles, shift):
    lane = lane_ids()
    zero = jnp.zeros((UNIT, LANES), jnp.float32)
    local_tiles = -(-n_local // LANES)
    before = zero
    for t in range(tiles):
        if t < local_tiles:
            now = load(t)
            if (t + 1) * LANES > n_local:
                now = jnp.where(lane < n_local - t * LANES, now, 0.0)
            now = pltpu.roll(now, shift, 1)
        else:
            now = zero
        store(t, jnp.where(lane < shift, before, now))
        before = now
    store(tiles, zero)


def unalign_from(load, store, n_local, tiles, shift):
    lane = lane_ids()
    local_tiles = -(-n_local // LANES)
    back = lax.rem(LANES - shift, LANES)
    now = pltpu.roll(load(0), back, 1)
    for t in range(local_tiles):
        later = pltpu.roll(load(t + 1), back, 1) if t + 1 < tiles else now
        store(t, jnp.where(lane < LANES - shift, now, later))
        now = later


def tile_lanes(t):
    return slice(t * LANES, (t + 1) * LANES)


def rows_at(unit, part=0, parts=1):
    return pl.ds(pl.multiple_of((unit * parts + part) * UNIT, UNIT), UNIT)


def both_at(unit):
    return pl.ds(pl.multiple_of(unit * 2 * UNIT, UNIT), 2 * UNIT)


def of_half(half, unit=0):
    return pl.ds(unit * 2 * UNIT + half, UNIT, stride=2)


def align_cot(cot_ref, unit, held, plan, shift):
    for part in range(2):
        align_into(
            lambda t: cot_ref[rows_at(unit, part, 2), tile_lanes(t)],
            lambda t, v: held.__setitem__((t, slice(part * UNIT, (part + 1) * UNIT)), v),
            plan["n_out"],
            plan["out_tiles"],
            shift,
        )


def tap_weights(w_ref, unit, half, lanes):
    rows = w_ref[of_half(half, unit), :]
    return [jnp.broadcast_to(rows[:, t : t + 1], (UNIT, LANES)) for t in lanes]


def in_turn(count, size, make, keep):
    for first in range(0, count, size):
        some = range(first, min(first + size, count))
        for j, v in [(j, make(j)) for j in some]:
            keep(j, v)


def over_units(ref, rows, body):
    lax.fori_loop(0, ref.shape[0] // rows, lambda u, c: (body(u), c)[1], 0)


def add_up(items):
    items = list(items)
    while len(items) > 1:
        items = [
            items[i] + items[i + 1] if i + 1 < len(items) else items[i]
            for i in range(0, len(items), 2)
        ]
    return items[0]


BIAS_LANE = 48
HEAD_BIAS_LANE = 72
HEAD_LANE = 96


def small_kernel(per_dev, cw, cb, fw, fb, sw, sb, hb, hw, ci, cc, out, square):
    square[...] = jnp.zeros_like(square)
    for part, (w, b) in enumerate(((cw, cb), (fw, fb), (sw, sb))):
        square[2 * SUBL * part : 2 * SUBL * part + TAPS, :per_dev] = w[...]
        square[BIAS_LANE + SUBL * part : BIAS_LANE + SUBL * part + 1, :per_dev] = b[...]
    square[HEAD_BIAS_LANE : HEAD_BIAS_LANE + 1, :per_dev] = hb[...]
    turned = square[...].T
    rows = hw.shape[0]
    lane = lax.broadcasted_iota(jnp.int32, (rows, LANES), 1)
    rest = pltpu.roll(jnp.where(lane < 2 * SUBL, hw[:, LANES:], 0.0), HEAD_LANE, 1)
    out[0:rows] = jnp.where(lane < HEAD_LANE, turned[0:rows], rest)
    out[rows : 2 * rows] = hw[:, :LANES]
    at, n = 2 * rows, ci.shape[0]
    out[at : at + n] = ci[:, :LANES]
    out[at + n : at + 2 * n] = cc[:, :LANES]
    out[at + 2 * n : at + 3 * n] = cc[:, LANES : 2 * LANES]
    lane = lax.broadcasted_iota(jnp.int32, (n, LANES), 1)
    left = jnp.where(lane < 2 * SUBL, ci[:, LANES:], 0.0)
    right = pltpu.roll(jnp.where(lane < 4 * SUBL, cc[:, 2 * LANES :], 0.0), 4 * SUBL, 1)
    out[at + 3 * n : at + 4 * n] = jnp.where(lane < 4 * SUBL, left, right)


def align_kernel(plan, tab, x_ref, cot_ref, after, x_out, cot_out, held):
    def body(unit):
        align_into(
            lambda t: x_ref[rows_at(unit), tile_lanes(t)],
            lambda t, v: x_out.__setitem__((t, rows_at(unit)), v),
            plan["n_in"],
            plan["in_tiles"],
            tab[0],
        )
        align_cot(cot_ref, unit, held, plan, tab[1])
        for j in range(plan["out_tiles"]):
            for half in range(2):
                cot_out[j, half, rows_at(unit)] = held[j, of_half(half)]

    over_units(x_ref, UNIT, body)


def pack_kernel(plan, tab, cot_ref, after, *refs):
    outs, held = refs[:-1], refs[-1]

    def body(unit):
        align_cot(cot_ref, unit, held, plan, tab[1])
        at = plan["at"]["own_slot"]
        for out, size in zip(outs, plan["sizes"]):
            in_turn(
                size,
                6,
                lambda j, at=at: [held[tab[at + j], of_half(half)] for half in range(2)],
                lambda j, v, out=out: keep_split(out, j, unit, v),
            )
            at += size

    over_units(cot_ref, 2 * UNIT, body)


def tap_sums(tab, at, held, weights):
    totals = [None, None]
    for t in range(TAPS):
        tile = held(tab[at + t])
        for half in range(2):
            term = tile * weights[half][t]
            totals[half] = term if t == 0 else totals[half] + term
    return totals


def keep_halves(ref, j, unit, values):
    for half, v in enumerate(values):
        ref[j, of_half(half, unit)] = v


def keep_split(ref, j, unit, values):
    for half, v in enumerate(values):
        ref[j, half, rows_at(unit)] = v


def partial_kernel(plan, tab, x_ref, w_ref, *refs):
    outs, done = refs[:-1], refs[-1]

    def body(unit):
        def held(slot):
            return x_ref[slot, rows_at(unit)]

        weights = [tap_weights(w_ref, unit, half, range(TAPS)) for half in range(2)]
        in_turn(
            plan["most"],
            4,
            lambda n: tap_sums(tab, plan["at"]["got_taps"] + (1 + TAPS) * n + 1, held, weights),
            lambda n, totals: keep_halves(done, n, 0, totals),
        )
        done[plan["most"]] = jnp.zeros(done.shape[1:], jnp.float32)
        at = plan["at"]["from_got"]
        for out, size in zip(outs, plan["back_sizes"]):
            in_turn(
                size,
                6,
                lambda j, at=at: done[tab[at + j]],
                lambda j, v, out=out: out.__setitem__((j, both_at(unit)), v),
            )
            at += size

    over_units(w_ref, 2 * UNIT, body)


def forward_kernel(plan, tab, x_ref, w_ref, after, out):
    def body(unit):
        def held(slot):
            return x_ref[slot, rows_at(unit)]

        weights = [
            tap_weights(w_ref, unit, half, [*range(TAPS), BIAS_LANE]) for half in range(2)
        ]
        in_turn(
            plan["out_tiles"],
            4,
            lambda j: tap_sums(tab, plan["at"]["own_taps"] + TAPS * j, held, weights),
            lambda j, totals: keep_halves(
                out, j, unit, [totals[half] + weights[half][TAPS] for half in range(2)]
            ),
        )

    over_units(w_ref, 2 * UNIT, body)


def take_cots(plan, unit, cot_ref, halos, cots):
    at = 0
    for ref, size in zip((cot_ref, *halos), (plan["out_tiles"], *plan["sizes"])):
        in_turn(
            size,
            5,
            lambda j, ref=ref: [ref[j, half, rows_at(unit)] for half in range(2)],
            lambda j, v, at=at: keep_split_all(cots, at + j, v),
        )
        at += size
    cots[at] = jnp.zeros(cots.shape[1:], jnp.float32)


def keep_split_all(ref, j, values):
    for half, v in enumerate(values):
        ref[j, half] = v


def merge_cots(plan, tab, cots):
    for n in range(plan["n_merges"]):
        at = plan["at"]["merges"] + 2 * n
        for half in range(2):
            cots[tab[at], half] = cots[tab[at], half] + cots[tab[at + 1], half]


def weights_kernel(plan, tab, x_ref, cot_ref, norms, after, *refs):
    halos = refs[: len(plan["sizes"])]
    sums_ref, cots, rows = refs[len(plan["sizes"]) :]
    step = pl.program_id(0)
    per = x_ref.shape[1] // UNIT
    zero = jnp.zeros((UNIT, LANES), jnp.float32)

    @pl.when(step == 0)
    def _():
        rows[...] = jnp.zeros_like(rows)

    def body(unit):
        take_cots(plan, unit, cot_ref, halos, cots)
        here = step * per + unit
        for half in range(2):
            bias = cots[0, half]
            for j in range(1, plan["out_tiles"]):
                bias = bias + cots[j, half]
            rows[TAPS, of_half(half, here), :] = bias
        merge_cots(plan, tab, cots)
        for q, (kind, size) in enumerate(zip(plan["kinds"], plan["kind_sizes"])):
            width = 1 + len(kind)
            total = [[zero] * len(kind) for _ in range(2)]
            for j in range(size):
                at = plan["at"][f"kind{q}"] + width * j
                tile = x_ref[tab[at], rows_at(unit)]
                for n in range(len(kind)):
                    slot = tab[at + 1 + n]
                    for half in range(2):
                        total[half][n] = total[half][n] + cots[slot, half] * tile
            for n, t in enumerate(kind):
                for half in range(2):
                    rows[t, of_half(half, here), :] = total[half][n]

    lax.fori_loop(0, per, lambda u, c: (body(u), c)[1], 0)

    @pl.when(step == pl.num_programs(0) - 1)
    def _():
        lane = lax.broadcasted_iota(jnp.int32, (LANES, LANES), 1)

        def block(b, carry):
            here = pl.ds(pl.multiple_of(b * LANES, LANES), LANES)
            total = jnp.zeros((LANES, LANES), jnp.float32)
            for t in range(TAPS + 1):
                one = jnp.sum(rows[t, here, :], axis=1, keepdims=True)
                total = jnp.where(lane == t, one, total)
            sums_ref[:, here] = total.T[: 2 * SUBL]
            return carry

        lax.fori_loop(0, rows.shape[1] // LANES, block, 0)
        n_lane = lax.broadcasted_iota(jnp.int32, (1, sums_ref.shape[1]), 1)
        extra = jnp.where(n_lane == 0, norms[0], jnp.where(n_lane == 1, norms[1], 0.0))
        sums_ref[TAPS + 1 : TAPS + 2, :] = extra


def patches_kernel(plan, tab, cot_ref, w_ref, after, *refs):
    halos = refs[: len(plan["sizes"])]
    grad_ref, cots, back = refs[len(plan["sizes"]) :]

    def body(unit):
        take_cots(plan, unit, cot_ref, halos, cots)
        merge_cots(plan, tab, cots)
        for q, (kind, size) in enumerate(zip(plan["kinds"], plan["kind_sizes"])):
            weights = [tap_weights(w_ref, unit, half, kind) for half in range(2)]
            width = 1 + len(kind)

            def one(j, q=q, kind=kind, weights=weights, width=width):
                at = plan["at"][f"kind{q}"] + width * j
                items = []
                for n in range(len(kind)):
                    slot = tab[at + 1 + n]
                    items += [cots[slot, half] * weights[half][n] for half in range(2)]
                return at, add_up(items)

            in_turn(size, 4, one, lambda j, v: back.__setitem__(tab[v[0]], v[1]))
        unalign_from(
            lambda t: back[t],
            lambda t, v: grad_ref.__setitem__((rows_at(unit), tile_lanes(t)), v),
            plan["n_in"],
            plan["in_tiles"],
            tab[0],
        )

    over_units(w_ref, 2 * UNIT, body)


def finish_kernel(plan, tab, own_ref, *refs):
    n_ops = len(plan["back_sizes"])
    halos = refs[:n_ops]
    out_ref, held, got = refs[n_ops:]
    tiles = plan["out_tiles"]

    def body(unit):
        at = 0
        for halo, size in zip(halos, plan["back_sizes"]):
            for j in range(size):
                got[at + j] = halo[j, both_at(unit)]
            at += size
        got[at] = jnp.zeros(got.shape[1:], jnp.float32)

        def whole_sum(j):
            total = own_ref[j, both_at(unit)]
            for n in range(plan["n_adds"]):
                total = total + got[tab[plan["at"]["adds"] + plan["n_adds"] * j + n]]
            return total

        in_turn(tiles, 5, whole_sum, held.__setitem__)
        for part in range(2):
            unalign_from(
                lambda t: held[t, part * UNIT : (part + 1) * UNIT],
                lambda t, v: out_ref.__setitem__((rows_at(unit, part, 2), tile_lanes(t)), v),
                plan["n_out"],
                tiles,
                tab[1],
            )

    over_units(out_ref, 2 * UNIT, body)


def spread_kernel(groups, per_dev, rounds, me, parts, ci, cc, after, wide_out, turned_out, class_out, class_grad, grad_out, norms_out, wide, head, cots, classes):
    rows = round_up(per_dev, SUBL)
    n = ci.shape[0]
    channels = groups * per_dev
    wide[...] = jnp.zeros_like(wide)
    head[...] = jnp.zeros_like(head)
    lane = lax.broadcasted_iota(jnp.int32, (n, LANES), 1)
    at = 2 * rows
    for dev in range(groups):
        apart = jnp.bitwise_xor(me[0], dev)
        part = 0
        for place, bit in enumerate(rounds):
            part = part + jnp.bitwise_and(lax.div(apart, bit), 1) * 2**place
        wide[dev * per_dev : (dev + 1) * per_dev, :] = parts[part, :per_dev]
        head[dev * per_dev : (dev + 1) * per_dev, :LANES] = parts[part, rows : rows + per_dev]
        here = slice(dev * n, (dev + 1) * n)
        classes[here, :LANES] = parts[part, at : at + n]
        cots[here, :LANES] = parts[part, at + n : at + 2 * n]
        cots[here, LANES : 2 * LANES] = parts[part, at + 2 * n : at + 3 * n]
        rest = parts[part, at + 3 * n : at + 4 * n]
        ones = jnp.where(lane == 2 * SUBL, 1.0, 0.0)
        classes[here, LANES:] = jnp.where(lane < 2 * SUBL, rest, ones)
        rest = pltpu.roll(rest, LANES - 4 * SUBL, 1)
        cots[here, 2 * LANES :] = jnp.where(lane < 4 * SUBL, rest, 0.0)
    table = wide[...]
    wide_out[...] = table[:channels]
    for b in range(table.shape[0] // LANES):
        turned_out[:, tile_lanes(b)] = table[tile_lanes(b)].T
    lane = lax.broadcasted_iota(jnp.int32, table.shape, 1)
    rest = jnp.where(lane < 2 * SUBL, pltpu.roll(table, LANES - HEAD_LANE, 1), 0.0)
    bias = pltpu.roll(table, LANES - HEAD_BIAS_LANE + 2 * SUBL, 1)
    main = head[:, :LANES]
    norm_b = jnp.sum(jnp.where(lane == 2 * SUBL, bias * bias, 0.0))
    norm_w = jnp.sum(main * main) + jnp.sum(rest * rest)
    head[:, LANES:] = jnp.where(lane == 2 * SUBL, bias, rest)
    conv = jnp.sum(jnp.where(lane < TAPS, table * table, 0.0))
    conv_b = jnp.sum(jnp.where(lane == BIAS_LANE, table * table, 0.0))
    n_lane = lax.broadcasted_iota(jnp.int32, (SUBL, LANES), 1)
    norms = jnp.zeros((SUBL, LANES), jnp.float32)
    for k, v in enumerate((conv, conv_b, norm_w, norm_b)):
        norms = jnp.where(n_lane == k, v, norms)
    norms_out[...] = norms
    lane = lax.broadcasted_iota(jnp.int32, (n, 2 * LANES), 1)
    edge = LANES + 2 * SUBL
    mine = jnp.where(lane < edge, ci[...], jnp.where(lane == edge, 1.0, 0.0))
    last = (((1,), (1,)), ((), ()))
    first = (((0,), (0,)), ((), ()))
    plain = (((1,), (0,)), ((), ()))

    def dot(a, b, dims):
        return lax.dot_general(
            a, b, dims, precision=highest, preferred_element_type=jnp.float32
        )

    class_out[...] = dot(mine, head[:channels, :], last)
    lane = lax.broadcasted_iota(jnp.int32, (n, 3 * LANES), 1)
    my_cot = jnp.where(lane < channels, cc[...], 0.0)
    class_grad[...] = dot(my_cot, head[...], plain)[:, : class_grad.shape[1]]
    pick = pick_rows(channels, per_dev, me[0], cots.shape[1])
    picked = dot(cots[...], pick, plain)
    grad_out[...] = dot(picked, classes[...], first)[:rows]


def pick_rows(channels, per_dev, me, padded):
    shape = (padded, LANES)
    channel = lax.broadcasted_iota(jnp.int32, shape, 0) - me * per_dev
    column = lax.broadcasted_iota(jnp.int32, shape, 1)
    return jnp.where((channel == column) & (column < per_dev), 1.0, 0.0)


def update_kernel(channels, per_dev, me, sums, table, norms, cw, cb, fw, fb, sw, sb, aw, ab, hw, hu, ha, hb, hub, hab,
                  fw_out, sw_out, w_out, a_out, hw_out, ha_out, rows_out):
    padded = sums.shape[1]
    real = lax.broadcasted_iota(jnp.int32, (1, padded), 1) < channels
    wide = moments(
        table[0:TAPS], sums[0:TAPS], table[16 : 16 + TAPS], table[32 : 32 + TAPS], 0.05
    )[2]
    wide_b = moments(table[48:49], sums[TAPS : TAPS + 1], table[56:57], table[64:65], 0.0)[2]
    lane = lax.broadcasted_iota(jnp.int32, (1, LANES), 1)
    update_sq = sums[TAPS + 1 : TAPS + 2, :LANES]
    update_sq = pltpu.roll(update_sq, 2, 1)
    update_sq = jnp.where(lane == 0, jnp.sum(jnp.where(real, wide * wide, 0.0)), update_sq)
    update_sq = jnp.where(lane == 1, jnp.sum(jnp.where(real, wide_b * wide_b, 0.0)), update_sq)
    ratios = jnp.sqrt(norms[0:1, :]) / jnp.sqrt(update_sq)
    rates = [
        learn_rate * jnp.sum(jnp.where(lane == k, ratios, 0.0), axis=1, keepdims=True)
        for k in range(4)
    ]
    mine = lax.dot_general(
        sums[...],
        pick_rows(channels, per_dev, me[0], padded),
        (((1,), (0,)), ((), ())),
        precision=highest,
        preferred_element_type=jnp.float32,
    )
    first, second, update = moments(cw[...], mine[0:TAPS, :per_dev], fw[...], sw[...], 0.05)
    fw_out[...] = first
    sw_out[...] = second
    w_new = cw[...] - rates[0] * update
    w_out[...] = w_new
    a_out[...] = keep_rate * aw[...] + (1.0 - keep_rate) * w_new
    first, second, update = moments(
        cb[...], mine[TAPS : TAPS + 1, :per_dev], fb[...], sb[...], 0.0
    )
    w_new = cb[...] - rates[1] * update
    rows_out[0:1, :per_dev] = first
    rows_out[1:2, :per_dev] = second
    rows_out[2:3, :per_dev] = w_new
    rows_out[3:4, :per_dev] = keep_rate * ab[...] + (1.0 - keep_rate) * w_new
    w_new = hb[...] - rates[3] * hub[...]
    rows_out[4:5, :per_dev] = w_new
    rows_out[5:6, :per_dev] = keep_rate * hab[...] + (1.0 - keep_rate) * w_new
    rows_out[6:7, :] = ratios
    rows_out[7:8, :] = jnp.zeros((1, LANES), jnp.float32)
    w_new = hw[...] - rates[2] * hu[...]
    hw_out[...] = w_new
    ha_out[...] = keep_rate * ha[...] + (1.0 - keep_rate) * w_new


def call(kernel, tables, operands, in_specs, outs, out_specs, scratch, steps, fills=False):
    moved = sum(4 * int(np.prod(a.shape)) for a in operands) + sum(
        4 * int(np.prod(o.shape)) for o in outs
    )
    return pl.pallas_call(
        kernel,
        grid_spec=pltpu.PrefetchScalarGridSpec(
            num_scalar_prefetch=len(tables),
            grid=(steps,),
            in_specs=in_specs,
            out_specs=out_specs,
            scratch_shapes=scratch,
        ),
        out_shape=outs,
        compiler_params=pltpu.CompilerParams(
            dimension_semantics=("arbitrary",), vmem_limit_bytes=60 * 1024 * 1024
        ),
        cost_estimate=pl.CostEstimate(
            flops=1, bytes_accessed=moved if fills else 1, transcendentals=0
        ),
    )(*tables, *operands)


def whole(*shape):
    return pl.BlockSpec(shape, lambda g, *tab: (0,) * len(shape))


def round_up(n, m):
    return -(-n // m) * m


def f32(*shape):
    return jax.ShapeDtypeStruct(shape, jnp.float32)


def swap(x, axis, bit):
    size = lax.axis_size(axis)
    return lax.ppermute(x, axis, [(k, k ^ bit) for k in range(size)])


def bits_of(axis):
    size = lax.axis_size(axis)
    assert size & (size - 1) == 0
    bits, b = [], 1
    while b < size:
        bits.append(b)
        b *= 2
    return bits


def sum_over(x, axis):
    for bit in reversed(bits_of(axis)):
        x = x + swap(x, axis, bit)
    return x


def tied(one, many):
    one, many = lax.optimization_barrier((one, list(many)))
    return one, many


def moments(weight, grad, first, second, decay):
    first_new = beta_one * first + (1.0 - beta_one) * grad
    second_new = beta_two * second + (1.0 - beta_two) * grad * grad
    update = (
        first_new / fix_first / (jnp.sqrt(second_new / fix_second) + small_eps) + decay * weight
    )
    return (first_new, second_new, update)


def per_device(
    patches,
    class_in,
    conv_weight,
    conv_bias,
    head_weight,
    head_bias,
    first_conv_w,
    first_conv_b,
    first_head_w,
    first_head_b,
    second_conv_w,
    second_conv_b,
    second_head_w,
    second_head_b,
    average_conv_w,
    average_conv_b,
    average_head_w,
    average_head_b,
    pooled_cot,
    class_cot,
):
    groups = lax.axis_size("chan")
    me = lax.axis_index("chan")
    my_id = me.astype(jnp.int32)[None]
    per_dev = conv_weight.shape[0]
    n_in, channels_in = patches.shape[1:]
    n_out, channels = pooled_cot.shape[1:]
    local_images = class_in.shape[1]
    images = local_images * groups
    plan = make_plan(groups, images, n_in, n_out)
    sizes, tiles, in_tiles = plan["sizes"], plan["out_tiles"], plan["in_tiles"]
    table = lax.dynamic_index_in_dim(jnp.asarray(plan["table"]), me, 0, keepdims=False)
    per = 3
    steps = channels_in // (UNIT * per)
    x = patches[0].T
    cot = pooled_cot[0].T
    in_lanes, out_lanes = round_up(n_in, LANES), round_up(n_out, LANES)
    rows, wide_rows = UNIT * per, 2 * UNIT * per
    x_spec = pl.BlockSpec((rows, in_lanes), lambda g, tab: (g, 0))
    cot_spec = pl.BlockSpec((wide_rows, out_lanes), lambda g, tab: (g, 0))
    halo_specs = [
        pl.BlockSpec((n, 2, rows, LANES), lambda g, tab: (0, 0, g, 0)) for n in sizes
    ]
    halo_outs = [f32(n, 2, channels_in, LANES) for n in sizes]
    back_sizes = plan["back_sizes"]
    back_specs = [
        pl.BlockSpec((n, wide_rows, LANES), lambda g, tab: (0, g, 0)) for n in back_sizes
    ]
    back_outs = [f32(n, channels, LANES) for n in back_sizes]
    held_spec = pl.BlockSpec((in_tiles + 1, rows, LANES), lambda g, tab: (0, g, 0))
    split_spec = pl.BlockSpec((tiles, 2, rows, LANES), lambda g, tab: (0, 0, g, 0))
    own_spec = pl.BlockSpec((tiles, wide_rows, LANES), lambda g, tab: (0, g, 0))
    w_spec = pl.BlockSpec((wide_rows, LANES), lambda g, tab: (g, 0))
    anywhere = pl.BlockSpec(memory_space=pl.ANY)
    cot_held = pltpu.VMEM((tiles + 1, 2 * UNIT, LANES), jnp.float32)

    pd_rows = round_up(per_dev, SUBL)
    small_rows = 2 * pd_rows + 4 * local_images
    pieces = [
        conv_weight.T,
        conv_bias[None],
        first_conv_w.T,
        first_conv_b[None],
        second_conv_w.T,
        second_conv_b[None],
        head_bias[None],
        head_weight.T,
        class_in[0],
        class_cot[0],
    ]
    own_specs = [
        *(whole(*p.shape) for p in pieces[:7]),
        whole(pd_rows, 2 * LANES),
        whole(local_images, 2 * LANES),
        whole(local_images, 3 * LANES),
    ]
    small = call(
        functools.partial(small_kernel, per_dev),
        [],
        pieces,
        own_specs,
        [f32(small_rows, LANES)],
        [whole(small_rows, LANES)],
        [pltpu.VMEM((LANES, LANES), jnp.float32)],
        1,
    )[0]

    sends = call(
        functools.partial(pack_kernel, plan),
        [table],
        [cot, small],
        [cot_spec, anywhere],
        halo_outs,
        halo_specs,
        [cot_held],
        steps,
    )
    x_held, cot_split = call(
        functools.partial(align_kernel, plan),
        [table],
        [x, cot, sends[0]],
        [x_spec, cot_spec, anywhere],
        [f32(in_tiles + 1, channels_in, LANES), f32(tiles, 2, channels_in, LANES)],
        [held_spec, split_spec],
        [cot_held],
        steps,
        fills=True,
    )

    sends = list(sends)
    cot_halo = [None] * len(sends)
    parts = small[None]
    rounds = bits_of("chan")
    rounds = rounds[:1] + rounds[:0:-1]
    for bit in rounds:
        got = swap(parts, "chan", bit)
        if bit == 1:
            got, sends = tied(got, sends)
        elif bit == rounds[1]:
            got, (x_held,) = tied(got, [x_held])
        parts = jnp.concatenate([parts, got], axis=0)
        if bit == 1:
            parts, sends = tied(parts, sends)
            for n, op in enumerate(plan["ops"]):
                if op["near"]:
                    cot_halo[n] = lax.ppermute(sends[n], "chan", op["pairs"])
    parts, sends = tied(parts, sends)
    if plan["ops"][0]["near"]:
        cot_halo[0], sends = tied(cot_halo[0], sends)
    for n, op in enumerate(plan["ops"]):
        if not op["near"]:
            cot_halo[n] = lax.ppermute(sends[n], "chan", op["pairs"])
    padded = round_up(channels, LANES)
    wide, turned, class_out, class_grad, grad_h, weight_norms = call(
        functools.partial(spread_kernel, groups, per_dev, rounds),
        [my_id],
        [parts, class_in[0], class_cot[0], x_held],
        [whole(*parts.shape), own_specs[8], own_specs[9], anywhere],
        [
            f32(channels, LANES),
            f32(LANES, padded),
            f32(local_images, channels),
            f32(local_images, channels_in),
            f32(pd_rows, 2 * LANES),
            f32(SUBL, LANES),
        ],
        [
            whole(channels, LANES),
            whole(LANES, padded),
            whole(local_images, channels),
            whole(local_images, channels_in),
            whole(pd_rows, 2 * LANES),
            whole(SUBL, LANES),
        ],
        [
            pltpu.VMEM((padded, LANES), jnp.float32),
            pltpu.VMEM((padded, 2 * LANES), jnp.float32),
            pltpu.VMEM((images, 3 * LANES), jnp.float32),
            pltpu.VMEM((images, 2 * LANES), jnp.float32),
        ],
        1,
    )

    partials = call(
        functools.partial(partial_kernel, plan),
        [table],
        [x_held, wide],
        [held_spec, w_spec],
        back_outs,
        back_specs,
        [pltpu.VMEM((plan["most"] + 1, 2 * UNIT, LANES), jnp.float32)],
        steps,
    )
    partials, late = list(partials), []
    pooled_halo = [None] * len(partials)
    for n, op in enumerate(plan["back_ops"]):
        if op["early"]:
            pooled_halo[n] = lax.ppermute(partials[n], "chan", op["pairs"])
        else:
            late.append(n)
    pooled_own = call(
        functools.partial(forward_kernel, plan),
        [table],
        [x_held, wide, partials[0]],
        [held_spec, w_spec, anywhere],
        [f32(tiles, channels, LANES)],
        [own_spec],
        [],
        steps,
    )[0]

    grad_h = sum_over(grad_h, "dp")
    head_t = head_weight.T
    head_first, head_second, head_update = moments(
        head_t, grad_h[:per_dev, :channels_in], first_head_w.T, second_head_w.T, 0.05
    )
    bias_first, bias_second, bias_update = moments(
        head_bias, grad_h[:per_dev, channels_in], first_head_b, second_head_b, 0.0
    )
    norms = jnp.stack([jnp.sum(head_update**2), jnp.sum(bias_update**2)])
    norms = jnp.where(lax.axis_index("dp") == 0, norms, 0.0)

    waiting = [partials[n] for n in late]
    waiting, cot_halo, pooled_own, norms = lax.optimization_barrier(
        (waiting, cot_halo, pooled_own, norms)
    )
    for n, v in zip(late, waiting):
        pooled_halo[n] = lax.ppermute(v, "chan", plan["back_ops"][n]["pairs"])
    cots_held = pltpu.VMEM((tiles + plan["halo"] + 1, 2, UNIT, LANES), jnp.float32)
    sums = call(
        functools.partial(weights_kernel, plan),
        [table],
        [x_held, cot_split, norms, pooled_own, *cot_halo],
        [held_spec, split_spec, pl.BlockSpec(memory_space=pltpu.SMEM), anywhere, *halo_specs],
        [f32(2 * SUBL, padded)],
        [whole(2 * SUBL, padded)],
        [cots_held, pltpu.VMEM((TAPS + 1, padded, LANES), jnp.float32)],
        steps,
    )[0]
    x_grad = call(
        functools.partial(patches_kernel, plan),
        [table],
        [cot_split, wide, sums, *cot_halo],
        [split_spec, w_spec, anywhere, *halo_specs],
        [f32(channels_in, n_in)],
        [x_spec],
        [cots_held, pltpu.VMEM((in_tiles + 1, UNIT, LANES), jnp.float32)],
        steps,
    )[0]
    sums = sum_over(sum_over(sums, "dp"), "chan")
    conv_shapes = [f32(TAPS, per_dev)] * 4
    head_shapes = [f32(per_dev, channels_in)] * 2
    operands = [
        sums,
        turned,
        weight_norms,
        *pieces[:6],
        average_conv_w.T,
        average_conv_b[None],
        head_t,
        head_update,
        average_head_w.T,
        head_bias[None],
        bias_update[None],
        average_head_b[None],
    ]
    out_shapes = [*conv_shapes, *head_shapes, f32(SUBL, LANES)]
    *conv_new, head_new, head_average, small_new = call(
        functools.partial(update_kernel, channels, per_dev),
        [my_id],
        operands,
        [whole(*v.shape) for v in operands],
        out_shapes,
        [whole(*v.shape) for v in out_shapes],
        [],
        1,
    )

    pooled = call(
        functools.partial(finish_kernel, plan),
        [table],
        [pooled_own, *pooled_halo],
        [own_spec, *back_specs],
        [f32(channels, n_out)],
        [cot_spec],
        [cot_held, pltpu.VMEM((plan["back_halo"] + 1, 2 * UNIT, LANES), jnp.float32)],
        steps,
    )[0]
    bias_new = [small_new[k, :per_dev] for k in range(6)]
    return (
        pooled.T[None],
        class_out[None],
        x_grad.T[None],
        class_grad[None],
        *(v.T for v in conv_new),
        *bias_new[:4],
        head_first.T,
        head_second.T,
        head_new.T,
        head_average.T,
        bias_first,
        bias_second,
        *bias_new[4:],
        small_new[6, :4],
    )


def solution(mesh):
    return jax.shard_map(
        per_device,
        mesh=mesh,
        in_specs=(
            P("dp", "chan", None),
            P("dp", "chan", None),
            P("chan", None),
            P("chan"),
            P(None, "chan"),
            P("chan"),
            P("chan", None),
            P("chan"),
            P(None, "chan"),
            P("chan"),
            P("chan", None),
            P("chan"),
            P(None, "chan"),
            P("chan"),
            P("chan", None),
            P("chan"),
            P(None, "chan"),
            P("chan"),
            P("dp", "chan", None),
            P("dp", "chan", None),
        ),
        out_specs=(
            P("dp", "chan", None),
            P("dp", "chan", None),
            P("dp", "chan", None),
            P("dp", "chan", None),
            P("chan", None),
            P("chan", None),
            P("chan", None),
            P("chan", None),
            P("chan"),
            P("chan"),
            P("chan"),
            P("chan"),
            P(None, "chan"),
            P(None, "chan"),
            P(None, "chan"),
            P(None, "chan"),
            P("chan"),
            P("chan"),
            P("chan"),
            P("chan"),
            P(),
        ),
        check_vma=False,
    )
```

```python
import functools

import jax
import jax.numpy as jnp
import numpy as np
from jax import lax
from jax.experimental import pallas as pl
from jax.experimental.pallas import tpu as pltpu
from jax.sharding import PartitionSpec as P

GRID = 27
TAPS = 9
OUTG = 14
LANES = 128
SUBL = 8
UNIT = 16

beta_one = 0.9
beta_two = 0.999
fix_first = 1.0 - 0.9**10
fix_second = 1.0 - 0.999**10
small_eps = 1e-06
learn_rate = 0.5
keep_rate = 0.9
highest = lax.Precision.HIGHEST


def grouped(messages, spare):
    ops = []
    for (src, dst), (full, half) in sorted(
        messages, key=lambda kv: (-2 * len(kv[1][0]) - len(kv[1][1]), kv[0])
    ):
        for op in ops:
            waste = op["full"] + op["half"] / 2 - len(full) - len(half) / 2
            if (
                len(full) <= op["full"]
                and len(half) <= op["half"]
                and waste <= spare
                and all(src != s and dst != d for s, d in op["pairs"])
            ):
                break
        else:
            op = {"full": len(full), "half": len(half), "pairs": [], "tiles": []}
            op["size"] = op["full"] + op["half"]
            ops.append(op)
        op["pairs"].append((src, dst))
        op["tiles"].append(
            [(j, *v) for j, v in enumerate(full)]
            + [(op["full"] + j, *v) for j, v in enumerate(half)]
        )
    for op in ops:
        op["near"] = all(src ^ dst == 1 for src, dst in op["pairs"])
    return ops


def make_plan(groups, images, n_in, n_out):
    tiles_img = images // LANES
    n_tiles = OUTG * OUTG * tiles_img
    tap_tile = np.full((n_tiles, TAPS), -1, np.int64)
    for i in range(OUTG):
        for j in range(OUTG):
            for it in range(tiles_img):
                for a in range(3):
                    for e in range(3):
                        r, s = 2 * i + a - 1, 2 * j + e - 1
                        if 0 <= r < GRID and 0 <= s < GRID:
                            tap_tile[(i * OUTG + j) * tiles_img + it, 3 * a + e] = (
                                r * GRID + s
                            ) * tiles_img + it
    step = int(np.gcd(np.gcd(n_in, n_out), LANES))
    wanted = {}
    for lane in range(0, LANES, step):
        p_owner = (np.arange(n_tiles) * LANES + lane) // n_out
        t_owner = (tap_tile * LANES + lane) // n_in
        for p in range(n_tiles):
            k = int(p_owner[p])
            for t in range(TAPS):
                if tap_tile[p, t] >= 0 and t_owner[p, t] != k:
                    lanes = wanted.setdefault((k, int(t_owner[p, t])), {}).setdefault(p, set())
                    lanes.update((lane, lane + step - 1))
    middle = LANES // 2
    for pair, tiles in wanted.items():
        full, half = [], []
        for p, lanes in sorted(tiles.items()):
            low, high = max(lanes) < middle, min(lanes) >= middle
            (half if low or high else full).append((p, int(high)))
        wanted[pair] = (full, half)
    near = {p: t for p, t in wanted.items() if p[0] ^ p[1] == 1}
    weight = {p: 2 * len(t[0]) + len(t[1]) for p, t in near.items()}
    even = max([min(w, weight.get(p[::-1], 0)) for p, w in weight.items()], default=0)
    begin, rest = [], []
    for p, (full, half) in near.items():
        some = max(even - len(half), 0) // 2
        begin.append((p, (full[:some], half)))
        if full[some:]:
            rest.append((p, (full[some:], [])))
    ops = grouped(begin, even) + grouped(rest, 2)
    ops += grouped([(p, t) for p, t in wanted.items() if p[0] ^ p[1] != 1], 2)
    back_ops = grouped([((d, s), t) for (s, d), t in wanted.items()], 2)
    longest = max(op["size"] for op in back_ops)
    for op in back_ops:
        op["early"] = op["near"] and 4 * op["size"] > 3 * longest
    in_base = np.arange(groups) * n_in // LANES
    in_shift = np.arange(groups) * n_in % LANES
    out_base = np.arange(groups) * n_out // LANES
    out_shift = np.arange(groups) * n_out % LANES
    in_tiles = int(max(-(-(in_shift + n_in) // LANES)))
    out_tiles = int(max(-(-(out_shift + n_out) // LANES)))
    sizes = [op["size"] for op in ops]
    halo = sum(sizes)
    back_sizes = [op["size"] for op in back_ops]
    back_halo = sum(back_sizes)
    owned = [
        range(int(out_base[k]), int(out_base[k]) - (-(int(out_shift[k]) + n_out) // LANES))
        for k in range(groups)
    ]
    none = out_tiles + halo
    own_slot = np.full((groups, halo), out_tiles, np.int64)
    got = [[] for _ in range(groups)]
    upper = np.zeros((4, groups, max(halo, back_halo)), np.int64)
    start = 0
    for op in ops:
        for (src, dst), tiles in zip(op["pairs"], op["tiles"]):
            for j, p, high in tiles:
                own_slot[src, start + j] = p - out_base[src]
                got[dst].append((p, start + j))
                upper[0, src, start + j] = upper[1, dst, start + j] = high
        start += op["size"]
    most = max(len(v) for v in got)

    def tap_rows(device, p):
        local = tap_tile[p] - in_base[device]
        first, last = device * n_in, (device + 1) * n_in
        held = (
            (tap_tile[p] >= 0)
            & (tap_tile[p] * LANES < last)
            & ((tap_tile[p] + 1) * LANES > first)
        )
        return np.where(held, local, in_tiles)

    own_taps = np.full((groups, out_tiles, TAPS), in_tiles, np.int64)
    got_taps = np.full((groups, most, 1 + TAPS), in_tiles, np.int64)
    got_taps[:, :, 0] = none
    from_got = np.full((groups, back_halo), most, np.int64)
    adds = [[[] for _ in range(out_tiles)] for _ in range(groups)]
    merges, slot_of = [], []
    for k in range(groups):
        for j, p in enumerate(owned[k]):
            own_taps[k, j] = tap_rows(k, p)
        slot_of.append({p: j for j, p in enumerate(owned[k])})
        merges.append([])
        for n, (p, place) in enumerate(got[k]):
            got_taps[k, n, 0] = out_tiles + place
            got_taps[k, n, 1:] = tap_rows(k, p)
            if p in slot_of[k]:
                merges[k].append([slot_of[k][p], out_tiles + place])
            else:
                slot_of[k][p] = out_tiles + place
    start = 0
    for op in back_ops:
        for (src, dst), tiles in zip(op["pairs"], op["tiles"]):
            names = [p for p, _ in got[src]]
            for j, p, high in tiles:
                from_got[src, start + j] = names.index(p)
                adds[dst][p - out_base[dst]].append(start + j)
                upper[2, src, start + j] = upper[3, dst, start + j] = high
        start += op["size"]
    n_merges = max(len(v) for v in merges)
    merges = np.array([v + [[none, none]] * (n_merges - len(v)) for v in merges], np.int64)
    n_adds = max(len(v) for per_dev in adds for v in per_dev)
    adds = np.array([[v + [back_halo] * (n_adds - len(v)) for v in per_dev] for per_dev in adds])
    kinds = [
        [(a, e) for a in ((1,), (0, 2))[row_odd] for e in ((1,), (0, 2))[col_odd]]
        for row_odd in range(2)
        for col_odd in range(2)
    ]
    lists = [[[] for _ in range(groups)] for _ in kinds]
    for k in range(groups):
        count = -(-(int(in_shift[k]) + n_in) // LANES)
        for t in range(count):
            position, it = divmod(int(in_base[k]) + t, tiles_img)
            r, s = divmod(position, GRID)
            kind = 2 * (r % 2) + s % 2
            entry = [t]
            for a, e in kinds[kind]:
                i, j = (r + 1 - a) // 2, (s + 1 - e) // 2
                entry.append(slot_of[k].get((i * OUTG + j) * tiles_img + it, none))
            lists[kind][k].append(entry)
    reach_tables, kind_sizes = [], []
    for kind, per_device_lists in enumerate(lists):
        width = 1 + len(kinds[kind])
        size = max(len(v) for v in per_device_lists)
        kind_sizes.append(size)
        filler = [in_tiles] + [none] * (width - 1)
        reach_tables.append(
            np.array([v + [filler] * (size - len(v)) for v in per_device_lists]).reshape(groups, -1)
        )
    parts = [
        ("shifts", np.stack([in_shift, out_shift], axis=1)),
        ("own_slot", own_slot),
        ("own_taps", own_taps.reshape(groups, -1)),
        ("got_taps", got_taps.reshape(groups, -1)),
        ("from_got", from_got),
        ("merges", merges.reshape(groups, -1)),
        ("adds", adds.reshape(groups, -1)),
        *((f"upper{q}", v) for q, v in enumerate(upper)),
        *((f"kind{q}", v) for q, v in enumerate(reach_tables)),
    ]
    at, total = {}, 0
    for name, v in parts:
        at[name] = total
        total += v.shape[1]
    return {
        "ops": ops,
        "sizes": sizes,
        "halo": halo,
        "back_ops": back_ops,
        "back_sizes": back_sizes,
        "back_halo": back_halo,
        "in_tiles": in_tiles,
        "out_tiles": out_tiles,
        "most": most,
        "n_merges": n_merges,
        "n_adds": n_adds,
        "n_in": n_in,
        "n_out": n_out,
        "kinds": [[3 * a + e for a, e in kind] for kind in kinds],
        "kind_sizes": kind_sizes,
        "at": at,
        "table": np.concatenate([v for _, v in parts], axis=1).astype(np.int32),
    }


def lane_ids():
    return lax.broadcasted_iota(jnp.int32, (UNIT, LANES), 1)


def align_into(load, store, n_local, tiles, shift):
    lane = lane_ids()
    zero = jnp.zeros((UNIT, LANES), jnp.float32)
    local_tiles = -(-n_local // LANES)
    before = zero
    for t in range(tiles):
        if t < local_tiles:
            now = load(t)
            if (t + 1) * LANES > n_local:
                now = jnp.where(lane < n_local - t * LANES, now, 0.0)
            now = pltpu.roll(now, shift, 1)
        else:
            now = zero
        store(t, jnp.where(lane < shift, before, now))
        before = now
    store(tiles, zero)


def unalign_from(load, store, n_local, tiles, shift):
    lane = lane_ids()
    local_tiles = -(-n_local // LANES)
    back = lax.rem(LANES - shift, LANES)
    now = pltpu.roll(load(0), back, 1)
    for t in range(local_tiles):
        later = pltpu.roll(load(t + 1), back, 1) if t + 1 < tiles else now
        store(t, jnp.where(lane < LANES - shift, now, later))
        now = later


def tile_lanes(t):
    return slice(t * LANES, (t + 1) * LANES)


def rows_at(unit, part=0, parts=1):
    return pl.ds(pl.multiple_of((unit * parts + part) * UNIT, UNIT), UNIT)


def both_at(unit):
    return pl.ds(pl.multiple_of(unit * 2 * UNIT, UNIT), 2 * UNIT)


def of_half(half, unit=0):
    return pl.ds(unit * 2 * UNIT + half, UNIT, stride=2)


def align_cot(cot_ref, unit, held, plan, shift):
    for part in range(2):
        align_into(
            lambda t: cot_ref[rows_at(unit, part, 2), tile_lanes(t)],
            lambda t, v: held.__setitem__((t, slice(part * UNIT, (part + 1) * UNIT)), v),
            plan["n_out"],
            plan["out_tiles"],
            shift,
        )


def tap_weights(w_ref, unit, half, lanes):
    rows = w_ref[of_half(half, unit), :]
    return [jnp.broadcast_to(rows[:, t : t + 1], (UNIT, LANES)) for t in lanes]


def in_turn(count, size, make, keep):
    for first in range(0, count, size):
        some = range(first, min(first + size, count))
        for j, v in [(j, make(j)) for j in some]:
            keep(j, v)


def over_units(ref, rows, body):
    lax.fori_loop(0, ref.shape[0] // rows, lambda u, c: (body(u), c)[1], 0)


def add_up(items):
    items = list(items)
    while len(items) > 1:
        items = [
            items[i] + items[i + 1] if i + 1 < len(items) else items[i]
            for i in range(0, len(items), 2)
        ]
    return items[0]


BIAS_LANE = 48
HEAD_BIAS_LANE = 72
HEAD_LANE = 96


def small_kernel(per_dev, cw, cb, fw, fb, sw, sb, hb, hw, ci, cc, out, square):
    square[...] = jnp.zeros_like(square)
    for part, (w, b) in enumerate(((cw, cb), (fw, fb), (sw, sb))):
        square[2 * SUBL * part : 2 * SUBL * part + TAPS, :per_dev] = w[...]
        square[BIAS_LANE + SUBL * part : BIAS_LANE + SUBL * part + 1, :per_dev] = b[...]
    square[HEAD_BIAS_LANE : HEAD_BIAS_LANE + 1, :per_dev] = hb[...]
    turned = square[...].T
    rows = hw.shape[0]
    lane = lax.broadcasted_iota(jnp.int32, (rows, LANES), 1)
    rest = pltpu.roll(jnp.where(lane < 2 * SUBL, hw[:, LANES:], 0.0), HEAD_LANE, 1)
    out[0:rows] = jnp.where(lane < HEAD_LANE, turned[0:rows], rest)
    out[rows : 2 * rows] = hw[:, :LANES]
    at, n = 2 * rows, ci.shape[0]
    out[at : at + n] = ci[:, :LANES]
    out[at + n : at + 2 * n] = cc[:, :LANES]
    out[at + 2 * n : at + 3 * n] = cc[:, LANES : 2 * LANES]
    lane = lax.broadcasted_iota(jnp.int32, (n, LANES), 1)
    left = jnp.where(lane < 2 * SUBL, ci[:, LANES:], 0.0)
    right = pltpu.roll(jnp.where(lane < 4 * SUBL, cc[:, 2 * LANES :], 0.0), 4 * SUBL, 1)
    out[at + 3 * n : at + 4 * n] = jnp.where(lane < 4 * SUBL, left, right)


def align_patches_kernel(plan, tab, x_ref, after, x_out):
    def body(unit):
        align_into(
            lambda t: x_ref[rows_at(unit), tile_lanes(t)],
            lambda t, v: x_out.__setitem__((t, rows_at(unit)), v),
            plan["n_in"],
            plan["in_tiles"],
            tab[0],
        )

    over_units(x_ref, UNIT, body)


def align_cot_kernel(plan, tab, cot_ref, after, cot_out, held):
    def body(unit):
        align_cot(cot_ref, unit, held, plan, tab[1])
        for j in range(plan["out_tiles"]):
            for half in range(2):
                cot_out[j, half, rows_at(unit)] = held[j, of_half(half)]

    over_units(cot_ref, 2 * UNIT, body)


def pack_kernel(plan, tab, cot_ref, after, *refs):
    outs, held = refs[:-1], refs[-1]

    def body(unit):
        align_cot(cot_ref, unit, held, plan, tab[1])
        at = 0
        for op, out in zip(plan["ops"], outs):
            send_tiles(
                op,
                lambda j, at=at: [
                    held[tab[plan["at"]["own_slot"] + at + j], of_half(half)] for half in range(2)
                ],
                lambda j, at=at: tab[plan["at"]["upper0"] + at + j],
                out,
                unit,
            )
            at += op["size"]

    over_units(cot_ref, 2 * UNIT, body)


def tap_sums(tab, at, held, weights):
    totals = [None, None]
    for t in range(TAPS):
        tile = held(tab[at + t])
        for half in range(2):
            term = tile * weights[half][t]
            totals[half] = term if t == 0 else totals[half] + term
    return totals


def keep_halves(ref, j, unit, values):
    for half, v in enumerate(values):
        ref[j, of_half(half, unit)] = v


def send_tiles(op, load, upper, out, unit):
    def store(j, pair):
        for half, v in enumerate(pair):
            out[2 * j + half, rows_at(unit)] = v

    in_turn(op["full"], 6, load, store)
    low = lane_ids() < LANES // 2
    for j in range(op["full"], op["size"]):
        even, odd = load(j)
        high = upper(j) > 0
        left = jnp.where(high, pltpu.roll(even, LANES // 2, 1), even)
        right = jnp.where(high, odd, pltpu.roll(odd, LANES // 2, 1))
        out[op["full"] + j, rows_at(unit)] = jnp.where(low, left, right)


def received_tiles(op, ref, upper, keep, unit):
    in_turn(
        op["full"],
        5,
        lambda j: [ref[2 * j + half, rows_at(unit)] for half in range(2)],
        keep,
    )
    low = lane_ids() < LANES // 2
    for j in range(op["full"], op["size"]):
        plane = ref[op["full"] + j, rows_at(unit)]
        turned = pltpu.roll(plane, LANES // 2, 1)
        high = upper(j) > 0
        even = jnp.where(high, jnp.where(low, 0.0, turned), jnp.where(low, plane, 0.0))
        odd = jnp.where(high, jnp.where(low, 0.0, plane), jnp.where(low, turned, 0.0))
        keep(j, [even, odd])


def partial_kernel(plan, tab, x_ref, w_ref, *refs):
    outs, done = refs[:-1], refs[-1]

    def body(unit):
        def held(slot):
            return x_ref[slot, rows_at(unit)]

        weights = [tap_weights(w_ref, unit, half, range(TAPS)) for half in range(2)]
        in_turn(
            plan["most"],
            4,
            lambda n: tap_sums(tab, plan["at"]["got_taps"] + (1 + TAPS) * n + 1, held, weights),
            lambda n, totals: keep_split_all(done, n, totals),
        )
        done[plan["most"]] = jnp.zeros(done.shape[1:], jnp.float32)
        at = 0
        for op, out in zip(plan["back_ops"], outs):
            send_tiles(
                op,
                lambda j, at=at: [
                    done[tab[plan["at"]["from_got"] + at + j], half] for half in range(2)
                ],
                lambda j, at=at: tab[plan["at"]["upper2"] + at + j],
                out,
                unit,
            )
            at += op["size"]

    over_units(w_ref, 2 * UNIT, body)


def forward_kernel(plan, tab, x_ref, w_ref, after, out):
    def body(unit):
        def held(slot):
            return x_ref[slot, rows_at(unit)]

        weights = [
            tap_weights(w_ref, unit, half, [*range(TAPS), BIAS_LANE]) for half in range(2)
        ]
        in_turn(
            plan["out_tiles"],
            4,
            lambda j: tap_sums(tab, plan["at"]["own_taps"] + TAPS * j, held, weights),
            lambda j, totals: keep_halves(
                out, j, unit, [totals[half] + weights[half][TAPS] for half in range(2)]
            ),
        )

    over_units(w_ref, 2 * UNIT, body)


def take_cots(plan, tab, unit, cot_ref, halos, cots):
    own = plan["out_tiles"]
    in_turn(
        own,
        5,
        lambda j: [cot_ref[j, half, rows_at(unit)] for half in range(2)],
        lambda j, v: keep_split_all(cots, j, v),
    )
    at = 0
    for op, ref in zip(plan["ops"], halos):
        received_tiles(
            op,
            ref,
            lambda j, at=at: tab[plan["at"]["upper1"] + at + j],
            lambda j, v, at=at: keep_split_all(cots, own + at + j, v),
            unit,
        )
        at += op["size"]
    cots[own + at] = jnp.zeros(cots.shape[1:], jnp.float32)


def keep_split_all(ref, j, values):
    for half, v in enumerate(values):
        ref[j, half] = v


def merge_cots(plan, tab, cots):
    for n in range(plan["n_merges"]):
        at = plan["at"]["merges"] + 2 * n
        for half in range(2):
            cots[tab[at], half] = cots[tab[at], half] + cots[tab[at + 1], half]


def weights_kernel(plan, tab, x_ref, cot_ref, *refs):
    halos = refs[: len(plan["sizes"])]
    sums_ref, cots, rows = refs[len(plan["sizes"]) :]
    step = pl.program_id(0)
    per = x_ref.shape[1] // UNIT
    zero = jnp.zeros((UNIT, LANES), jnp.float32)

    @pl.when(step == 0)
    def _():
        rows[...] = jnp.zeros_like(rows)

    def body(unit):
        take_cots(plan, tab, unit, cot_ref, halos, cots)
        here = step * per + unit
        for half in range(2):
            bias = cots[0, half]
            for j in range(1, plan["out_tiles"]):
                bias = bias + cots[j, half]
            rows[TAPS, of_half(half, here), :] = bias
        merge_cots(plan, tab, cots)
        for q, (kind, size) in enumerate(zip(plan["kinds"], plan["kind_sizes"])):
            width = 1 + len(kind)
            total = [[zero] * len(kind) for _ in range(2)]
            for j in range(size):
                at = plan["at"][f"kind{q}"] + width * j
                tile = x_ref[tab[at], rows_at(unit)]
                for n in range(len(kind)):
                    slot = tab[at + 1 + n]
                    for half in range(2):
                        total[half][n] = total[half][n] + cots[slot, half] * tile
            for n, t in enumerate(kind):
                for half in range(2):
                    rows[t, of_half(half, here), :] = total[half][n]

    lax.fori_loop(0, per, lambda u, c: (body(u), c)[1], 0)

    @pl.when(step == pl.num_programs(0) - 1)
    def _():
        lane = lax.broadcasted_iota(jnp.int32, (LANES, LANES), 1)

        def block(b, carry):
            here = pl.ds(pl.multiple_of(b * LANES, LANES), LANES)
            total = jnp.zeros((LANES, LANES), jnp.float32)
            for t in range(TAPS + 1):
                one = jnp.sum(rows[t, here, :], axis=1, keepdims=True)
                total = jnp.where(lane == t, one, total)
            sums_ref[:, here] = total.T[: 2 * SUBL]
            return carry

        lax.fori_loop(0, rows.shape[1] // LANES, block, 0)


def patches_kernel(plan, tab, cot_ref, w_ref, after, *refs):
    halos = refs[: len(plan["sizes"])]
    grad_ref, cots, back = refs[len(plan["sizes"]) :]

    def body(unit):
        take_cots(plan, tab, unit, cot_ref, halos, cots)
        merge_cots(plan, tab, cots)
        for q, (kind, size) in enumerate(zip(plan["kinds"], plan["kind_sizes"])):
            weights = [tap_weights(w_ref, unit, half, kind) for half in range(2)]
            width = 1 + len(kind)

            def one(j, q=q, kind=kind, weights=weights, width=width):
                at = plan["at"][f"kind{q}"] + width * j
                items = []
                for n in range(len(kind)):
                    slot = tab[at + 1 + n]
                    items += [cots[slot, half] * weights[half][n] for half in range(2)]
                return at, add_up(items)

            in_turn(size, 4, one, lambda j, v: back.__setitem__(tab[v[0]], v[1]))
        unalign_from(
            lambda t: back[t],
            lambda t, v: grad_ref.__setitem__((rows_at(unit), tile_lanes(t)), v),
            plan["n_in"],
            plan["in_tiles"],
            tab[0],
        )

    over_units(w_ref, 2 * UNIT, body)


def finish_kernel(plan, tab, own_ref, *refs):
    n_ops = len(plan["back_sizes"])
    halos = refs[:n_ops]
    out_ref, held, got = refs[n_ops:]
    tiles = plan["out_tiles"]

    def body(unit):
        at = 0
        for op, halo in zip(plan["back_ops"], halos):
            received_tiles(
                op,
                halo,
                lambda j, at=at: tab[plan["at"]["upper3"] + at + j],
                lambda j, v, at=at: keep_halves(got, at + j, 0, v),
                unit,
            )
            at += op["size"]
        got[at] = jnp.zeros(got.shape[1:], jnp.float32)

        def whole_sum(j):
            total = own_ref[j, both_at(unit)]
            for n in range(plan["n_adds"]):
                total = total + got[tab[plan["at"]["adds"] + plan["n_adds"] * j + n]]
            return total

        in_turn(tiles, 5, whole_sum, held.__setitem__)
        for part in range(2):
            unalign_from(
                lambda t: held[t, part * UNIT : (part + 1) * UNIT],
                lambda t, v: out_ref.__setitem__((rows_at(unit, part, 2), tile_lanes(t)), v),
                plan["n_out"],
                tiles,
                tab[1],
            )

    over_units(out_ref, 2 * UNIT, body)


def spread_kernel(groups, per_dev, rounds, me, parts, ci, cc, after, wide_out, turned_out, class_out, class_grad, grad_out, norms_out, wide, head, cots, classes):
    rows = round_up(per_dev, SUBL)
    n = ci.shape[0]
    channels = groups * per_dev
    wide[...] = jnp.zeros_like(wide)
    head[...] = jnp.zeros_like(head)
    lane = lax.broadcasted_iota(jnp.int32, (n, LANES), 1)
    at = 2 * rows
    for dev in range(groups):
        apart = jnp.bitwise_xor(me[0], dev)
        part = 0
        for place, bit in enumerate(rounds):
            part = part + jnp.bitwise_and(lax.div(apart, bit), 1) * 2**place
        wide[dev * per_dev : (dev + 1) * per_dev, :] = parts[part, :per_dev]
        head[dev * per_dev : (dev + 1) * per_dev, :LANES] = parts[part, rows : rows + per_dev]
        here = slice(dev * n, (dev + 1) * n)
        classes[here, :LANES] = parts[part, at : at + n]
        cots[here, :LANES] = parts[part, at + n : at + 2 * n]
        cots[here, LANES : 2 * LANES] = parts[part, at + 2 * n : at + 3 * n]
        rest = parts[part, at + 3 * n : at + 4 * n]
        ones = jnp.where(lane == 2 * SUBL, 1.0, 0.0)
        classes[here, LANES:] = jnp.where(lane < 2 * SUBL, rest, ones)
        rest = pltpu.roll(rest, LANES - 4 * SUBL, 1)
        cots[here, 2 * LANES :] = jnp.where(lane < 4 * SUBL, rest, 0.0)
    table = wide[...]
    wide_out[...] = table[:channels]
    for b in range(table.shape[0] // LANES):
        turned_out[:, tile_lanes(b)] = table[tile_lanes(b)].T
    lane = lax.broadcasted_iota(jnp.int32, table.shape, 1)
    rest = jnp.where(lane < 2 * SUBL, pltpu.roll(table, LANES - HEAD_LANE, 1), 0.0)
    bias = pltpu.roll(table, LANES - HEAD_BIAS_LANE + 2 * SUBL, 1)
    main = head[:, :LANES]
    norm_b = jnp.sum(jnp.where(lane == 2 * SUBL, bias * bias, 0.0))
    norm_w = jnp.sum(main * main) + jnp.sum(rest * rest)
    head[:, LANES:] = jnp.where(lane == 2 * SUBL, bias, rest)
    conv = jnp.sum(jnp.where(lane < TAPS, table * table, 0.0))
    conv_b = jnp.sum(jnp.where(lane == BIAS_LANE, table * table, 0.0))
    n_lane = lax.broadcasted_iota(jnp.int32, (SUBL, LANES), 1)
    norms = jnp.zeros((SUBL, LANES), jnp.float32)
    for k, v in enumerate((conv, conv_b, norm_w, norm_b)):
        norms = jnp.where(n_lane == k, v, norms)
    norms_out[...] = norms
    lane = lax.broadcasted_iota(jnp.int32, (n, 2 * LANES), 1)
    edge = LANES + 2 * SUBL
    mine = jnp.where(lane < edge, ci[...], jnp.where(lane == edge, 1.0, 0.0))
    last = (((1,), (1,)), ((), ()))
    first = (((0,), (0,)), ((), ()))
    plain = (((1,), (0,)), ((), ()))

    def dot(a, b, dims):
        return lax.dot_general(
            a, b, dims, precision=highest, preferred_element_type=jnp.float32
        )

    class_out[...] = dot(mine, head[:channels, :], last)
    lane = lax.broadcasted_iota(jnp.int32, (n, 3 * LANES), 1)
    my_cot = jnp.where(lane < channels, cc[...], 0.0)
    class_grad[...] = dot(my_cot, head[...], plain)[:, : class_grad.shape[1]]
    pick = pick_rows(channels, per_dev, me[0], cots.shape[1])
    picked = dot(cots[...], pick, plain)
    grad_out[...] = dot(picked, classes[...], first)[:rows]


def pick_rows(channels, per_dev, me, padded):
    shape = (padded, LANES)
    channel = lax.broadcasted_iota(jnp.int32, shape, 0) - me * per_dev
    column = lax.broadcasted_iota(jnp.int32, shape, 1)
    return jnp.where((channel == column) & (column < per_dev), 1.0, 0.0)


def update_kernel(channels, per_dev, me, sums, table, norms, cw, cb, fw, fb, sw, sb, aw, ab, hw, hu, ha, hb, hub, hab,
                  fw_out, sw_out, w_out, a_out, hw_out, ha_out, fb_out, sb_out, b_out, ab_out, hb_out, hab_out, ratio_out):
    padded = sums.shape[1]
    real = lax.broadcasted_iota(jnp.int32, (1, padded), 1) < channels
    wide = moments(
        table[0:TAPS], sums[0:TAPS], table[16 : 16 + TAPS], table[32 : 32 + TAPS], 0.05
    )[2]
    wide_b = moments(table[48:49], sums[TAPS : TAPS + 1], table[56:57], table[64:65], 0.0)[2]
    lane = lax.broadcasted_iota(jnp.int32, (1, LANES), 1)
    update_sq = sums[TAPS + 1 : TAPS + 2, :LANES]
    update_sq = pltpu.roll(update_sq, 2, 1)
    update_sq = jnp.where(lane == 0, jnp.sum(jnp.where(real, wide * wide, 0.0)), update_sq)
    update_sq = jnp.where(lane == 1, jnp.sum(jnp.where(real, wide_b * wide_b, 0.0)), update_sq)
    ratios = jnp.sqrt(norms[0:1, :]) / jnp.sqrt(update_sq)
    rates = [
        learn_rate * jnp.sum(jnp.where(lane == k, ratios, 0.0), axis=1, keepdims=True)
        for k in range(4)
    ]
    mine = lax.dot_general(
        sums[...],
        pick_rows(channels, per_dev, me[0], padded),
        (((1,), (0,)), ((), ())),
        precision=highest,
        preferred_element_type=jnp.float32,
    )
    first, second, update = moments(cw[...], mine[0:TAPS, :per_dev], fw[...], sw[...], 0.05)
    fw_out[...] = first
    sw_out[...] = second
    w_new = cw[...] - rates[0] * update
    w_out[...] = w_new
    a_out[...] = keep_rate * aw[...] + (1.0 - keep_rate) * w_new
    first, second, update = moments(
        cb[...], mine[TAPS : TAPS + 1, :per_dev], fb[...], sb[...], 0.0
    )
    w_new = cb[...] - rates[1] * update
    fb_out[...] = first.reshape(per_dev)
    sb_out[...] = second.reshape(per_dev)
    b_out[...] = w_new.reshape(per_dev)
    ab_out[...] = (keep_rate * ab[...] + (1.0 - keep_rate) * w_new).reshape(per_dev)
    w_new = hb[...] - rates[3] * hub[...]
    hb_out[...] = w_new.reshape(per_dev)
    hab_out[...] = (keep_rate * hab[...] + (1.0 - keep_rate) * w_new).reshape(per_dev)
    ratio_out[...] = ratios[:, :4].reshape(4)
    w_new = hw[...] - rates[2] * hu[...]
    hw_out[...] = w_new
    ha_out[...] = keep_rate * ha[...] + (1.0 - keep_rate) * w_new


def call(kernel, tables, operands, in_specs, outs, out_specs, scratch, steps, fills=False, tight=False):
    moved = sum(4 * int(np.prod(a.shape)) for a in operands) + sum(
        4 * int(np.prod(o.shape)) for o in outs
    )
    limit = 60
    if tight:
        blocks = [s.block_shape for s in [*in_specs, *out_specs] if s.block_shape]
        need = 8 * sum(int(np.prod(b)) for b in blocks)
        need += 4 * sum(int(np.prod(v.shape)) for v in scratch)
        limit = min(limit, max(24, need * 5 // 2**22 + 4))
    return pl.pallas_call(
        kernel,
        grid_spec=pltpu.PrefetchScalarGridSpec(
            num_scalar_prefetch=len(tables),
            grid=(steps,),
            in_specs=in_specs,
            out_specs=out_specs,
            scratch_shapes=scratch,
        ),
        out_shape=outs,
        compiler_params=pltpu.CompilerParams(
            dimension_semantics=("arbitrary",), vmem_limit_bytes=limit * 1024 * 1024
        ),
        cost_estimate=pl.CostEstimate(
            flops=1, bytes_accessed=moved if fills else 1, transcendentals=0
        ),
    )(*tables, *operands)


def whole(*shape):
    return pl.BlockSpec(shape, lambda g, *tab: (0,) * len(shape))


def round_up(n, m):
    return -(-n // m) * m


def f32(*shape):
    return jax.ShapeDtypeStruct(shape, jnp.float32)


def swap(x, axis, bit):
    size = lax.axis_size(axis)
    return lax.ppermute(x, axis, [(k, k ^ bit) for k in range(size)])


def bits_of(axis):
    size = lax.axis_size(axis)
    assert size & (size - 1) == 0
    bits, b = [], 1
    while b < size:
        bits.append(b)
        b *= 2
    return bits


def sum_over(x, axis):
    for bit in reversed(bits_of(axis)):
        x = x + swap(x, axis, bit)
    return x


def tied(one, many):
    one, many = lax.optimization_barrier((one, list(many)))
    return one, many


def moments(weight, grad, first, second, decay):
    first_new = beta_one * first + (1.0 - beta_one) * grad
    second_new = beta_two * second + (1.0 - beta_two) * grad * grad
    update = (
        first_new / fix_first / (jnp.sqrt(second_new / fix_second) + small_eps) + decay * weight
    )
    return (first_new, second_new, update)


def per_device(
    patches,
    class_in,
    conv_weight,
    conv_bias,
    head_weight,
    head_bias,
    first_conv_w,
    first_conv_b,
    first_head_w,
    first_head_b,
    second_conv_w,
    second_conv_b,
    second_head_w,
    second_head_b,
    average_conv_w,
    average_conv_b,
    average_head_w,
    average_head_b,
    pooled_cot,
    class_cot,
):
    groups = lax.axis_size("chan")
    me = lax.axis_index("chan")
    my_id = me.astype(jnp.int32)[None]
    per_dev = conv_weight.shape[0]
    n_in, channels_in = patches.shape[1:]
    n_out, channels = pooled_cot.shape[1:]
    local_images = class_in.shape[1]
    images = local_images * groups
    plan = make_plan(groups, images, n_in, n_out)
    tiles, in_tiles = plan["out_tiles"], plan["in_tiles"]
    table = lax.dynamic_index_in_dim(jnp.asarray(plan["table"]), me, 0, keepdims=False)
    per = 3
    steps = channels_in // (UNIT * per)
    x = patches[0].T
    cot = pooled_cot[0].T
    in_lanes, out_lanes = round_up(n_in, LANES), round_up(n_out, LANES)
    rows, wide_rows = UNIT * per, 2 * UNIT * per
    x_spec = pl.BlockSpec((rows, in_lanes), lambda g, tab: (g, 0))
    cot_spec = pl.BlockSpec((wide_rows, out_lanes), lambda g, tab: (g, 0))
    planes = [2 * op["full"] + op["half"] for op in plan["ops"]]
    halo_specs = [pl.BlockSpec((n, rows, LANES), lambda g, tab: (0, g, 0)) for n in planes]
    halo_outs = [f32(n, channels_in, LANES) for n in planes]
    planes = [2 * op["full"] + op["half"] for op in plan["back_ops"]]
    back_specs = [pl.BlockSpec((n, rows, LANES), lambda g, tab: (0, g, 0)) for n in planes]
    back_outs = [f32(n, channels_in, LANES) for n in planes]
    held_spec = pl.BlockSpec((in_tiles + 1, rows, LANES), lambda g, tab: (0, g, 0))
    split_spec = pl.BlockSpec((tiles, 2, rows, LANES), lambda g, tab: (0, 0, g, 0))
    own_spec = pl.BlockSpec((tiles, wide_rows, LANES), lambda g, tab: (0, g, 0))
    w_spec = pl.BlockSpec((wide_rows, LANES), lambda g, tab: (g, 0))
    anywhere = pl.BlockSpec(memory_space=pl.ANY)
    cot_held = pltpu.VMEM((tiles + 1, 2 * UNIT, LANES), jnp.float32)

    pd_rows = round_up(per_dev, SUBL)
    small_rows = 2 * pd_rows + 4 * local_images
    pieces = [
        conv_weight.T,
        conv_bias[None],
        first_conv_w.T,
        first_conv_b[None],
        second_conv_w.T,
        second_conv_b[None],
        head_bias[None],
        head_weight.T,
        class_in[0],
        class_cot[0],
    ]
    own_specs = [
        *(whole(*p.shape) for p in pieces[:7]),
        whole(pd_rows, 2 * LANES),
        whole(local_images, 2 * LANES),
        whole(local_images, 3 * LANES),
    ]
    small = call(
        functools.partial(small_kernel, per_dev),
        [],
        pieces,
        own_specs,
        [f32(small_rows, LANES)],
        [whole(small_rows, LANES)],
        [pltpu.VMEM((LANES, LANES), jnp.float32)],
        1,
    )[0]

    sends = call(
        functools.partial(pack_kernel, plan),
        [table],
        [cot, small],
        [cot_spec, anywhere],
        halo_outs,
        halo_specs,
        [cot_held],
        steps,
    )
    x_held = call(
        functools.partial(align_patches_kernel, plan),
        [table],
        [x, sends[0]],
        [x_spec, anywhere],
        [f32(in_tiles + 1, channels_in, LANES)],
        [held_spec],
        [],
        steps,
    )[0]
    cot_split = call(
        functools.partial(align_cot_kernel, plan),
        [table],
        [cot, x_held],
        [cot_spec, anywhere],
        [f32(tiles, 2, channels_in, LANES)],
        [split_spec],
        [cot_held],
        steps,
    )[0]

    sends = list(sends)
    cot_halo = [None] * len(sends)
    parts = small[None]
    rounds = bits_of("chan")
    rounds = rounds[:1] + rounds[:0:-1]
    for bit in rounds:
        got = swap(parts, "chan", bit)
        if bit == 1:
            got, sends = tied(got, sends)
        elif bit == rounds[1]:
            got, (x_held,) = tied(got, [x_held])
        elif bit == rounds[-1]:
            got, (cot_split,) = tied(got, [cot_split])
        parts = jnp.concatenate([parts, got], axis=0)
        if bit == 1:
            parts, sends = tied(parts, sends)
            for n, op in enumerate(plan["ops"]):
                if op["near"]:
                    cot_halo[n] = lax.ppermute(sends[n], "chan", op["pairs"])
    parts, sends = tied(parts, sends)
    near = [n for n, op in enumerate(plan["ops"]) if op["near"]]
    if near:
        cot_halo[near[0]], sends = tied(cot_halo[near[0]], sends)
    for n, op in enumerate(plan["ops"]):
        if not op["near"]:
            cot_halo[n] = lax.ppermute(sends[n], "chan", op["pairs"])
    padded = round_up(channels, LANES)
    wide, turned, class_out, class_grad, grad_h, weight_norms = call(
        functools.partial(spread_kernel, groups, per_dev, rounds),
        [my_id],
        [parts, class_in[0], class_cot[0], x_held],
        [whole(*parts.shape), own_specs[8], own_specs[9], anywhere],
        [
            f32(channels, LANES),
            f32(LANES, padded),
            f32(local_images, channels),
            f32(local_images, channels_in),
            f32(pd_rows, 2 * LANES),
            f32(SUBL, LANES),
        ],
        [
            whole(channels, LANES),
            whole(LANES, padded),
            whole(local_images, channels),
            whole(local_images, channels_in),
            whole(pd_rows, 2 * LANES),
            whole(SUBL, LANES),
        ],
        [
            pltpu.VMEM((padded, LANES), jnp.float32),
            pltpu.VMEM((padded, 2 * LANES), jnp.float32),
            pltpu.VMEM((images, 3 * LANES), jnp.float32),
            pltpu.VMEM((images, 2 * LANES), jnp.float32),
        ],
        1,
    )

    partials = call(
        functools.partial(partial_kernel, plan),
        [table],
        [x_held, wide],
        [held_spec, w_spec],
        back_outs,
        back_specs,
        [pltpu.VMEM((plan["most"] + 1, 2, UNIT, LANES), jnp.float32)],
        steps,
        tight=True,
    )
    partials, late = list(partials), []
    pooled_halo = [None] * len(partials)
    for n, op in enumerate(plan["back_ops"]):
        if op["early"]:
            pooled_halo[n] = lax.ppermute(partials[n], "chan", op["pairs"])
        else:
            late.append(n)
    grad_h = sum_over(grad_h, "dp")
    head_t = head_weight.T
    head_first, head_second, head_update = moments(
        head_t, grad_h[:per_dev, :channels_in], first_head_w.T, second_head_w.T, 0.05
    )
    bias_first, bias_second, bias_update = moments(
        head_bias, grad_h[:per_dev, channels_in], first_head_b, second_head_b, 0.0
    )
    norms = [jnp.sum(head_update**2), jnp.sum(bias_update**2)]

    pooled_own = call(
        functools.partial(forward_kernel, plan),
        [table],
        [x_held, wide, head_update],
        [held_spec, w_spec, anywhere],
        [f32(tiles, channels, LANES)],
        [own_spec],
        [],
        steps,
        tight=True,
    )[0]

    waiting = [partials[n] for n in late]
    waiting, cot_halo, pooled_own, norms = lax.optimization_barrier(
        (waiting, cot_halo, pooled_own, norms)
    )
    for n, v in zip(late, waiting):
        pooled_halo[n] = lax.ppermute(v, "chan", plan["back_ops"][n]["pairs"])
    cots_held = pltpu.VMEM((tiles + plan["halo"] + 1, 2, UNIT, LANES), jnp.float32)
    sums = call(
        functools.partial(weights_kernel, plan),
        [table],
        [x_held, cot_split, *cot_halo],
        [held_spec, split_spec, *halo_specs],
        [f32(2 * SUBL, padded)],
        [whole(2 * SUBL, padded)],
        [cots_held, pltpu.VMEM((TAPS + 1, padded, LANES), jnp.float32)],
        steps,
        tight=True,
    )[0]
    x_grad = call(
        functools.partial(patches_kernel, plan),
        [table],
        [cot_split, wide, sums, *cot_halo],
        [split_spec, w_spec, anywhere, *halo_specs],
        [f32(channels_in, n_in)],
        [x_spec],
        [cots_held, pltpu.VMEM((in_tiles + 1, UNIT, LANES), jnp.float32)],
        steps,
        tight=True,
    )[0]
    sums = sum_over(sums, "dp")
    row = lax.broadcasted_iota(jnp.int32, sums.shape, 0)
    lane = lax.broadcasted_iota(jnp.int32, sums.shape, 1)
    for k, v in enumerate(norms):
        sums = jnp.where((row == TAPS + 1) & (lane == k), v, sums)
    pooled = call(
        functools.partial(finish_kernel, plan),
        [table],
        [pooled_own, *pooled_halo],
        [own_spec, *back_specs],
        [f32(channels, n_out)],
        [cot_spec],
        [cot_held, pltpu.VMEM((plan["back_halo"] + 1, 2 * UNIT, LANES), jnp.float32)],
        steps,
        tight=True,
    )[0]
    for bit in bits_of("chan")[::-1]:
        got = swap(sums, "chan", bit)
        if bit == bits_of("chan")[-1]:
            got, (x_grad,) = tied(got, [x_grad])
        if bit == 1:
            got, (pooled,) = tied(got, [pooled])
        sums = sums + got
    conv_shapes = [f32(TAPS, per_dev)] * 4
    head_shapes = [f32(per_dev, channels_in)] * 2
    operands = [
        sums,
        turned,
        weight_norms,
        *pieces[:6],
        average_conv_w.T,
        average_conv_b[None],
        head_t,
        head_update,
        average_head_w.T,
        head_bias[None],
        bias_update[None],
        average_head_b[None],
    ]
    specs = [whole(*v.shape) for v in operands]
    out_shapes = [*conv_shapes, *head_shapes, *[f32(per_dev)] * 6, f32(4)]
    *new, trust = call(
        functools.partial(update_kernel, channels, per_dev),
        [my_id],
        operands,
        specs,
        out_shapes,
        [whole(*v.shape) for v in out_shapes],
        [],
        1,
    )

    conv_new, (head_new, head_average), bias_new = new[:4], new[4:6], new[6:]
    return (
        pooled.T[None],
        class_out[None],
        x_grad.T[None],
        class_grad[None],
        *(v.T for v in conv_new),
        *bias_new[:4],
        head_first.T,
        head_second.T,
        head_new.T,
        head_average.T,
        bias_first,
        bias_second,
        *bias_new[4:],
        trust,
    )


def solution(mesh):
    return jax.shard_map(
        per_device,
        mesh=mesh,
        in_specs=(
            P("dp", "chan", None),
            P("dp", "chan", None),
            P("chan", None),
            P("chan"),
            P(None, "chan"),
            P("chan"),
            P("chan", None),
            P("chan"),
            P(None, "chan"),
            P("chan"),
            P("chan", None),
            P("chan"),
            P(None, "chan"),
            P("chan"),
            P("chan", None),
            P("chan"),
            P(None, "chan"),
            P("chan"),
            P("dp", "chan", None),
            P("dp", "chan", None),
        ),
        out_specs=(
            P("dp", "chan", None),
            P("dp", "chan", None),
            P("dp", "chan", None),
            P("dp", "chan", None),
            P("chan", None),
            P("chan", None),
            P("chan", None),
            P("chan", None),
            P("chan"),
            P("chan"),
            P("chan"),
            P("chan"),
            P(None, "chan"),
            P(None, "chan"),
            P(None, "chan"),
            P(None, "chan"),
            P("chan"),
            P("chan"),
            P("chan"),
            P("chan"),
            P(),
        ),
        check_vma=False,
    )
```

```python
import functools

import jax
import jax.numpy as jnp
import numpy as np
from jax import lax
from jax.experimental import pallas as pl
from jax.experimental.pallas import tpu as pltpu
from jax.sharding import PartitionSpec as P

GRID = 27
TAPS = 9
OUTG = 14
LANES = 128
SUBL = 8
UNIT = 16

beta_one = 0.9
beta_two = 0.999
fix_first = 1.0 - 0.9**10
fix_second = 1.0 - 0.999**10
small_eps = 1e-06
learn_rate = 0.5
keep_rate = 0.9
highest = lax.Precision.HIGHEST


def sized(parts):
    full = max(len(f) for _, (f, _) in parts)
    half = max(len(h) for _, (_, h) in parts)
    return {
        "full": full,
        "half": half,
        "size": full + half,
        "parts": parts,
        "pairs": [pair for pair, _ in parts],
        "tiles": [
            [(j, *v) for j, v in enumerate(f)] + [(full + j, *v) for j, v in enumerate(h)]
            for _, (f, h) in parts
        ],
        "near": all(src ^ dst == 1 for (src, dst), _ in parts),
    }


def halves(message):
    return 2 * len(message[0]) + len(message[1])


def free_in(parts, pair):
    return all(pair[0] != s and pair[1] != d for (s, d), _ in parts)


def grouped(messages, spare):
    groups = []
    for pair, message in sorted(messages, key=lambda kv: (-halves(kv[1]), kv[0])):
        for parts in groups:
            first = parts[0][1]
            if (
                len(message[0]) <= len(first[0])
                and len(message[1]) <= len(first[1])
                and halves(first) - halves(message) <= 2 * spare
                and free_in(parts, pair)
            ):
                break
        else:
            parts = []
            groups.append(parts)
        parts.append((pair, message))
    return [sized(parts) for parts in groups]


def loads(ops, groups):
    got = np.zeros(groups, np.int64)
    for op in ops:
        for _, dst in op["pairs"]:
            got[dst] += 2 * op["full"] + op["half"]
    return got


def joined(ops, others, groups):
    for n in range(1, len(ops)):
        for m in range(n):
            if not (ops[n]["near"] and ops[m]["near"]):
                continue
            for pair, message in list(ops[n]["parts"]):
                got = loads(ops + others, groups)
                more = halves(ops[m]["parts"][0][1]) - 2 * ops[n]["full"] - ops[n]["half"]
                if (
                    len(ops[n]["parts"]) > 1
                    and free_in(ops[m]["parts"], pair)
                    and got[pair[1]] + more < 0.9 * max(got)
                ):
                    ops[n] = sized([v for v in ops[n]["parts"] if v[0] != pair])
                    ops[m] = sized(ops[m]["parts"] + [(pair, message)])
    return ops


def make_plan(groups, images, n_in, n_out):
    tiles_img = images // LANES
    n_tiles = OUTG * OUTG * tiles_img
    tap_tile = np.full((n_tiles, TAPS), -1, np.int64)
    for i in range(OUTG):
        for j in range(OUTG):
            for it in range(tiles_img):
                for a in range(3):
                    for e in range(3):
                        r, s = 2 * i + a - 1, 2 * j + e - 1
                        if 0 <= r < GRID and 0 <= s < GRID:
                            tap_tile[(i * OUTG + j) * tiles_img + it, 3 * a + e] = (
                                r * GRID + s
                            ) * tiles_img + it
    step = int(np.gcd(np.gcd(n_in, n_out), LANES))
    wanted = {}
    for lane in range(0, LANES, step):
        p_owner = (np.arange(n_tiles) * LANES + lane) // n_out
        t_owner = (tap_tile * LANES + lane) // n_in
        for p in range(n_tiles):
            k = int(p_owner[p])
            for t in range(TAPS):
                if tap_tile[p, t] >= 0 and t_owner[p, t] != k:
                    lanes = wanted.setdefault((k, int(t_owner[p, t])), {}).setdefault(p, set())
                    lanes.update((lane, lane + step - 1))
    middle = LANES // 2
    for pair, tiles in wanted.items():
        full, half = [], []
        for p, lanes in sorted(tiles.items()):
            low, high = max(lanes) < middle, min(lanes) >= middle
            (half if low or high else full).append((p, int(high)))
        wanted[pair] = (full, half)
    near = {p: t for p, t in wanted.items() if p[0] ^ p[1] == 1}
    weight = {p: 2 * len(t[0]) + len(t[1]) for p, t in near.items()}
    even = max([min(w, weight.get(p[::-1], 0)) for p, w in weight.items()], default=0)
    begin, rest = [], []
    for p, (full, half) in near.items():
        some = max(even - len(half), 0) // 2
        begin.append((p, (full[:some], half)))
        if full[some:]:
            rest.append((p, (full[some:], [])))
    ops = grouped(begin, even) + grouped(rest, 2)
    ops += grouped([(p, t) for p, t in wanted.items() if p[0] ^ p[1] != 1], 2)
    back_ops = grouped([((d, s), t) for (s, d), t in wanted.items()], 2)
    back_ops = joined(back_ops, ops, groups)
    longest = max(op["size"] for op in back_ops)
    for op in back_ops:
        op["early"] = op["near"] and 4 * op["size"] > 3 * longest
    in_base = np.arange(groups) * n_in // LANES
    in_shift = np.arange(groups) * n_in % LANES
    out_base = np.arange(groups) * n_out // LANES
    out_shift = np.arange(groups) * n_out % LANES
    in_tiles = int(max(-(-(in_shift + n_in) // LANES)))
    out_tiles = int(max(-(-(out_shift + n_out) // LANES)))
    sizes = [op["size"] for op in ops]
    halo = sum(sizes)
    back_sizes = [op["size"] for op in back_ops]
    back_halo = sum(back_sizes)
    owned = [
        range(int(out_base[k]), int(out_base[k]) - (-(int(out_shift[k]) + n_out) // LANES))
        for k in range(groups)
    ]
    none = out_tiles + halo
    own_slot = np.full((groups, halo), out_tiles, np.int64)
    got = [[] for _ in range(groups)]
    upper = np.zeros((4, groups, max(halo, back_halo)), np.int64)
    start = 0
    for op in ops:
        for (src, dst), tiles in zip(op["pairs"], op["tiles"]):
            for j, p, high in tiles:
                own_slot[src, start + j] = p - out_base[src]
                got[dst].append((p, start + j))
                upper[0, src, start + j] = upper[1, dst, start + j] = high
        start += op["size"]
    most = max(len(v) for v in got)

    def tap_rows(device, p):
        local = tap_tile[p] - in_base[device]
        first, last = device * n_in, (device + 1) * n_in
        held = (
            (tap_tile[p] >= 0)
            & (tap_tile[p] * LANES < last)
            & ((tap_tile[p] + 1) * LANES > first)
        )
        return np.where(held, local, in_tiles)

    own_taps = np.full((groups, out_tiles, TAPS), in_tiles, np.int64)
    got_taps = np.full((groups, most, 1 + TAPS), in_tiles, np.int64)
    got_taps[:, :, 0] = none
    from_got = np.full((groups, back_halo), most, np.int64)
    adds = [[[] for _ in range(out_tiles)] for _ in range(groups)]
    merges, slot_of = [], []
    for k in range(groups):
        for j, p in enumerate(owned[k]):
            own_taps[k, j] = tap_rows(k, p)
        slot_of.append({p: j for j, p in enumerate(owned[k])})
        merges.append([])
        for n, (p, place) in enumerate(got[k]):
            got_taps[k, n, 0] = out_tiles + place
            got_taps[k, n, 1:] = tap_rows(k, p)
            if p in slot_of[k]:
                merges[k].append([slot_of[k][p], out_tiles + place])
            else:
                slot_of[k][p] = out_tiles + place
    start = 0
    for op in back_ops:
        for (src, dst), tiles in zip(op["pairs"], op["tiles"]):
            names = [p for p, _ in got[src]]
            for j, p, high in tiles:
                from_got[src, start + j] = names.index(p)
                adds[dst][p - out_base[dst]].append(start + j)
                upper[2, src, start + j] = upper[3, dst, start + j] = high
        start += op["size"]
    n_merges = max(len(v) for v in merges)
    merges = np.array([v + [[none, none]] * (n_merges - len(v)) for v in merges], np.int64)
    n_adds = max(len(v) for per_dev in adds for v in per_dev)
    adds = np.array([[v + [back_halo] * (n_adds - len(v)) for v in per_dev] for per_dev in adds])
    kinds = [
        [(a, e) for a in ((1,), (0, 2))[row_odd] for e in ((1,), (0, 2))[col_odd]]
        for row_odd in range(2)
        for col_odd in range(2)
    ]
    lists = [[[] for _ in range(groups)] for _ in kinds]
    for k in range(groups):
        count = -(-(int(in_shift[k]) + n_in) // LANES)
        for t in range(count):
            position, it = divmod(int(in_base[k]) + t, tiles_img)
            r, s = divmod(position, GRID)
            kind = 2 * (r % 2) + s % 2
            entry = [t]
            for a, e in kinds[kind]:
                i, j = (r + 1 - a) // 2, (s + 1 - e) // 2
                entry.append(slot_of[k].get((i * OUTG + j) * tiles_img + it, none))
            lists[kind][k].append(entry)
    reach_tables, kind_sizes = [], []
    for kind, per_device_lists in enumerate(lists):
        width = 1 + len(kinds[kind])
        size = max(len(v) for v in per_device_lists)
        kind_sizes.append(size)
        filler = [in_tiles] + [none] * (width - 1)
        reach_tables.append(
            np.array([v + [filler] * (size - len(v)) for v in per_device_lists]).reshape(groups, -1)
        )
    parts = [
        ("shifts", np.stack([in_shift, out_shift], axis=1)),
        ("own_slot", own_slot),
        ("own_taps", own_taps.reshape(groups, -1)),
        ("got_taps", got_taps.reshape(groups, -1)),
        ("from_got", from_got),
        ("merges", merges.reshape(groups, -1)),
        ("adds", adds.reshape(groups, -1)),
        *((f"upper{q}", v) for q, v in enumerate(upper)),
        *((f"kind{q}", v) for q, v in enumerate(reach_tables)),
    ]
    at, total = {}, 0
    for name, v in parts:
        at[name] = total
        total += v.shape[1]
    return {
        "ops": ops,
        "sizes": sizes,
        "halo": halo,
        "back_ops": back_ops,
        "back_sizes": back_sizes,
        "back_halo": back_halo,
        "in_tiles": in_tiles,
        "out_tiles": out_tiles,
        "most": most,
        "n_merges": n_merges,
        "n_adds": n_adds,
        "n_in": n_in,
        "n_out": n_out,
        "kinds": [[3 * a + e for a, e in kind] for kind in kinds],
        "kind_sizes": kind_sizes,
        "at": at,
        "table": np.concatenate([v for _, v in parts], axis=1).astype(np.int32),
    }


def lane_ids():
    return lax.broadcasted_iota(jnp.int32, (UNIT, LANES), 1)


def align_into(load, store, n_local, tiles, shift):
    lane = lane_ids()
    zero = jnp.zeros((UNIT, LANES), jnp.float32)
    local_tiles = -(-n_local // LANES)
    before = zero
    for t in range(tiles):
        if t < local_tiles:
            now = load(t)
            if (t + 1) * LANES > n_local:
                now = jnp.where(lane < n_local - t * LANES, now, 0.0)
            now = pltpu.roll(now, shift, 1)
        else:
            now = zero
        store(t, jnp.where(lane < shift, before, now))
        before = now
    store(tiles, zero)


def unalign_from(load, store, n_local, tiles, shift):
    lane = lane_ids()
    local_tiles = -(-n_local // LANES)
    back = lax.rem(LANES - shift, LANES)
    now = pltpu.roll(load(0), back, 1)
    for t in range(local_tiles):
        later = pltpu.roll(load(t + 1), back, 1) if t + 1 < tiles else now
        store(t, jnp.where(lane < LANES - shift, now, later))
        now = later


def tile_lanes(t):
    return slice(t * LANES, (t + 1) * LANES)


def rows_at(unit, part=0, parts=1):
    return pl.ds(pl.multiple_of((unit * parts + part) * UNIT, UNIT), UNIT)


def both_at(unit):
    return pl.ds(pl.multiple_of(unit * 2 * UNIT, UNIT), 2 * UNIT)


def of_half(half, unit=0):
    return pl.ds(unit * 2 * UNIT + half, UNIT, stride=2)


def align_cot(cot_ref, unit, held, plan, shift):
    for part in range(2):
        align_into(
            lambda t: cot_ref[rows_at(unit, part, 2), tile_lanes(t)],
            lambda t, v: held.__setitem__((t, slice(part * UNIT, (part + 1) * UNIT)), v),
            plan["n_out"],
            plan["out_tiles"],
            shift,
        )


def tap_weights(w_ref, unit, half, lanes):
    rows = w_ref[of_half(half, unit), :]
    return [jnp.broadcast_to(rows[:, t : t + 1], (UNIT, LANES)) for t in lanes]


def in_turn(count, size, make, keep):
    for first in range(0, count, size):
        some = range(first, min(first + size, count))
        for j, v in [(j, make(j)) for j in some]:
            keep(j, v)


def over_units(ref, rows, body):
    lax.fori_loop(0, ref.shape[0] // rows, lambda u, c: (body(u), c)[1], 0)


def add_up(items):
    items = list(items)
    while len(items) > 1:
        items = [
            items[i] + items[i + 1] if i + 1 < len(items) else items[i]
            for i in range(0, len(items), 2)
        ]
    return items[0]


BIAS_LANE = 48
HEAD_BIAS_LANE = 72
HEAD_LANE = 96


def small_kernel(per_dev, cw, cb, fw, fb, sw, sb, hb, hw, ci, cc, out, square):
    square[...] = jnp.zeros_like(square)
    for part, (w, b) in enumerate(((cw, cb), (fw, fb), (sw, sb))):
        square[2 * SUBL * part : 2 * SUBL * part + TAPS, :per_dev] = w[...]
        square[BIAS_LANE + SUBL * part : BIAS_LANE + SUBL * part + 1, :per_dev] = b[...]
    square[HEAD_BIAS_LANE : HEAD_BIAS_LANE + 1, :per_dev] = hb[...]
    turned = square[...].T
    rows = hw.shape[0]
    lane = lax.broadcasted_iota(jnp.int32, (rows, LANES), 1)
    rest = pltpu.roll(jnp.where(lane < 2 * SUBL, hw[:, LANES:], 0.0), HEAD_LANE, 1)
    out[0:rows] = jnp.where(lane < HEAD_LANE, turned[0:rows], rest)
    out[rows : 2 * rows] = hw[:, :LANES]
    at, n = 2 * rows, ci.shape[0]
    out[at : at + n] = ci[:, :LANES]
    out[at + n : at + 2 * n] = cc[:, :LANES]
    out[at + 2 * n : at + 3 * n] = cc[:, LANES : 2 * LANES]
    lane = lax.broadcasted_iota(jnp.int32, (n, LANES), 1)
    left = jnp.where(lane < 2 * SUBL, ci[:, LANES:], 0.0)
    right = pltpu.roll(jnp.where(lane < 4 * SUBL, cc[:, 2 * LANES :], 0.0), 4 * SUBL, 1)
    out[at + 3 * n : at + 4 * n] = jnp.where(lane < 4 * SUBL, left, right)


def align_patches_kernel(plan, tab, x_ref, after, x_out):
    def body(unit):
        align_into(
            lambda t: x_ref[rows_at(unit), tile_lanes(t)],
            lambda t, v: x_out.__setitem__((t, rows_at(unit)), v),
            plan["n_in"],
            plan["in_tiles"],
            tab[0],
        )

    over_units(x_ref, UNIT, body)


def align_cot_kernel(plan, tab, cot_ref, after, cot_out, held):
    def body(unit):
        align_cot(cot_ref, unit, held, plan, tab[1])
        for j in range(plan["out_tiles"]):
            for half in range(2):
                cot_out[j, half, rows_at(unit)] = held[j, of_half(half)]

    over_units(cot_ref, 2 * UNIT, body)


def pack_kernel(plan, tab, cot_ref, after, *refs):
    outs, held = refs[:-1], refs[-1]

    def body(unit):
        align_cot(cot_ref, unit, held, plan, tab[1])
        at = 0
        for op, out in zip(plan["ops"], outs):
            send_tiles(
                op,
                lambda j, at=at: [
                    held[tab[plan["at"]["own_slot"] + at + j], of_half(half)] for half in range(2)
                ],
                lambda j, at=at: tab[plan["at"]["upper0"] + at + j],
                out,
                unit,
            )
            at += op["size"]

    over_units(cot_ref, 2 * UNIT, body)


def tap_sums(tab, at, held, weights):
    totals = [None, None]
    for t in range(TAPS):
        tile = held(tab[at + t])
        for half in range(2):
            term = tile * weights[half][t]
            totals[half] = term if t == 0 else totals[half] + term
    return totals


def keep_halves(ref, j, unit, values):
    for half, v in enumerate(values):
        ref[j, of_half(half, unit)] = v


def send_tiles(op, load, upper, out, unit):
    def store(j, pair):
        for half, v in enumerate(pair):
            out[2 * j + half, rows_at(unit)] = v

    in_turn(op["full"], 6, load, store)
    low = lane_ids() < LANES // 2
    for j in range(op["full"], op["size"]):
        even, odd = load(j)
        high = upper(j) > 0
        left = jnp.where(high, pltpu.roll(even, LANES // 2, 1), even)
        right = jnp.where(high, odd, pltpu.roll(odd, LANES // 2, 1))
        out[op["full"] + j, rows_at(unit)] = jnp.where(low, left, right)


def received_tiles(op, ref, upper, keep, unit):
    in_turn(
        op["full"],
        5,
        lambda j: [ref[2 * j + half, rows_at(unit)] for half in range(2)],
        keep,
    )
    low = lane_ids() < LANES // 2
    for j in range(op["full"], op["size"]):
        plane = ref[op["full"] + j, rows_at(unit)]
        turned = pltpu.roll(plane, LANES // 2, 1)
        high = upper(j) > 0
        even = jnp.where(high, jnp.where(low, 0.0, turned), jnp.where(low, plane, 0.0))
        odd = jnp.where(high, jnp.where(low, 0.0, plane), jnp.where(low, turned, 0.0))
        keep(j, [even, odd])


def partial_kernel(plan, tab, x_ref, w_ref, *refs):
    outs, done = refs[:-1], refs[-1]

    def body(unit):
        def held(slot):
            return x_ref[slot, rows_at(unit)]

        weights = [tap_weights(w_ref, unit, half, range(TAPS)) for half in range(2)]
        in_turn(
            plan["most"],
            4,
            lambda n: tap_sums(tab, plan["at"]["got_taps"] + (1 + TAPS) * n + 1, held, weights),
            lambda n, totals: keep_split_all(done, n, totals),
        )
        done[plan["most"]] = jnp.zeros(done.shape[1:], jnp.float32)
        at = 0
        for op, out in zip(plan["back_ops"], outs):
            send_tiles(
                op,
                lambda j, at=at: [
                    done[tab[plan["at"]["from_got"] + at + j], half] for half in range(2)
                ],
                lambda j, at=at: tab[plan["at"]["upper2"] + at + j],
                out,
                unit,
            )
            at += op["size"]

    over_units(w_ref, 2 * UNIT, body)


def forward_kernel(plan, tab, x_ref, w_ref, after, out):
    def body(unit):
        def held(slot):
            return x_ref[slot, rows_at(unit)]

        weights = [
            tap_weights(w_ref, unit, half, [*range(TAPS), BIAS_LANE]) for half in range(2)
        ]
        in_turn(
            plan["out_tiles"],
            4,
            lambda j: tap_sums(tab, plan["at"]["own_taps"] + TAPS * j, held, weights),
            lambda j, totals: keep_halves(
                out, j, unit, [totals[half] + weights[half][TAPS] for half in range(2)]
            ),
        )

    over_units(w_ref, 2 * UNIT, body)


def take_cots(plan, tab, unit, cot_ref, halos, cots):
    own = plan["out_tiles"]
    in_turn(
        own,
        5,
        lambda j: [cot_ref[j, half, rows_at(unit)] for half in range(2)],
        lambda j, v: keep_split_all(cots, j, v),
    )
    at = 0
    for op, ref in zip(plan["ops"], halos):
        received_tiles(
            op,
            ref,
            lambda j, at=at: tab[plan["at"]["upper1"] + at + j],
            lambda j, v, at=at: keep_split_all(cots, own + at + j, v),
            unit,
        )
        at += op["size"]
    cots[own + at] = jnp.zeros(cots.shape[1:], jnp.float32)


def keep_split_all(ref, j, values):
    for half, v in enumerate(values):
        ref[j, half] = v


def merge_cots(plan, tab, cots):
    for n in range(plan["n_merges"]):
        at = plan["at"]["merges"] + 2 * n
        for half in range(2):
            cots[tab[at], half] = cots[tab[at], half] + cots[tab[at + 1], half]


def weights_kernel(plan, tab, x_ref, cot_ref, *refs):
    halos = refs[: len(plan["sizes"])]
    sums_ref, cots, rows = refs[len(plan["sizes"]) :]
    step = pl.program_id(0)
    per = x_ref.shape[1] // UNIT
    zero = jnp.zeros((UNIT, LANES), jnp.float32)

    @pl.when(step == 0)
    def _():
        rows[...] = jnp.zeros_like(rows)

    def body(unit):
        take_cots(plan, tab, unit, cot_ref, halos, cots)
        here = step * per + unit
        for half in range(2):
            bias = cots[0, half]
            for j in range(1, plan["out_tiles"]):
                bias = bias + cots[j, half]
            rows[TAPS, of_half(half, here), :] = bias
        merge_cots(plan, tab, cots)
        for q, (kind, size) in enumerate(zip(plan["kinds"], plan["kind_sizes"])):
            width = 1 + len(kind)
            total = [[zero] * len(kind) for _ in range(2)]
            for j in range(size):
                at = plan["at"][f"kind{q}"] + width * j
                tile = x_ref[tab[at], rows_at(unit)]
                for n in range(len(kind)):
                    slot = tab[at + 1 + n]
                    for half in range(2):
                        total[half][n] = total[half][n] + cots[slot, half] * tile
            for n, t in enumerate(kind):
                for half in range(2):
                    rows[t, of_half(half, here), :] = total[half][n]

    lax.fori_loop(0, per, lambda u, c: (body(u), c)[1], 0)

    @pl.when(step == pl.num_programs(0) - 1)
    def _():
        lane = lax.broadcasted_iota(jnp.int32, (LANES, LANES), 1)

        def block(b, carry):
            here = pl.ds(pl.multiple_of(b * LANES, LANES), LANES)
            total = jnp.zeros((LANES, LANES), jnp.float32)
            for t in range(TAPS + 1):
                one = jnp.sum(rows[t, here, :], axis=1, keepdims=True)
                total = jnp.where(lane == t, one, total)
            sums_ref[:, here] = total.T[: 2 * SUBL]
            return carry

        lax.fori_loop(0, rows.shape[1] // LANES, block, 0)


def patches_kernel(plan, tab, cot_ref, w_ref, after, *refs):
    halos = refs[: len(plan["sizes"])]
    grad_ref, cots, back = refs[len(plan["sizes"]) :]

    def body(unit):
        take_cots(plan, tab, unit, cot_ref, halos, cots)
        merge_cots(plan, tab, cots)
        for q, (kind, size) in enumerate(zip(plan["kinds"], plan["kind_sizes"])):
            weights = [tap_weights(w_ref, unit, half, kind) for half in range(2)]
            width = 1 + len(kind)

            def one(j, q=q, kind=kind, weights=weights, width=width):
                at = plan["at"][f"kind{q}"] + width * j
                items = []
                for n in range(len(kind)):
                    slot = tab[at + 1 + n]
                    items += [cots[slot, half] * weights[half][n] for half in range(2)]
                return at, add_up(items)

            in_turn(size, 4, one, lambda j, v: back.__setitem__(tab[v[0]], v[1]))
        unalign_from(
            lambda t: back[t],
            lambda t, v: grad_ref.__setitem__((rows_at(unit), tile_lanes(t)), v),
            plan["n_in"],
            plan["in_tiles"],
            tab[0],
        )

    over_units(w_ref, 2 * UNIT, body)


def finish_kernel(plan, tab, own_ref, *refs):
    n_ops = len(plan["back_sizes"])
    halos = refs[:n_ops]
    out_ref, held, got = refs[n_ops:]
    tiles = plan["out_tiles"]

    def body(unit):
        at = 0
        for op, halo in zip(plan["back_ops"], halos):
            received_tiles(
                op,
                halo,
                lambda j, at=at: tab[plan["at"]["upper3"] + at + j],
                lambda j, v, at=at: keep_halves(got, at + j, 0, v),
                unit,
            )
            at += op["size"]
        got[at] = jnp.zeros(got.shape[1:], jnp.float32)

        def whole_sum(j):
            total = own_ref[j, both_at(unit)]
            for n in range(plan["n_adds"]):
                total = total + got[tab[plan["at"]["adds"] + plan["n_adds"] * j + n]]
            return total

        in_turn(tiles, 5, whole_sum, held.__setitem__)
        for part in range(2):
            unalign_from(
                lambda t: held[t, part * UNIT : (part + 1) * UNIT],
                lambda t, v: out_ref.__setitem__((rows_at(unit, part, 2), tile_lanes(t)), v),
                plan["n_out"],
                tiles,
                tab[1],
            )

    over_units(out_ref, 2 * UNIT, body)


def spread_kernel(groups, per_dev, rounds, me, parts, ci, cc, after, wide_out, turned_out, class_out, class_grad, grad_out, norms_out, wide, head, cots, classes):
    rows = round_up(per_dev, SUBL)
    n = ci.shape[0]
    channels = groups * per_dev
    wide[...] = jnp.zeros_like(wide)
    head[...] = jnp.zeros_like(head)
    lane = lax.broadcasted_iota(jnp.int32, (n, LANES), 1)
    at = 2 * rows
    for dev in range(groups):
        apart = jnp.bitwise_xor(me[0], dev)
        part = 0
        for place, bit in enumerate(rounds):
            part = part + jnp.bitwise_and(lax.div(apart, bit), 1) * 2**place
        wide[dev * per_dev : (dev + 1) * per_dev, :] = parts[part, :per_dev]
        head[dev * per_dev : (dev + 1) * per_dev, :LANES] = parts[part, rows : rows + per_dev]
        here = slice(dev * n, (dev + 1) * n)
        classes[here, :LANES] = parts[part, at : at + n]
        cots[here, :LANES] = parts[part, at + n : at + 2 * n]
        cots[here, LANES : 2 * LANES] = parts[part, at + 2 * n : at + 3 * n]
        rest = parts[part, at + 3 * n : at + 4 * n]
        ones = jnp.where(lane == 2 * SUBL, 1.0, 0.0)
        classes[here, LANES:] = jnp.where(lane < 2 * SUBL, rest, ones)
        rest = pltpu.roll(rest, LANES - 4 * SUBL, 1)
        cots[here, 2 * LANES :] = jnp.where(lane < 4 * SUBL, rest, 0.0)
    table = wide[...]
    wide_out[...] = table[:channels]
    for b in range(table.shape[0] // LANES):
        turned_out[:, tile_lanes(b)] = table[tile_lanes(b)].T
    lane = lax.broadcasted_iota(jnp.int32, table.shape, 1)
    rest = jnp.where(lane < 2 * SUBL, pltpu.roll(table, LANES - HEAD_LANE, 1), 0.0)
    bias = pltpu.roll(table, LANES - HEAD_BIAS_LANE + 2 * SUBL, 1)
    main = head[:, :LANES]
    norm_b = jnp.sum(jnp.where(lane == 2 * SUBL, bias * bias, 0.0))
    norm_w = jnp.sum(main * main) + jnp.sum(rest * rest)
    head[:, LANES:] = jnp.where(lane == 2 * SUBL, bias, rest)
    conv = jnp.sum(jnp.where(lane < TAPS, table * table, 0.0))
    conv_b = jnp.sum(jnp.where(lane == BIAS_LANE, table * table, 0.0))
    n_lane = lax.broadcasted_iota(jnp.int32, (SUBL, LANES), 1)
    norms = jnp.zeros((SUBL, LANES), jnp.float32)
    for k, v in enumerate((conv, conv_b, norm_w, norm_b)):
        norms = jnp.where(n_lane == k, v, norms)
    norms_out[...] = norms
    lane = lax.broadcasted_iota(jnp.int32, (n, 2 * LANES), 1)
    edge = LANES + 2 * SUBL
    mine = jnp.where(lane < edge, ci[...], jnp.where(lane == edge, 1.0, 0.0))
    last = (((1,), (1,)), ((), ()))
    first = (((0,), (0,)), ((), ()))
    plain = (((1,), (0,)), ((), ()))

    def dot(a, b, dims):
        return lax.dot_general(
            a, b, dims, precision=highest, preferred_element_type=jnp.float32
        )

    class_out[...] = dot(mine, head[:channels, :], last)
    lane = lax.broadcasted_iota(jnp.int32, (n, 3 * LANES), 1)
    my_cot = jnp.where(lane < channels, cc[...], 0.0)
    class_grad[...] = dot(my_cot, head[...], plain)[:, : class_grad.shape[1]]
    pick = pick_rows(channels, per_dev, me[0], cots.shape[1])
    picked = dot(cots[...], pick, plain)
    grad_out[...] = dot(picked, classes[...], first)[:rows]


def pick_rows(channels, per_dev, me, padded):
    shape = (padded, LANES)
    channel = lax.broadcasted_iota(jnp.int32, shape, 0) - me * per_dev
    column = lax.broadcasted_iota(jnp.int32, shape, 1)
    return jnp.where((channel == column) & (column < per_dev), 1.0, 0.0)


def update_kernel(channels, per_dev, me, sums, table, norms, cw, cb, fw, fb, sw, sb, aw, ab, hw, hu, ha, hb, hub, hab,
                  fw_out, sw_out, w_out, a_out, hw_out, ha_out, fb_out, sb_out, b_out, ab_out, hb_out, hab_out, ratio_out):
    padded = sums.shape[1]
    real = lax.broadcasted_iota(jnp.int32, (1, padded), 1) < channels
    wide = moments(
        table[0:TAPS], sums[0:TAPS], table[16 : 16 + TAPS], table[32 : 32 + TAPS], 0.05
    )[2]
    wide_b = moments(table[48:49], sums[TAPS : TAPS + 1], table[56:57], table[64:65], 0.0)[2]
    lane = lax.broadcasted_iota(jnp.int32, (1, LANES), 1)
    update_sq = sums[TAPS + 1 : TAPS + 2, :LANES]
    update_sq = pltpu.roll(update_sq, 2, 1)
    update_sq = jnp.where(lane == 0, jnp.sum(jnp.where(real, wide * wide, 0.0)), update_sq)
    update_sq = jnp.where(lane == 1, jnp.sum(jnp.where(real, wide_b * wide_b, 0.0)), update_sq)
    ratios = jnp.sqrt(norms[0:1, :]) / jnp.sqrt(update_sq)
    rates = [
        learn_rate * jnp.sum(jnp.where(lane == k, ratios, 0.0), axis=1, keepdims=True)
        for k in range(4)
    ]
    mine = lax.dot_general(
        sums[...],
        pick_rows(channels, per_dev, me[0], padded),
        (((1,), (0,)), ((), ())),
        precision=highest,
        preferred_element_type=jnp.float32,
    )
    first, second, update = moments(cw[...], mine[0:TAPS, :per_dev], fw[...], sw[...], 0.05)
    fw_out[...] = first
    sw_out[...] = second
    w_new = cw[...] - rates[0] * update
    w_out[...] = w_new
    a_out[...] = keep_rate * aw[...] + (1.0 - keep_rate) * w_new
    first, second, update = moments(
        cb[...], mine[TAPS : TAPS + 1, :per_dev], fb[...], sb[...], 0.0
    )
    w_new = cb[...] - rates[1] * update
    fb_out[...] = first.reshape(per_dev)
    sb_out[...] = second.reshape(per_dev)
    b_out[...] = w_new.reshape(per_dev)
    ab_out[...] = (keep_rate * ab[...] + (1.0 - keep_rate) * w_new).reshape(per_dev)
    w_new = hb[...] - rates[3] * hub[...]
    hb_out[...] = w_new.reshape(per_dev)
    hab_out[...] = (keep_rate * hab[...] + (1.0 - keep_rate) * w_new).reshape(per_dev)
    ratio_out[...] = ratios[:, :4].reshape(4)
    w_new = hw[...] - rates[2] * hu[...]
    hw_out[...] = w_new
    ha_out[...] = keep_rate * ha[...] + (1.0 - keep_rate) * w_new


def call(kernel, tables, operands, in_specs, outs, out_specs, scratch, steps, fills=False, tight=False):
    moved = sum(4 * int(np.prod(a.shape)) for a in operands) + sum(
        4 * int(np.prod(o.shape)) for o in outs
    )
    limit = 60
    if tight:
        blocks = [s.block_shape for s in [*in_specs, *out_specs] if s.block_shape]
        need = 8 * sum(int(np.prod(b)) for b in blocks)
        need += 4 * sum(int(np.prod(v.shape)) for v in scratch)
        limit = min(limit, max(24, need * 5 // 2**22 + 4))
    return pl.pallas_call(
        kernel,
        grid_spec=pltpu.PrefetchScalarGridSpec(
            num_scalar_prefetch=len(tables),
            grid=(steps,),
            in_specs=in_specs,
            out_specs=out_specs,
            scratch_shapes=scratch,
        ),
        out_shape=outs,
        compiler_params=pltpu.CompilerParams(
            dimension_semantics=("arbitrary",), vmem_limit_bytes=limit * 1024 * 1024
        ),
        cost_estimate=pl.CostEstimate(
            flops=1, bytes_accessed=moved if fills else 1, transcendentals=0
        ),
    )(*tables, *operands)


def whole(*shape):
    return pl.BlockSpec(shape, lambda g, *tab: (0,) * len(shape))


def round_up(n, m):
    return -(-n // m) * m


def f32(*shape):
    return jax.ShapeDtypeStruct(shape, jnp.float32)


def swap(x, axis, bit):
    size = lax.axis_size(axis)
    return lax.ppermute(x, axis, [(k, k ^ bit) for k in range(size)])


def bits_of(axis):
    size = lax.axis_size(axis)
    assert size & (size - 1) == 0
    bits, b = [], 1
    while b < size:
        bits.append(b)
        b *= 2
    return bits


def sum_over(x, axis):
    for bit in reversed(bits_of(axis)):
        x = x + swap(x, axis, bit)
    return x


def tied(one, many):
    one, many = lax.optimization_barrier((one, list(many)))
    return one, many


def moments(weight, grad, first, second, decay):
    first_new = beta_one * first + (1.0 - beta_one) * grad
    second_new = beta_two * second + (1.0 - beta_two) * grad * grad
    update = (
        first_new / fix_first / (jnp.sqrt(second_new / fix_second) + small_eps) + decay * weight
    )
    return (first_new, second_new, update)


def per_device(
    patches,
    class_in,
    conv_weight,
    conv_bias,
    head_weight,
    head_bias,
    first_conv_w,
    first_conv_b,
    first_head_w,
    first_head_b,
    second_conv_w,
    second_conv_b,
    second_head_w,
    second_head_b,
    average_conv_w,
    average_conv_b,
    average_head_w,
    average_head_b,
    pooled_cot,
    class_cot,
):
    groups = lax.axis_size("chan")
    me = lax.axis_index("chan")
    my_id = me.astype(jnp.int32)[None]
    per_dev = conv_weight.shape[0]
    n_in, channels_in = patches.shape[1:]
    n_out, channels = pooled_cot.shape[1:]
    local_images = class_in.shape[1]
    images = local_images * groups
    plan = make_plan(groups, images, n_in, n_out)
    tiles, in_tiles = plan["out_tiles"], plan["in_tiles"]
    table = lax.dynamic_index_in_dim(jnp.asarray(plan["table"]), me, 0, keepdims=False)
    per = 3
    steps = channels_in // (UNIT * per)
    x = patches[0].T
    cot = pooled_cot[0].T
    in_lanes, out_lanes = round_up(n_in, LANES), round_up(n_out, LANES)
    rows, wide_rows = UNIT * per, 2 * UNIT * per
    x_spec = pl.BlockSpec((rows, in_lanes), lambda g, tab: (g, 0))
    cot_spec = pl.BlockSpec((wide_rows, out_lanes), lambda g, tab: (g, 0))
    planes = [2 * op["full"] + op["half"] for op in plan["ops"]]
    halo_specs = [pl.BlockSpec((n, rows, LANES), lambda g, tab: (0, g, 0)) for n in planes]
    halo_outs = [f32(n, channels_in, LANES) for n in planes]
    planes = [2 * op["full"] + op["half"] for op in plan["back_ops"]]
    back_specs = [pl.BlockSpec((n, rows, LANES), lambda g, tab: (0, g, 0)) for n in planes]
    back_outs = [f32(n, channels_in, LANES) for n in planes]
    held_spec = pl.BlockSpec((in_tiles + 1, rows, LANES), lambda g, tab: (0, g, 0))
    split_spec = pl.BlockSpec((tiles, 2, rows, LANES), lambda g, tab: (0, 0, g, 0))
    own_spec = pl.BlockSpec((tiles, wide_rows, LANES), lambda g, tab: (0, g, 0))
    w_spec = pl.BlockSpec((wide_rows, LANES), lambda g, tab: (g, 0))
    anywhere = pl.BlockSpec(memory_space=pl.ANY)
    cot_held = pltpu.VMEM((tiles + 1, 2 * UNIT, LANES), jnp.float32)

    pd_rows = round_up(per_dev, SUBL)
    small_rows = 2 * pd_rows + 4 * local_images
    pieces = [
        conv_weight.T,
        conv_bias[None],
        first_conv_w.T,
        first_conv_b[None],
        second_conv_w.T,
        second_conv_b[None],
        head_bias[None],
        head_weight.T,
        class_in[0],
        class_cot[0],
    ]
    own_specs = [
        *(whole(*p.shape) for p in pieces[:7]),
        whole(pd_rows, 2 * LANES),
        whole(local_images, 2 * LANES),
        whole(local_images, 3 * LANES),
    ]
    small = call(
        functools.partial(small_kernel, per_dev),
        [],
        pieces,
        own_specs,
        [f32(small_rows, LANES)],
        [whole(small_rows, LANES)],
        [pltpu.VMEM((LANES, LANES), jnp.float32)],
        1,
    )[0]

    sends = call(
        functools.partial(pack_kernel, plan),
        [table],
        [cot, small],
        [cot_spec, anywhere],
        halo_outs,
        halo_specs,
        [cot_held],
        steps,
    )
    cot_split = call(
        functools.partial(align_cot_kernel, plan),
        [table],
        [cot, sends[0]],
        [cot_spec, anywhere],
        [f32(tiles, 2, channels_in, LANES)],
        [split_spec],
        [cot_held],
        steps,
    )[0]
    x_held = call(
        functools.partial(align_patches_kernel, plan),
        [table],
        [x, cot_split],
        [x_spec, anywhere],
        [f32(in_tiles + 1, channels_in, LANES)],
        [held_spec],
        [],
        steps,
    )[0]

    sends = list(sends)
    cot_halo = [None] * len(sends)
    parts = small[None]
    rounds = bits_of("chan")
    rounds = rounds[:1] + rounds[:0:-1]
    for bit in rounds:
        got = swap(parts, "chan", bit)
        if bit == 1:
            got, sends = tied(got, sends)
        elif bit == rounds[-1]:
            got, (x_held,) = tied(got, [x_held])
        elif bit == rounds[1]:
            got, (cot_split,) = tied(got, [cot_split])
        parts = jnp.concatenate([parts, got], axis=0)
        if bit == 1:
            parts, sends = tied(parts, sends)
            for n, op in enumerate(plan["ops"]):
                if op["near"]:
                    cot_halo[n] = lax.ppermute(sends[n], "chan", op["pairs"])
    parts, sends = tied(parts, sends)
    near = [n for n, op in enumerate(plan["ops"]) if op["near"]]
    if near:
        cot_halo[near[0]], sends = tied(cot_halo[near[0]], sends)
    for n, op in enumerate(plan["ops"]):
        if not op["near"]:
            cot_halo[n] = lax.ppermute(sends[n], "chan", op["pairs"])
    padded = round_up(channels, LANES)
    wide, turned, class_out, class_grad, grad_h, weight_norms = call(
        functools.partial(spread_kernel, groups, per_dev, rounds),
        [my_id],
        [parts, class_in[0], class_cot[0], x_held],
        [whole(*parts.shape), own_specs[8], own_specs[9], anywhere],
        [
            f32(channels, LANES),
            f32(LANES, padded),
            f32(local_images, channels),
            f32(local_images, channels_in),
            f32(pd_rows, 2 * LANES),
            f32(SUBL, LANES),
        ],
        [
            whole(channels, LANES),
            whole(LANES, padded),
            whole(local_images, channels),
            whole(local_images, channels_in),
            whole(pd_rows, 2 * LANES),
            whole(SUBL, LANES),
        ],
        [
            pltpu.VMEM((padded, LANES), jnp.float32),
            pltpu.VMEM((padded, 2 * LANES), jnp.float32),
            pltpu.VMEM((images, 3 * LANES), jnp.float32),
            pltpu.VMEM((images, 2 * LANES), jnp.float32),
        ],
        1,
    )

    partials = call(
        functools.partial(partial_kernel, plan),
        [table],
        [x_held, wide],
        [held_spec, w_spec],
        back_outs,
        back_specs,
        [pltpu.VMEM((plan["most"] + 1, 2, UNIT, LANES), jnp.float32)],
        steps,
        tight=True,
    )
    partials, late = list(partials), []
    pooled_halo = [None] * len(partials)
    for n, op in enumerate(plan["back_ops"]):
        if op["early"]:
            pooled_halo[n] = lax.ppermute(partials[n], "chan", op["pairs"])
        else:
            late.append(n)
    grad_h = sum_over(grad_h, "dp")
    head_t = head_weight.T
    head_first, head_second, head_update = moments(
        head_t, grad_h[:per_dev, :channels_in], first_head_w.T, second_head_w.T, 0.05
    )
    bias_first, bias_second, bias_update = moments(
        head_bias, grad_h[:per_dev, channels_in], first_head_b, second_head_b, 0.0
    )
    norms = [jnp.sum(head_update**2), jnp.sum(bias_update**2)]

    pooled_own = call(
        functools.partial(forward_kernel, plan),
        [table],
        [x_held, wide, head_update],
        [held_spec, w_spec, anywhere],
        [f32(tiles, channels, LANES)],
        [own_spec],
        [],
        steps,
        tight=True,
    )[0]

    waiting = [partials[n] for n in late]
    waiting, cot_halo, pooled_own, norms = lax.optimization_barrier(
        (waiting, cot_halo, pooled_own, norms)
    )
    for n, v in zip(late, waiting):
        pooled_halo[n] = lax.ppermute(v, "chan", plan["back_ops"][n]["pairs"])
    cots_held = pltpu.VMEM((tiles + plan["halo"] + 1, 2, UNIT, LANES), jnp.float32)
    sums = call(
        functools.partial(weights_kernel, plan),
        [table],
        [x_held, cot_split, *cot_halo],
        [held_spec, split_spec, *halo_specs],
        [f32(2 * SUBL, padded)],
        [whole(2 * SUBL, padded)],
        [cots_held, pltpu.VMEM((TAPS + 1, padded, LANES), jnp.float32)],
        steps,
        tight=True,
    )[0]
    x_grad = call(
        functools.partial(patches_kernel, plan),
        [table],
        [cot_split, wide, sums, *cot_halo],
        [split_spec, w_spec, anywhere, *halo_specs],
        [f32(channels_in, n_in)],
        [x_spec],
        [cots_held, pltpu.VMEM((in_tiles + 1, UNIT, LANES), jnp.float32)],
        steps,
        tight=True,
    )[0]
    sums = sum_over(sums, "dp")
    row = lax.broadcasted_iota(jnp.int32, sums.shape, 0)
    lane = lax.broadcasted_iota(jnp.int32, sums.shape, 1)
    for k, v in enumerate(norms):
        sums = jnp.where((row == TAPS + 1) & (lane == k), v, sums)
    pooled = call(
        functools.partial(finish_kernel, plan),
        [table],
        [pooled_own, *pooled_halo],
        [own_spec, *back_specs],
        [f32(channels, n_out)],
        [cot_spec],
        [cot_held, pltpu.VMEM((plan["back_halo"] + 1, 2 * UNIT, LANES), jnp.float32)],
        steps,
        tight=True,
    )[0]
    for bit in bits_of("chan")[::-1]:
        got = swap(sums, "chan", bit)
        if bit == bits_of("chan")[-1]:
            got, (x_grad,) = tied(got, [x_grad])
        if bit == 1:
            got, (pooled,) = tied(got, [pooled])
        sums = sums + got
    conv_shapes = [f32(TAPS, per_dev)] * 4
    head_shapes = [f32(per_dev, channels_in)] * 2
    operands = [
        sums,
        turned,
        weight_norms,
        *pieces[:6],
        average_conv_w.T,
        average_conv_b[None],
        head_t,
        head_update,
        average_head_w.T,
        head_bias[None],
        bias_update[None],
        average_head_b[None],
    ]
    specs = [whole(*v.shape) for v in operands]
    out_shapes = [*conv_shapes, *head_shapes, *[f32(per_dev)] * 6, f32(4)]
    *new, trust = call(
        functools.partial(update_kernel, channels, per_dev),
        [my_id],
        operands,
        specs,
        out_shapes,
        [whole(*v.shape) for v in out_shapes],
        [],
        1,
    )

    conv_new, (head_new, head_average), bias_new = new[:4], new[4:6], new[6:]
    return (
        pooled.T[None],
        class_out[None],
        x_grad.T[None],
        class_grad[None],
        *(v.T for v in conv_new),
        *bias_new[:4],
        head_first.T,
        head_second.T,
        head_new.T,
        head_average.T,
        bias_first,
        bias_second,
        *bias_new[4:],
        trust,
    )


def solution(mesh):
    return jax.shard_map(
        per_device,
        mesh=mesh,
        in_specs=(
            P("dp", "chan", None),
            P("dp", "chan", None),
            P("chan", None),
            P("chan"),
            P(None, "chan"),
            P("chan"),
            P("chan", None),
            P("chan"),
            P(None, "chan"),
            P("chan"),
            P("chan", None),
            P("chan"),
            P(None, "chan"),
            P("chan"),
            P("chan", None),
            P("chan"),
            P(None, "chan"),
            P("chan"),
            P("dp", "chan", None),
            P("dp", "chan", None),
        ),
        out_specs=(
            P("dp", "chan", None),
            P("dp", "chan", None),
            P("dp", "chan", None),
            P("dp", "chan", None),
            P("chan", None),
            P("chan", None),
            P("chan", None),
            P("chan", None),
            P("chan"),
            P("chan"),
            P("chan"),
            P("chan"),
            P(None, "chan"),
            P(None, "chan"),
            P(None, "chan"),
            P(None, "chan"),
            P("chan"),
            P("chan"),
            P("chan"),
            P("chan"),
            P(),
        ),
        check_vma=False,
    )
```

```python
import functools
import types

import jax
import jax.numpy as jnp
import numpy as np
from jax import lax
from jax.experimental import pallas as pl
from jax.experimental.pallas import tpu as pltpu
from jax.sharding import PartitionSpec as P

GRID = 27
TAPS = 9
OUTG = 14
LANES = 128
SUBL = 8
CHAN = "chan"
UNIT = 16

beta_one = 0.9
beta_two = 0.999
fix_first = 1.0 - 0.9**10
fix_second = 1.0 - 0.999**10
small_eps = 1e-06
learn_rate = 0.5
keep_rate = 0.9
highest = lax.Precision.HIGHEST


def sized(parts):
    full = max(len(f) for _, (f, _) in parts)
    half = max(len(h) for _, (_, h) in parts)
    return types.SimpleNamespace(
        full=full,
        half=half,
        size=full + half,
        parts=parts,
        pairs=[pair for pair, _ in parts],
        tiles=[
            [(j, *v) for j, v in enumerate(f)] + [(full + j, *v) for j, v in enumerate(h)]
            for _, (f, h) in parts
        ],
        near=all(src ^ dst == 1 for (src, dst), _ in parts),
    )


def halves(message):
    return 2 * len(message[0]) + len(message[1])


def free_in(parts, pair):
    return all(pair[0] != s and pair[1] != d for (s, d), _ in parts)


def grouped(messages, spare):
    groups = []
    for pair, message in sorted(messages, key=lambda kv: (-halves(kv[1]), kv[0])):
        for parts in groups:
            first = parts[0][1]
            if (
                len(message[0]) <= len(first[0])
                and len(message[1]) <= len(first[1])
                and halves(first) - halves(message) <= 2 * spare
                and free_in(parts, pair)
            ):
                break
        else:
            parts = []
            groups.append(parts)
        parts.append((pair, message))
    return [sized(parts) for parts in groups]


def loads(ops, groups):
    got = np.zeros(groups, np.int64)
    for op in ops:
        for _, dst in op.pairs:
            got[dst] += 2 * op.full + op.half
    return got


def joined(ops, others, groups):
    for n in range(1, len(ops)):
        for m in range(n):
            if not (ops[n].near and ops[m].near):
                continue
            for pair, message in list(ops[n].parts):
                got = loads(ops + others, groups)
                more = halves(ops[m].parts[0][1]) - 2 * ops[n].full - ops[n].half
                if (
                    len(ops[n].parts) > 1
                    and free_in(ops[m].parts, pair)
                    and got[pair[1]] + more < 0.9 * max(got)
                ):
                    ops[n] = sized([v for v in ops[n].parts if v[0] != pair])
                    ops[m] = sized(ops[m].parts + [(pair, message)])
    return ops


def make_plan(groups, images, n_in, n_out):
    tiles_img = images // LANES
    n_tiles = OUTG * OUTG * tiles_img
    tap_tile = np.full((n_tiles, TAPS), -1, np.int64)
    for i in range(OUTG):
        for j in range(OUTG):
            for it in range(tiles_img):
                for a in range(3):
                    for e in range(3):
                        r, s = 2 * i + a - 1, 2 * j + e - 1
                        if 0 <= r < GRID and 0 <= s < GRID:
                            tap_tile[(i * OUTG + j) * tiles_img + it, 3 * a + e] = (
                                r * GRID + s
                            ) * tiles_img + it
    step = int(np.gcd(np.gcd(n_in, n_out), LANES))
    wanted = {}
    for lane in range(0, LANES, step):
        p_owner = (np.arange(n_tiles) * LANES + lane) // n_out
        t_owner = (tap_tile * LANES + lane) // n_in
        for p in range(n_tiles):
            k = int(p_owner[p])
            for t in range(TAPS):
                if tap_tile[p, t] >= 0 and t_owner[p, t] != k:
                    lanes = wanted.setdefault((k, int(t_owner[p, t])), {}).setdefault(p, set())
                    lanes.update((lane, lane + step - 1))
    middle = LANES // 2
    for pair, tiles in wanted.items():
        full, half = [], []
        for p, lanes in sorted(tiles.items()):
            low, high = max(lanes) < middle, min(lanes) >= middle
            (half if low or high else full).append((p, int(high)))
        wanted[pair] = (full, half)
    near = {p: t for p, t in wanted.items() if p[0] ^ p[1] == 1}
    weight = {p: 2 * len(t[0]) + len(t[1]) for p, t in near.items()}
    even = max([min(w, weight.get(p[::-1], 0)) for p, w in weight.items()], default=0)
    begin, rest = [], []
    for p, (full, half) in near.items():
        some = max(even - len(half), 0) // 2
        begin.append((p, (full[:some], half)))
        if full[some:]:
            rest.append((p, (full[some:], [])))
    ops = grouped(begin, even) + grouped(rest, 2)
    ops += grouped([(p, t) for p, t in wanted.items() if p[0] ^ p[1] != 1], 2)
    back_ops = grouped([((d, s), t) for (s, d), t in wanted.items()], 2)
    back_ops = joined(back_ops, ops, groups)
    longest = max(op.size for op in back_ops)
    for op in back_ops:
        op.early = op.near and 4 * op.size > 3 * longest
    in_base = np.arange(groups) * n_in // LANES
    in_shift = np.arange(groups) * n_in % LANES
    out_base = np.arange(groups) * n_out // LANES
    out_shift = np.arange(groups) * n_out % LANES
    in_tiles = int(max(-(-(in_shift + n_in) // LANES)))
    out_tiles = int(max(-(-(out_shift + n_out) // LANES)))
    sizes = [op.size for op in ops]
    halo = sum(sizes)
    back_sizes = [op.size for op in back_ops]
    back_halo = sum(back_sizes)
    owned = [
        range(int(out_base[k]), int(out_base[k]) - (-(int(out_shift[k]) + n_out) // LANES))
        for k in range(groups)
    ]
    none = out_tiles + halo
    own_slot = np.full((groups, halo), out_tiles, np.int64)
    got = [[] for _ in range(groups)]
    upper = np.zeros((4, groups, max(halo, back_halo)), np.int64)
    start = 0
    for op in ops:
        for (src, dst), tiles in zip(op.pairs, op.tiles):
            for j, p, high in tiles:
                own_slot[src, start + j] = p - out_base[src]
                got[dst].append((p, start + j))
                upper[0, src, start + j] = upper[1, dst, start + j] = high
        start += op.size
    most = max(len(v) for v in got)

    def tap_rows(device, p):
        local = tap_tile[p] - in_base[device]
        first, last = device * n_in, (device + 1) * n_in
        held = (
            (tap_tile[p] >= 0)
            & (tap_tile[p] * LANES < last)
            & ((tap_tile[p] + 1) * LANES > first)
        )
        return np.where(held, local, in_tiles)

    own_taps = np.full((groups, out_tiles, TAPS), in_tiles, np.int64)
    got_taps = np.full((groups, most, 1 + TAPS), in_tiles, np.int64)
    got_taps[:, :, 0] = none
    from_got = np.full((groups, back_halo), most, np.int64)
    adds = [[[] for _ in range(out_tiles)] for _ in range(groups)]
    merges, slot_of = [], []
    for k in range(groups):
        for j, p in enumerate(owned[k]):
            own_taps[k, j] = tap_rows(k, p)
        slot_of.append({p: j for j, p in enumerate(owned[k])})
        merges.append([])
        for n, (p, place) in enumerate(got[k]):
            got_taps[k, n, 0] = out_tiles + place
            got_taps[k, n, 1:] = tap_rows(k, p)
            if p in slot_of[k]:
                merges[k].append([slot_of[k][p], out_tiles + place])
            else:
                slot_of[k][p] = out_tiles + place
    start = 0
    for op in back_ops:
        for (src, dst), tiles in zip(op.pairs, op.tiles):
            names = [p for p, _ in got[src]]
            for j, p, high in tiles:
                from_got[src, start + j] = names.index(p)
                adds[dst][p - out_base[dst]].append(start + j)
                upper[2, src, start + j] = upper[3, dst, start + j] = high
        start += op.size
    n_merges = max(len(v) for v in merges)
    merges = np.array([v + [[none, none]] * (n_merges - len(v)) for v in merges], np.int64)
    n_adds = max(len(v) for per_dev in adds for v in per_dev)
    adds = np.array([[v + [back_halo] * (n_adds - len(v)) for v in per_dev] for per_dev in adds])
    kinds = [
        [(a, e) for a in ((1,), (0, 2))[row_odd] for e in ((1,), (0, 2))[col_odd]]
        for row_odd in range(2)
        for col_odd in range(2)
    ]
    lists = [[[] for _ in range(groups)] for _ in kinds]
    for k in range(groups):
        count = -(-(int(in_shift[k]) + n_in) // LANES)
        for t in range(count):
            position, it = divmod(int(in_base[k]) + t, tiles_img)
            r, s = divmod(position, GRID)
            kind = 2 * (r % 2) + s % 2
            entry = [t]
            for a, e in kinds[kind]:
                i, j = (r + 1 - a) // 2, (s + 1 - e) // 2
                entry.append(slot_of[k].get((i * OUTG + j) * tiles_img + it, none))
            lists[kind][k].append(entry)
    reach_tables, kind_sizes = [], []
    for kind, per_device_lists in enumerate(lists):
        width = 1 + len(kinds[kind])
        size = max(len(v) for v in per_device_lists)
        kind_sizes.append(size)
        filler = [in_tiles] + [none] * (width - 1)
        reach_tables.append(
            np.array([v + [filler] * (size - len(v)) for v in per_device_lists]).reshape(groups, -1)
        )
    parts = types.SimpleNamespace(
        shifts=np.stack([in_shift, out_shift], axis=1),
        own_slot=own_slot,
        own_taps=own_taps.reshape(groups, -1),
        got_taps=got_taps.reshape(groups, -1),
        from_got=from_got,
        merges=merges.reshape(groups, -1),
        adds=adds.reshape(groups, -1),
        upper=list(upper),
        kinds=reach_tables,
    )
    at, total, columns = types.SimpleNamespace(), 0, []
    for name, v in vars(parts).items():
        places = []
        for one in v if isinstance(v, list) else [v]:
            places.append(total)
            total += one.shape[1]
            columns.append(one)
        setattr(at, name, places if isinstance(v, list) else places[0])
    return types.SimpleNamespace(
        ops=ops,
        sizes=sizes,
        halo=halo,
        back_ops=back_ops,
        back_sizes=back_sizes,
        back_halo=back_halo,
        in_tiles=in_tiles,
        out_tiles=out_tiles,
        most=most,
        n_merges=n_merges,
        n_adds=n_adds,
        n_in=n_in,
        n_out=n_out,
        kinds=[[3 * a + e for a, e in kind] for kind in kinds],
        kind_sizes=kind_sizes,
        at=at,
        table=np.concatenate(columns, axis=1).astype(np.int32),
    )


def lane_ids():
    return lax.broadcasted_iota(jnp.int32, (UNIT, LANES), 1)


def align_into(load, store, n_local, tiles, shift):
    lane = lane_ids()
    zero = jnp.zeros((UNIT, LANES), jnp.float32)
    local_tiles = -(-n_local // LANES)
    before = zero
    for t in range(tiles):
        if t < local_tiles:
            now = load(t)
            if (t + 1) * LANES > n_local:
                now = jnp.where(lane < n_local - t * LANES, now, 0.0)
            now = pltpu.roll(now, shift, 1)
        else:
            now = zero
        store(t, jnp.where(lane < shift, before, now))
        before = now
    store(tiles, zero)


def unalign_from(load, store, n_local, tiles, shift):
    lane = lane_ids()
    local_tiles = -(-n_local // LANES)
    back = lax.rem(LANES - shift, LANES)
    now = pltpu.roll(load(0), back, 1)
    for t in range(local_tiles):
        later = pltpu.roll(load(t + 1), back, 1) if t + 1 < tiles else now
        store(t, jnp.where(lane < LANES - shift, now, later))
        now = later


def tile_lanes(t):
    return slice(t * LANES, (t + 1) * LANES)


def rows_at(unit, part=0, parts=1):
    return pl.ds(pl.multiple_of((unit * parts + part) * UNIT, UNIT), UNIT)


def both_at(unit):
    return pl.ds(pl.multiple_of(unit * 2 * UNIT, UNIT), 2 * UNIT)


def of_half(half, unit=0):
    return pl.ds(unit * 2 * UNIT + half, UNIT, stride=2)


def align_cot(cot_ref, unit, held, plan, shift):
    for part in range(2):
        align_into(
            lambda t: cot_ref[rows_at(unit, part, 2), tile_lanes(t)],
            lambda t, v: held.__setitem__((t, slice(part * UNIT, (part + 1) * UNIT)), v),
            plan.n_out,
            plan.out_tiles,
            shift,
        )


def tap_weights(w_ref, unit, half, lanes):
    rows = w_ref[of_half(half, unit), :]
    return [jnp.broadcast_to(rows[:, t : t + 1], (UNIT, LANES)) for t in lanes]


def in_turn(count, size, make, keep):
    for first in range(0, count, size):
        some = range(first, min(first + size, count))
        for j, v in [(j, make(j)) for j in some]:
            keep(j, v)


def over_units(ref, rows, body):
    lax.fori_loop(0, ref.shape[0] // rows, lambda u, c: (body(u), c)[1], 0)


def add_up(items):
    items = list(items)
    while len(items) > 1:
        items = [
            items[i] + items[i + 1] if i + 1 < len(items) else items[i]
            for i in range(0, len(items), 2)
        ]
    return items[0]


BIAS_LANE = 48
HEAD_BIAS_LANE = 72
HEAD_LANE = 96


def small_kernel(per_dev, me, cw, cb, fw, fb, sw, sb, hb, hw, ci, cc, row, out, row_out, square):
    row_out[...] = row[...]
    square[...] = jnp.zeros_like(square)
    for part, (w, b) in enumerate(((cw, cb), (fw, fb), (sw, sb))):
        square[2 * SUBL * part : 2 * SUBL * part + TAPS, :per_dev] = w[...]
        square[BIAS_LANE + SUBL * part : BIAS_LANE + SUBL * part + 1, :per_dev] = b[...]
    square[HEAD_BIAS_LANE : HEAD_BIAS_LANE + 1, :per_dev] = hb[...]
    turned = square[...].T
    rows = hw.shape[0]
    lane = lax.broadcasted_iota(jnp.int32, (rows, LANES), 1)
    rest = pltpu.roll(jnp.where(lane < 2 * SUBL, hw[:, LANES:], 0.0), HEAD_LANE, 1)
    out[0:rows] = jnp.where(lane < HEAD_LANE, turned[0:rows], rest)
    out[rows : 2 * rows] = hw[:, :LANES]
    at, n = 2 * rows, ci.shape[0]
    out[at : at + n] = ci[:, :LANES]
    out[at + n : at + 2 * n] = cc[:, :LANES]
    out[at + 2 * n : at + 3 * n] = cc[:, LANES : 2 * LANES]
    lane = lax.broadcasted_iota(jnp.int32, (n, LANES), 1)
    left = jnp.where(lane < 2 * SUBL, ci[:, LANES:], 0.0)
    right = pltpu.roll(jnp.where(lane < 4 * SUBL, cc[:, 2 * LANES :], 0.0), 4 * SUBL, 1)
    out[at + 3 * n : at + 4 * n] = jnp.where(lane < 4 * SUBL, left, right)


def align_patches_kernel(plan, tab, x_ref, after, x_out):
    def body(unit):
        align_into(
            lambda t: x_ref[rows_at(unit), tile_lanes(t)],
            lambda t, v: x_out.__setitem__((t, rows_at(unit)), v),
            plan.n_in,
            plan.in_tiles,
            tab[0],
        )

    over_units(x_ref, UNIT, body)


def align_cot_kernel(plan, tab, cot_ref, after, cot_out, held):
    def body(unit):
        align_cot(cot_ref, unit, held, plan, tab[1])
        for j in range(plan.out_tiles):
            for half in range(2):
                cot_out[j, half, rows_at(unit)] = held[j, of_half(half)]

    over_units(cot_ref, 2 * UNIT, body)


def pack_kernel(plan, tab, cot_ref, after, *refs):
    outs, held = refs[:-1], refs[-1]

    def body(unit):
        align_cot(cot_ref, unit, held, plan, tab[1])
        at = 0
        for op, out in zip(plan.ops, outs):
            send_tiles(
                op,
                lambda j, at=at: [
                    held[tab[plan.at.own_slot + at + j], of_half(half)] for half in range(2)
                ],
                lambda j, at=at: tab[plan.at.upper[0] + at + j],
                out,
                unit,
            )
            at += op.size

    over_units(cot_ref, 2 * UNIT, body)


def tap_sums(tab, at, held, weights):
    totals = [None, None]
    for t in range(TAPS):
        tile = held(tab[at + t])
        for half in range(2):
            term = tile * weights[half][t]
            totals[half] = term if t == 0 else totals[half] + term
    return totals


def keep_halves(ref, j, unit, values):
    for half, v in enumerate(values):
        ref[j, of_half(half, unit)] = v


def send_tiles(op, load, upper, out, unit):
    def store(j, pair):
        for half, v in enumerate(pair):
            out[2 * j + half, rows_at(unit)] = v

    in_turn(op.full, 6, load, store)
    low = lane_ids() < LANES // 2
    for j in range(op.full, op.size):
        even, odd = load(j)
        high = upper(j) > 0
        left = jnp.where(high, pltpu.roll(even, LANES // 2, 1), even)
        right = jnp.where(high, odd, pltpu.roll(odd, LANES // 2, 1))
        out[op.full + j, rows_at(unit)] = jnp.where(low, left, right)


def received_tiles(op, ref, upper, keep, unit):
    in_turn(
        op.full,
        5,
        lambda j: [ref[2 * j + half, rows_at(unit)] for half in range(2)],
        keep,
    )
    low = lane_ids() < LANES // 2
    for j in range(op.full, op.size):
        plane = ref[op.full + j, rows_at(unit)]
        turned = pltpu.roll(plane, LANES // 2, 1)
        high = upper(j) > 0
        even = jnp.where(high, jnp.where(low, 0.0, turned), jnp.where(low, plane, 0.0))
        odd = jnp.where(high, jnp.where(low, 0.0, plane), jnp.where(low, turned, 0.0))
        keep(j, [even, odd])


def partial_kernel(plan, tab, x_ref, w_ref, *refs):
    outs, done = refs[:-1], refs[-1]

    def body(unit):
        def held(slot):
            return x_ref[slot, rows_at(unit)]

        weights = [tap_weights(w_ref, unit, half, range(TAPS)) for half in range(2)]
        in_turn(
            plan.most,
            4,
            lambda n: tap_sums(tab, plan.at.got_taps + (1 + TAPS) * n + 1, held, weights),
            lambda n, totals: keep_split_all(done, n, totals),
        )
        done[plan.most] = jnp.zeros(done.shape[1:], jnp.float32)
        at = 0
        for op, out in zip(plan.back_ops, outs):
            send_tiles(
                op,
                lambda j, at=at: [
                    done[tab[plan.at.from_got + at + j], half] for half in range(2)
                ],
                lambda j, at=at: tab[plan.at.upper[2] + at + j],
                out,
                unit,
            )
            at += op.size

    over_units(w_ref, 2 * UNIT, body)


def forward_kernel(plan, tab, x_ref, w_ref, after, out):
    def body(unit):
        def held(slot):
            return x_ref[slot, rows_at(unit)]

        weights = [
            tap_weights(w_ref, unit, half, [*range(TAPS), BIAS_LANE]) for half in range(2)
        ]
        in_turn(
            plan.out_tiles,
            4,
            lambda j: tap_sums(tab, plan.at.own_taps + TAPS * j, held, weights),
            lambda j, totals: keep_halves(
                out, j, unit, [totals[half] + weights[half][TAPS] for half in range(2)]
            ),
        )

    over_units(w_ref, 2 * UNIT, body)


def take_cots(plan, tab, unit, cot_ref, halos, cots):
    own = plan.out_tiles
    in_turn(
        own,
        5,
        lambda j: [cot_ref[j, half, rows_at(unit)] for half in range(2)],
        lambda j, v: keep_split_all(cots, j, v),
    )
    at = 0
    for op, ref in zip(plan.ops, halos):
        received_tiles(
            op,
            ref,
            lambda j, at=at: tab[plan.at.upper[1] + at + j],
            lambda j, v, at=at: keep_split_all(cots, own + at + j, v),
            unit,
        )
        at += op.size
    cots[own + at] = jnp.zeros(cots.shape[1:], jnp.float32)


def keep_split_all(ref, j, values):
    for half, v in enumerate(values):
        ref[j, half] = v


def merge_cots(plan, tab, cots):
    for n in range(plan.n_merges):
        at = plan.at.merges + 2 * n
        for half in range(2):
            cots[tab[at], half] = cots[tab[at], half] + cots[tab[at + 1], half]


def weights_kernel(plan, tab, x_ref, cot_ref, *refs):
    halos = refs[: len(plan.sizes)]
    sums_ref, cots, rows = refs[len(plan.sizes) :]
    step = pl.program_id(0)
    per = x_ref.shape[1] // UNIT
    zero = jnp.zeros((UNIT, LANES), jnp.float32)

    @pl.when(step == 0)
    def _():
        rows[...] = jnp.zeros_like(rows)

    def body(unit):
        take_cots(plan, tab, unit, cot_ref, halos, cots)
        here = step * per + unit
        for half in range(2):
            bias = cots[0, half]
            for j in range(1, plan.out_tiles):
                bias = bias + cots[j, half]
            rows[TAPS, of_half(half, here), :] = bias
        merge_cots(plan, tab, cots)
        for q, (kind, size) in enumerate(zip(plan.kinds, plan.kind_sizes)):
            width = 1 + len(kind)
            total = [[zero] * len(kind) for _ in range(2)]
            for j in range(size):
                at = plan.at.kinds[q] + width * j
                tile = x_ref[tab[at], rows_at(unit)]
                for n in range(len(kind)):
                    slot = tab[at + 1 + n]
                    for half in range(2):
                        total[half][n] = total[half][n] + cots[slot, half] * tile
            for n, t in enumerate(kind):
                for half in range(2):
                    rows[t, of_half(half, here), :] = total[half][n]

    lax.fori_loop(0, per, lambda u, c: (body(u), c)[1], 0)

    @pl.when(step == pl.num_programs(0) - 1)
    def _():
        lane = lax.broadcasted_iota(jnp.int32, (LANES, LANES), 1)

        def block(b, carry):
            here = pl.ds(pl.multiple_of(b * LANES, LANES), LANES)
            total = jnp.zeros((LANES, LANES), jnp.float32)
            for t in range(TAPS + 1):
                one = jnp.sum(rows[t, here, :], axis=1, keepdims=True)
                total = jnp.where(lane == t, one, total)
            sums_ref[:, here] = total.T[: 2 * SUBL]
            return carry

        lax.fori_loop(0, rows.shape[1] // LANES, block, 0)


def patches_kernel(plan, tab, cot_ref, w_ref, after, *refs):
    halos = refs[: len(plan.sizes)]
    grad_ref, cots, back = refs[len(plan.sizes) :]

    def body(unit):
        take_cots(plan, tab, unit, cot_ref, halos, cots)
        merge_cots(plan, tab, cots)
        for q, (kind, size) in enumerate(zip(plan.kinds, plan.kind_sizes)):
            weights = [tap_weights(w_ref, unit, half, kind) for half in range(2)]
            width = 1 + len(kind)

            def one(j, q=q, kind=kind, weights=weights, width=width):
                at = plan.at.kinds[q] + width * j
                items = []
                for n in range(len(kind)):
                    slot = tab[at + 1 + n]
                    items += [cots[slot, half] * weights[half][n] for half in range(2)]
                return at, add_up(items)

            in_turn(size, 4, one, lambda j, v: back.__setitem__(tab[v[0]], v[1]))
        unalign_from(
            lambda t: back[t],
            lambda t, v: grad_ref.__setitem__((rows_at(unit), tile_lanes(t)), v),
            plan.n_in,
            plan.in_tiles,
            tab[0],
        )

    over_units(w_ref, 2 * UNIT, body)


def finish_kernel(plan, tab, own_ref, *refs):
    n_ops = len(plan.back_sizes)
    halos = refs[:n_ops]
    out_ref, held, got = refs[n_ops:]
    tiles = plan.out_tiles

    def body(unit):
        at = 0
        for op, halo in zip(plan.back_ops, halos):
            received_tiles(
                op,
                halo,
                lambda j, at=at: tab[plan.at.upper[3] + at + j],
                lambda j, v, at=at: keep_halves(got, at + j, 0, v),
                unit,
            )
            at += op.size
        got[at] = jnp.zeros(got.shape[1:], jnp.float32)

        def whole_sum(j):
            total = own_ref[j, both_at(unit)]
            for n in range(plan.n_adds):
                total = total + got[tab[plan.at.adds + plan.n_adds * j + n]]
            return total

        in_turn(tiles, 5, whole_sum, held.__setitem__)
        for part in range(2):
            unalign_from(
                lambda t: held[t, part * UNIT : (part + 1) * UNIT],
                lambda t, v: out_ref.__setitem__((rows_at(unit, part, 2), tile_lanes(t)), v),
                plan.n_out,
                tiles,
                tab[1],
            )

    over_units(out_ref, 2 * UNIT, body)


def spread_kernel(groups, per_dev, rounds, me, parts, ci, cc, after, wide_out, turned_out, class_out, class_grad, grad_out, norms_out, wide, head, cots, classes):
    rows = round_up(per_dev, SUBL)
    n = ci.shape[0]
    channels = groups * per_dev
    wide[...] = jnp.zeros_like(wide)
    head[...] = jnp.zeros_like(head)
    lane = lax.broadcasted_iota(jnp.int32, (n, LANES), 1)
    at = 2 * rows
    for dev in range(groups):
        apart = jnp.bitwise_xor(me[0], dev)
        part = 0
        for place, bit in enumerate(rounds):
            part = part + jnp.bitwise_and(lax.div(apart, bit), 1) * 2**place
        wide[dev * per_dev : (dev + 1) * per_dev, :] = parts[part, :per_dev]
        head[dev * per_dev : (dev + 1) * per_dev, :LANES] = parts[part, rows : rows + per_dev]
        here = slice(dev * n, (dev + 1) * n)
        classes[here, :LANES] = parts[part, at : at + n]
        cots[here, :LANES] = parts[part, at + n : at + 2 * n]
        cots[here, LANES : 2 * LANES] = parts[part, at + 2 * n : at + 3 * n]
        rest = parts[part, at + 3 * n : at + 4 * n]
        ones = jnp.where(lane == 2 * SUBL, 1.0, 0.0)
        classes[here, LANES:] = jnp.where(lane < 2 * SUBL, rest, ones)
        rest = pltpu.roll(rest, LANES - 4 * SUBL, 1)
        cots[here, 2 * LANES :] = jnp.where(lane < 4 * SUBL, rest, 0.0)
    table = wide[...]
    wide_out[...] = table[:channels]
    for b in range(table.shape[0] // LANES):
        turned_out[:, tile_lanes(b)] = table[tile_lanes(b)].T
    lane = lax.broadcasted_iota(jnp.int32, table.shape, 1)
    rest = jnp.where(lane < 2 * SUBL, pltpu.roll(table, LANES - HEAD_LANE, 1), 0.0)
    bias = pltpu.roll(table, LANES - HEAD_BIAS_LANE + 2 * SUBL, 1)
    main = head[:, :LANES]
    norm_b = jnp.sum(jnp.where(lane == 2 * SUBL, bias * bias, 0.0))
    norm_w = jnp.sum(main * main) + jnp.sum(rest * rest)
    head[:, LANES:] = jnp.where(lane == 2 * SUBL, bias, rest)
    conv = jnp.sum(jnp.where(lane < TAPS, table * table, 0.0))
    conv_b = jnp.sum(jnp.where(lane == BIAS_LANE, table * table, 0.0))
    n_lane = lax.broadcasted_iota(jnp.int32, (SUBL, LANES), 1)
    norms = jnp.zeros((SUBL, LANES), jnp.float32)
    for k, v in enumerate((conv, conv_b, norm_w, norm_b)):
        norms = jnp.where(n_lane == k, v, norms)
    norms_out[...] = norms
    lane = lax.broadcasted_iota(jnp.int32, (n, 2 * LANES), 1)
    edge = LANES + 2 * SUBL
    mine = jnp.where(lane < edge, ci[...], jnp.where(lane == edge, 1.0, 0.0))
    last = (((1,), (1,)), ((), ()))
    first = (((0,), (0,)), ((), ()))
    plain = (((1,), (0,)), ((), ()))

    def dot(a, b, dims):
        return lax.dot_general(
            a, b, dims, precision=highest, preferred_element_type=jnp.float32
        )

    class_out[...] = dot(mine, head[:channels, :], last)
    lane = lax.broadcasted_iota(jnp.int32, (n, 3 * LANES), 1)
    my_cot = jnp.where(lane < channels, cc[...], 0.0)
    class_grad[...] = dot(my_cot, head[...], plain)[:, : class_grad.shape[1]]
    pick = pick_rows(channels, per_dev, me[0], cots.shape[1])
    picked = dot(cots[...], pick, plain)
    grad_out[...] = dot(picked, classes[...], first)[:rows]


def pick_rows(channels, per_dev, me, padded):
    shape = (padded, LANES)
    channel = lax.broadcasted_iota(jnp.int32, shape, 0) - me * per_dev
    column = lax.broadcasted_iota(jnp.int32, shape, 1)
    return jnp.where((channel == column) & (column < per_dev), 1.0, 0.0)


def update_kernel(channels, per_dev, me, sums, table, norms, cw, cb, fw, fb, sw, sb, aw, ab, hw, hu, ha, hb, hub, hab,
                  fw_out, sw_out, w_out, a_out, hw_out, ha_out, fb_out, sb_out, b_out, ab_out, hb_out, hab_out, ratio_out):
    padded = sums.shape[1]
    real = lax.broadcasted_iota(jnp.int32, (1, padded), 1) < channels
    wide = moments(
        table[0:TAPS], sums[0:TAPS], table[16 : 16 + TAPS], table[32 : 32 + TAPS], 0.05
    )[2]
    wide_b = moments(table[48:49], sums[TAPS : TAPS + 1], table[56:57], table[64:65], 0.0)[2]
    lane = lax.broadcasted_iota(jnp.int32, (1, LANES), 1)
    update_sq = sums[TAPS + 1 : TAPS + 2, :LANES]
    update_sq = pltpu.roll(update_sq, 2, 1)
    update_sq = jnp.where(lane == 0, jnp.sum(jnp.where(real, wide * wide, 0.0)), update_sq)
    update_sq = jnp.where(lane == 1, jnp.sum(jnp.where(real, wide_b * wide_b, 0.0)), update_sq)
    ratios = jnp.sqrt(norms[0:1, :]) / jnp.sqrt(update_sq)
    rates = [
        learn_rate * jnp.sum(jnp.where(lane == k, ratios, 0.0), axis=1, keepdims=True)
        for k in range(4)
    ]
    mine = lax.dot_general(
        sums[...],
        pick_rows(channels, per_dev, me[0], padded),
        (((1,), (0,)), ((), ())),
        precision=highest,
        preferred_element_type=jnp.float32,
    )
    first, second, update = moments(cw[...], mine[0:TAPS, :per_dev], fw[...], sw[...], 0.05)
    fw_out[...] = first
    sw_out[...] = second
    w_new = cw[...] - rates[0] * update
    w_out[...] = w_new
    a_out[...] = keep_rate * aw[...] + (1.0 - keep_rate) * w_new
    first, second, update = moments(
        cb[...], mine[TAPS : TAPS + 1, :per_dev], fb[...], sb[...], 0.0
    )
    w_new = cb[...] - rates[1] * update
    fb_out[...] = first.reshape(per_dev)
    sb_out[...] = second.reshape(per_dev)
    b_out[...] = w_new.reshape(per_dev)
    ab_out[...] = (keep_rate * ab[...] + (1.0 - keep_rate) * w_new).reshape(per_dev)
    w_new = hb[...] - rates[3] * hub[...]
    hb_out[...] = w_new.reshape(per_dev)
    hab_out[...] = (keep_rate * hab[...] + (1.0 - keep_rate) * w_new).reshape(per_dev)
    ratio_out[...] = ratios[:, :4].reshape(4)
    w_new = hw[...] - rates[2] * hu[...]
    hw_out[...] = w_new
    ha_out[...] = keep_rate * ha[...] + (1.0 - keep_rate) * w_new


class Row:
    def __init__(self, ref):
        self.ref = ref

    def __getitem__(self, place):
        return self.ref[0, place]


def call(kernel, tables, operands, in_specs, outs, out_specs, scratch, steps, fills=False, tight=False):
    moved = sum(4 * int(np.prod(a.shape)) for a in operands) + sum(
        4 * int(np.prod(o.shape)) for o in outs
    )
    if tables[0].ndim == 2:
        by_place, kernel = kernel, lambda tab, *refs: by_place(Row(tab), *refs)
    limit = 60
    if tight:
        blocks = [s.block_shape for s in [*in_specs, *out_specs] if s.block_shape]
        need = 8 * sum(int(np.prod(b)) for b in blocks)
        need += 4 * sum(int(np.prod(v.shape)) for v in scratch)
        limit = min(limit, max(24, need * 5 // 2**22 + 4))
    return pl.pallas_call(
        kernel,
        grid_spec=pltpu.PrefetchScalarGridSpec(
            num_scalar_prefetch=len(tables),
            grid=(steps,),
            in_specs=in_specs,
            out_specs=out_specs,
            scratch_shapes=scratch,
        ),
        out_shape=outs,
        compiler_params=pltpu.CompilerParams(
            dimension_semantics=("arbitrary",), vmem_limit_bytes=limit * 1024 * 1024
        ),
        cost_estimate=pl.CostEstimate(
            flops=1, bytes_accessed=moved if fills else 1, transcendentals=0
        ),
    )(*tables, *operands)


def whole(*shape):
    return pl.BlockSpec(shape, lambda g, *tab: (0,) * len(shape))


def round_up(n, m):
    return -(-n // m) * m


def f32(*shape):
    return jax.ShapeDtypeStruct(shape, jnp.float32)


def swap(x, axis, bit):
    size = lax.axis_size(axis)
    return lax.ppermute(x, axis, [(k, k ^ bit) for k in range(size)])


def bits_of(axis):
    size = lax.axis_size(axis)
    assert size & (size - 1) == 0
    bits, b = [], 1
    while b < size:
        bits.append(b)
        b *= 2
    return bits


def sum_over(x, axis):
    for bit in reversed(bits_of(axis)):
        x = x + swap(x, axis, bit)
    return x


def tied(one, many):
    one, many = lax.optimization_barrier((one, list(many)))
    return one, many


def moments(weight, grad, first, second, decay):
    first_new = beta_one * first + (1.0 - beta_one) * grad
    second_new = beta_two * second + (1.0 - beta_two) * grad * grad
    update = (
        first_new / fix_first / (jnp.sqrt(second_new / fix_second) + small_eps) + decay * weight
    )
    return (first_new, second_new, update)


def per_device(
    patches,
    class_in,
    conv_weight,
    conv_bias,
    head_weight,
    head_bias,
    first_conv_w,
    first_conv_b,
    first_head_w,
    first_head_b,
    second_conv_w,
    second_conv_b,
    second_head_w,
    second_head_b,
    average_conv_w,
    average_conv_b,
    average_head_w,
    average_head_b,
    pooled_cot,
    class_cot,
):
    groups = lax.axis_size(CHAN)
    me = lax.axis_index(CHAN)
    my_id = me.astype(jnp.int32)[None]
    per_dev = conv_weight.shape[0]
    n_in, channels_in = patches.shape[1:]
    n_out, channels = pooled_cot.shape[1:]
    local_images = class_in.shape[1]
    images = local_images * groups
    plan = make_plan(groups, images, n_in, n_out)
    tiles, in_tiles = plan.out_tiles, plan.in_tiles
    width = plan.table.shape[1]
    per = 3
    steps = channels_in // (UNIT * per)
    x = patches[0].T
    cot = pooled_cot[0].T
    in_lanes, out_lanes = round_up(n_in, LANES), round_up(n_out, LANES)
    rows, wide_rows = UNIT * per, 2 * UNIT * per
    x_spec = pl.BlockSpec((rows, in_lanes), lambda g, tab: (g, 0))
    cot_spec = pl.BlockSpec((wide_rows, out_lanes), lambda g, tab: (g, 0))
    planes = [2 * op.full + op.half for op in plan.ops]
    halo_specs = [pl.BlockSpec((n, rows, LANES), lambda g, tab: (0, g, 0)) for n in planes]
    halo_outs = [f32(n, channels_in, LANES) for n in planes]
    planes = [2 * op.full + op.half for op in plan.back_ops]
    back_specs = [pl.BlockSpec((n, rows, LANES), lambda g, tab: (0, g, 0)) for n in planes]
    back_outs = [f32(n, channels_in, LANES) for n in planes]
    held_spec = pl.BlockSpec((in_tiles + 1, rows, LANES), lambda g, tab: (0, g, 0))
    split_spec = pl.BlockSpec((tiles, 2, rows, LANES), lambda g, tab: (0, 0, g, 0))
    own_spec = pl.BlockSpec((tiles, wide_rows, LANES), lambda g, tab: (0, g, 0))
    w_spec = pl.BlockSpec((wide_rows, LANES), lambda g, tab: (g, 0))
    anywhere = pl.BlockSpec(memory_space=pl.ANY)
    cot_held = pltpu.VMEM((tiles + 1, 2 * UNIT, LANES), jnp.float32)

    pd_rows = round_up(per_dev, SUBL)
    small_rows = 2 * pd_rows + 4 * local_images
    pieces = [
        conv_weight.T,
        conv_bias[None],
        first_conv_w.T,
        first_conv_b[None],
        second_conv_w.T,
        second_conv_b[None],
        head_bias[None],
        head_weight.T,
        class_in[0],
        class_cot[0],
    ]
    own_specs = [
        *(whole(*p.shape) for p in pieces[:7]),
        whole(pd_rows, 2 * LANES),
        whole(local_images, 2 * LANES),
        whole(local_images, 3 * LANES),
    ]
    small, table = call(
        functools.partial(small_kernel, per_dev),
        [my_id],
        [*pieces, jnp.asarray(plan.table)[:, None]],
        [*own_specs, pl.BlockSpec((None, 1, width), lambda g, tab: (tab[0], 0, 0))],
        [f32(small_rows, LANES), jax.ShapeDtypeStruct((1, width), jnp.int32)],
        [whole(small_rows, LANES), whole(1, width)],
        [pltpu.VMEM((LANES, LANES), jnp.float32)],
        1,
    )

    sends = call(
        functools.partial(pack_kernel, plan),
        [table],
        [cot, small],
        [cot_spec, anywhere],
        halo_outs,
        halo_specs,
        [cot_held],
        steps,
    )
    cot_split = call(
        functools.partial(align_cot_kernel, plan),
        [table],
        [cot, sends[0]],
        [cot_spec, anywhere],
        [f32(tiles, 2, channels_in, LANES)],
        [split_spec],
        [cot_held],
        steps,
    )[0]
    x_held = call(
        functools.partial(align_patches_kernel, plan),
        [table],
        [x, cot_split],
        [x_spec, anywhere],
        [f32(in_tiles + 1, channels_in, LANES)],
        [held_spec],
        [],
        steps,
    )[0]

    sends = list(sends)
    cot_halo = [None] * len(sends)
    parts = small[None]
    rounds = bits_of(CHAN)
    rounds = rounds[:1] + rounds[:0:-1]
    for bit in rounds:
        got = swap(parts, CHAN, bit)
        if bit == 1:
            got, sends = tied(got, sends)
        elif bit == rounds[-1]:
            got, (x_held,) = tied(got, [x_held])
        elif bit == rounds[1]:
            got, (cot_split,) = tied(got, [cot_split])
        parts = jnp.concatenate([parts, got], axis=0)
        if bit == 1:
            parts, sends = tied(parts, sends)
            for n, op in enumerate(plan.ops):
                if op.near:
                    cot_halo[n] = lax.ppermute(sends[n], CHAN, op.pairs)
    parts, sends = tied(parts, sends)
    near = [n for n, op in enumerate(plan.ops) if op.near]
    if near:
        cot_halo[near[0]], sends = tied(cot_halo[near[0]], sends)
    for n, op in enumerate(plan.ops):
        if not op.near:
            cot_halo[n] = lax.ppermute(sends[n], CHAN, op.pairs)
    padded = round_up(channels, LANES)
    wide, turned, class_out, class_grad, grad_h, weight_norms = call(
        functools.partial(spread_kernel, groups, per_dev, rounds),
        [my_id],
        [parts, class_in[0], class_cot[0], x_held],
        [whole(*parts.shape), own_specs[8], own_specs[9], anywhere],
        [
            f32(channels, LANES),
            f32(LANES, padded),
            f32(local_images, channels),
            f32(local_images, channels_in),
            f32(pd_rows, 2 * LANES),
            f32(SUBL, LANES),
        ],
        [
            whole(channels, LANES),
            whole(LANES, padded),
            whole(local_images, channels),
            whole(local_images, channels_in),
            whole(pd_rows, 2 * LANES),
            whole(SUBL, LANES),
        ],
        [
            pltpu.VMEM((padded, LANES), jnp.float32),
            pltpu.VMEM((padded, 2 * LANES), jnp.float32),
            pltpu.VMEM((images, 3 * LANES), jnp.float32),
            pltpu.VMEM((images, 2 * LANES), jnp.float32),
        ],
        1,
    )

    partials = call(
        functools.partial(partial_kernel, plan),
        [table],
        [x_held, wide],
        [held_spec, w_spec],
        back_outs,
        back_specs,
        [pltpu.VMEM((plan.most + 1, 2, UNIT, LANES), jnp.float32)],
        steps,
        tight=True,
    )
    partials, late = list(partials), []
    pooled_halo = [None] * len(partials)
    for n, op in enumerate(plan.back_ops):
        if op.early:
            pooled_halo[n] = lax.ppermute(partials[n], CHAN, op.pairs)
        else:
            late.append(n)
    grad_h = sum_over(grad_h, "dp")
    head_t = head_weight.T
    head_first, head_second, head_update = moments(
        head_t, grad_h[:per_dev, :channels_in], first_head_w.T, second_head_w.T, 0.05
    )
    bias_first, bias_second, bias_update = moments(
        head_bias, grad_h[:per_dev, channels_in], first_head_b, second_head_b, 0.0
    )
    norms = [jnp.sum(head_update**2), jnp.sum(bias_update**2)]

    pooled_own = call(
        functools.partial(forward_kernel, plan),
        [table],
        [x_held, wide, head_update],
        [held_spec, w_spec, anywhere],
        [f32(tiles, channels, LANES)],
        [own_spec],
        [],
        steps,
        tight=True,
    )[0]

    waiting = [partials[n] for n in late]
    waiting, cot_halo, pooled_own, norms = lax.optimization_barrier(
        (waiting, cot_halo, pooled_own, norms)
    )
    for n, v in zip(late, waiting):
        pooled_halo[n] = lax.ppermute(v, CHAN, plan.back_ops[n].pairs)
    cots_held = pltpu.VMEM((tiles + plan.halo + 1, 2, UNIT, LANES), jnp.float32)
    sums = call(
        functools.partial(weights_kernel, plan),
        [table],
        [x_held, cot_split, *cot_halo],
        [held_spec, split_spec, *halo_specs],
        [f32(2 * SUBL, padded)],
        [whole(2 * SUBL, padded)],
        [cots_held, pltpu.VMEM((TAPS + 1, padded, LANES), jnp.float32)],
        steps,
        tight=True,
    )[0]
    x_grad = call(
        functools.partial(patches_kernel, plan),
        [table],
        [cot_split, wide, sums, *cot_halo],
        [split_spec, w_spec, anywhere, *halo_specs],
        [f32(channels_in, n_in)],
        [x_spec],
        [cots_held, pltpu.VMEM((in_tiles + 1, UNIT, LANES), jnp.float32)],
        steps,
        tight=True,
    )[0]
    sums = sum_over(sums, "dp")
    row = lax.broadcasted_iota(jnp.int32, sums.shape, 0)
    lane = lax.broadcasted_iota(jnp.int32, sums.shape, 1)
    for k, v in enumerate(norms):
        sums = jnp.where((row == TAPS + 1) & (lane == k), v, sums)
    pooled = call(
        functools.partial(finish_kernel, plan),
        [table],
        [pooled_own, *pooled_halo],
        [own_spec, *back_specs],
        [f32(channels, n_out)],
        [cot_spec],
        [cot_held, pltpu.VMEM((plan.back_halo + 1, 2 * UNIT, LANES), jnp.float32)],
        steps,
        tight=True,
    )[0]
    for bit in bits_of(CHAN)[::-1]:
        got = swap(sums, CHAN, bit)
        if bit == bits_of(CHAN)[-1]:
            got, (x_grad,) = tied(got, [x_grad])
        if bit == 1:
            got, (pooled,) = tied(got, [pooled])
        sums = sums + got
    conv_shapes = [f32(TAPS, per_dev)] * 4
    head_shapes = [f32(per_dev, channels_in)] * 2
    operands = [
        sums,
        turned,
        weight_norms,
        *pieces[:6],
        average_conv_w.T,
        average_conv_b[None],
        head_t,
        head_update,
        average_head_w.T,
        head_bias[None],
        bias_update[None],
        average_head_b[None],
    ]
    specs = [whole(*v.shape) for v in operands]
    out_shapes = [*conv_shapes, *head_shapes, *[f32(per_dev)] * 6, f32(4)]
    *new, trust = call(
        functools.partial(update_kernel, channels, per_dev),
        [my_id],
        operands,
        specs,
        out_shapes,
        [whole(*v.shape) for v in out_shapes],
        [],
        1,
    )

    conv_new, (head_new, head_average), bias_new = new[:4], new[4:6], new[6:]
    return (
        pooled.T[None],
        class_out[None],
        x_grad.T[None],
        class_grad[None],
        *(v.T for v in conv_new),
        *bias_new[:4],
        head_first.T,
        head_second.T,
        head_new.T,
        head_average.T,
        bias_first,
        bias_second,
        *bias_new[4:],
        trust,
    )


def solution(mesh):
    by_row, by_column = P("dp", CHAN, None), P(None, CHAN)
    by_channel, by_name = P(CHAN, None), P(CHAN)
    return jax.shard_map(
        per_device,
        mesh=mesh,
        in_specs=(
            by_row,
            by_row,
            by_channel,
            by_name,
            by_column,
            by_name,
            by_channel,
            by_name,
            by_column,
            by_name,
            by_channel,
            by_name,
            by_column,
            by_name,
            by_channel,
            by_name,
            by_column,
            by_name,
            by_row,
            by_row,
        ),
        out_specs=(
            by_row,
            by_row,
            by_row,
            by_row,
            by_channel,
            by_channel,
            by_channel,
            by_channel,
            by_name,
            by_name,
            by_name,
            by_name,
            by_column,
            by_column,
            by_column,
            by_column,
            by_name,
            by_name,
            by_name,
            by_name,
            P(),
        ),
        check_vma=False,
    )
```

```python
import functools
import types

import jax
import jax.numpy as jnp
import numpy as np
from jax import lax
from jax.experimental import pallas as pl
from jax.experimental.pallas import tpu as pltpu
from jax.sharding import PartitionSpec as P

GRID = 27
TAPS = 9
OUTG = 14
LANES = 128
SUBL = 8
CHAN = "chan"
UNIT = 16

beta_one = 0.9
beta_two = 0.999
fix_first = 1.0 - 0.9**10
fix_second = 1.0 - 0.999**10
small_eps = 1e-06
learn_rate = 0.5
keep_rate = 0.9
highest = lax.Precision.HIGHEST


def sized(parts):
    full = max(len(f) for _, (f, _) in parts)
    half = max(len(h) for _, (_, h) in parts)
    return types.SimpleNamespace(
        full=full,
        half=half,
        size=full + half,
        parts=parts,
        pairs=[pair for pair, _ in parts],
        tiles=[
            [(j, *v) for j, v in enumerate(f)] + [(full + j, *v) for j, v in enumerate(h)]
            for _, (f, h) in parts
        ],
        near=all(src ^ dst == 1 for (src, dst), _ in parts),
    )


def halves(message):
    return 2 * len(message[0]) + len(message[1])


def free_in(parts, pair):
    return all(pair[0] != s and pair[1] != d for (s, d), _ in parts)


def grouped(messages, spare):
    groups = []
    for pair, message in sorted(messages, key=lambda kv: (-halves(kv[1]), kv[0])):
        for parts in groups:
            first = parts[0][1]
            if (
                len(message[0]) <= len(first[0])
                and len(message[1]) <= len(first[1])
                and halves(first) - halves(message) <= 2 * spare
                and free_in(parts, pair)
            ):
                break
        else:
            parts = []
            groups.append(parts)
        parts.append((pair, message))
    return [sized(parts) for parts in groups]


def loads(ops, groups):
    got = np.zeros(groups, np.int64)
    for op in ops:
        for _, dst in op.pairs:
            got[dst] += 2 * op.full + op.half
    return got


def joined(ops, others, groups):
    for n in range(1, len(ops)):
        for m in range(n):
            if not (ops[n].near and ops[m].near):
                continue
            for pair, message in list(ops[n].parts):
                got = loads(ops + others, groups)
                more = halves(ops[m].parts[0][1]) - 2 * ops[n].full - ops[n].half
                if (
                    len(ops[n].parts) > 1
                    and free_in(ops[m].parts, pair)
                    and got[pair[1]] + more < 0.9 * max(got)
                ):
                    ops[n] = sized([v for v in ops[n].parts if v[0] != pair])
                    ops[m] = sized(ops[m].parts + [(pair, message)])
    return ops


def make_plan(groups, images, n_in, n_out):
    tiles_img = images // LANES
    n_tiles = OUTG * OUTG * tiles_img
    tap_tile = np.full((n_tiles, TAPS), -1, np.int64)
    for i in range(OUTG):
        for j in range(OUTG):
            for it in range(tiles_img):
                for a in range(3):
                    for e in range(3):
                        r, s = 2 * i + a - 1, 2 * j + e - 1
                        if 0 <= r < GRID and 0 <= s < GRID:
                            tap_tile[(i * OUTG + j) * tiles_img + it, 3 * a + e] = (
                                r * GRID + s
                            ) * tiles_img + it
    step = int(np.gcd(np.gcd(n_in, n_out), LANES))
    wanted = {}
    for lane in range(0, LANES, step):
        p_owner = (np.arange(n_tiles) * LANES + lane) // n_out
        t_owner = (tap_tile * LANES + lane) // n_in
        for p in range(n_tiles):
            k = int(p_owner[p])
            for t in range(TAPS):
                if tap_tile[p, t] >= 0 and t_owner[p, t] != k:
                    lanes = wanted.setdefault((k, int(t_owner[p, t])), {}).setdefault(p, set())
                    lanes.update((lane, lane + step - 1))
    middle = LANES // 2
    for pair, tiles in wanted.items():
        full, half = [], []
        for p, lanes in sorted(tiles.items()):
            low, high = max(lanes) < middle, min(lanes) >= middle
            (half if low or high else full).append((p, int(high)))
        wanted[pair] = (full, half)
    near = {p: t for p, t in wanted.items() if p[0] ^ p[1] == 1}
    weight = {p: 2 * len(t[0]) + len(t[1]) for p, t in near.items()}
    even = max([min(w, weight.get(p[::-1], 0)) for p, w in weight.items()], default=0)
    begin, rest = [], []
    for p, (full, half) in near.items():
        some = max(even - len(half), 0) // 2
        begin.append((p, (full[:some], half)))
        if full[some:]:
            rest.append((p, (full[some:], [])))
    ops = grouped(begin, even) + grouped(rest, 2)
    ops += grouped([(p, t) for p, t in wanted.items() if p[0] ^ p[1] != 1], 2)
    back_ops = grouped([((d, s), t) for (s, d), t in wanted.items()], 2)
    back_ops = joined(back_ops, ops, groups)
    longest = max(op.size for op in back_ops)
    for op in back_ops:
        op.early = op.near and 4 * op.size > 3 * longest
    in_base = np.arange(groups) * n_in // LANES
    in_shift = np.arange(groups) * n_in % LANES
    out_base = np.arange(groups) * n_out // LANES
    out_shift = np.arange(groups) * n_out % LANES
    in_tiles = int(max(-(-(in_shift + n_in) // LANES)))
    out_tiles = int(max(-(-(out_shift + n_out) // LANES)))
    sizes = [op.size for op in ops]
    halo = sum(sizes)
    back_sizes = [op.size for op in back_ops]
    back_halo = sum(back_sizes)
    owned = [
        range(int(out_base[k]), int(out_base[k]) - (-(int(out_shift[k]) + n_out) // LANES))
        for k in range(groups)
    ]
    none = out_tiles + halo
    own_slot = np.full((groups, halo), out_tiles, np.int64)
    got = [[] for _ in range(groups)]
    upper = np.zeros((4, groups, max(halo, back_halo)), np.int64)
    start = 0
    for op in ops:
        for (src, dst), tiles in zip(op.pairs, op.tiles):
            for j, p, high in tiles:
                own_slot[src, start + j] = p - out_base[src]
                got[dst].append((p, start + j))
                upper[0, src, start + j] = upper[1, dst, start + j] = high
        start += op.size
    most = max(len(v) for v in got)

    def tap_rows(device, p):
        local = tap_tile[p] - in_base[device]
        first, last = device * n_in, (device + 1) * n_in
        held = (
            (tap_tile[p] >= 0)
            & (tap_tile[p] * LANES < last)
            & ((tap_tile[p] + 1) * LANES > first)
        )
        return np.where(held, local, in_tiles)

    own_taps = np.full((groups, out_tiles, TAPS), in_tiles, np.int64)
    got_taps = np.full((groups, most, 1 + TAPS), in_tiles, np.int64)
    got_taps[:, :, 0] = none
    from_got = np.full((groups, back_halo), most, np.int64)
    adds = [[[] for _ in range(out_tiles)] for _ in range(groups)]
    merges, slot_of = [], []
    for k in range(groups):
        for j, p in enumerate(owned[k]):
            own_taps[k, j] = tap_rows(k, p)
        slot_of.append({p: j for j, p in enumerate(owned[k])})
        merges.append([])
        for n, (p, place) in enumerate(got[k]):
            got_taps[k, n, 0] = out_tiles + place
            got_taps[k, n, 1:] = tap_rows(k, p)
            if p in slot_of[k]:
                merges[k].append([slot_of[k][p], out_tiles + place])
            else:
                slot_of[k][p] = out_tiles + place
    start = 0
    for op in back_ops:
        for (src, dst), tiles in zip(op.pairs, op.tiles):
            names = [p for p, _ in got[src]]
            for j, p, high in tiles:
                from_got[src, start + j] = names.index(p)
                adds[dst][p - out_base[dst]].append(start + j)
                upper[2, src, start + j] = upper[3, dst, start + j] = high
        start += op.size
    n_merges = max(len(v) for v in merges)
    merges = np.array([v + [[none, none]] * (n_merges - len(v)) for v in merges], np.int64)
    n_adds = max(len(v) for per_dev in adds for v in per_dev)
    adds = np.array([[v + [back_halo] * (n_adds - len(v)) for v in per_dev] for per_dev in adds])
    kinds = [
        [(a, e) for a in ((1,), (0, 2))[row_odd] for e in ((1,), (0, 2))[col_odd]]
        for row_odd in range(2)
        for col_odd in range(2)
    ]
    lists = [[[] for _ in range(groups)] for _ in kinds]
    for k in range(groups):
        count = -(-(int(in_shift[k]) + n_in) // LANES)
        for t in range(count):
            position, it = divmod(int(in_base[k]) + t, tiles_img)
            r, s = divmod(position, GRID)
            kind = 2 * (r % 2) + s % 2
            entry = [t]
            for a, e in kinds[kind]:
                i, j = (r + 1 - a) // 2, (s + 1 - e) // 2
                entry.append(slot_of[k].get((i * OUTG + j) * tiles_img + it, none))
            lists[kind][k].append(entry)
    reach_tables, kind_sizes = [], []
    for kind, per_device_lists in enumerate(lists):
        width = 1 + len(kinds[kind])
        size = max(len(v) for v in per_device_lists)
        kind_sizes.append(size)
        filler = [in_tiles] + [none] * (width - 1)
        reach_tables.append(
            np.array([v + [filler] * (size - len(v)) for v in per_device_lists]).reshape(groups, -1)
        )
    parts = types.SimpleNamespace(
        shifts=np.stack([in_shift, out_shift], axis=1),
        own_slot=own_slot,
        own_taps=own_taps.reshape(groups, -1),
        got_taps=got_taps.reshape(groups, -1),
        from_got=from_got,
        merges=merges.reshape(groups, -1),
        adds=adds.reshape(groups, -1),
        upper=list(upper),
        kinds=reach_tables,
    )
    at, total, columns = types.SimpleNamespace(), 0, []
    for name, v in vars(parts).items():
        places = []
        for one in v if isinstance(v, list) else [v]:
            places.append(total)
            total += one.shape[1]
            columns.append(one)
        setattr(at, name, places if isinstance(v, list) else places[0])
    return types.SimpleNamespace(
        ops=ops,
        sizes=sizes,
        halo=halo,
        back_ops=back_ops,
        back_sizes=back_sizes,
        back_halo=back_halo,
        in_tiles=in_tiles,
        out_tiles=out_tiles,
        most=most,
        n_merges=n_merges,
        n_adds=n_adds,
        n_in=n_in,
        n_out=n_out,
        kinds=[[3 * a + e for a, e in kind] for kind in kinds],
        kind_sizes=kind_sizes,
        at=at,
        table=np.concatenate(columns, axis=1).astype(np.int32),
    )


def lane_ids():
    return lax.broadcasted_iota(jnp.int32, (UNIT, LANES), 1)


def align_into(load, store, n_local, tiles, shift):
    lane = lane_ids()
    zero = jnp.zeros((UNIT, LANES), jnp.float32)
    local_tiles = -(-n_local // LANES)
    before = zero
    for t in range(tiles):
        if t < local_tiles:
            now = load(t)
            if (t + 1) * LANES > n_local:
                now = jnp.where(lane < n_local - t * LANES, now, 0.0)
            now = pltpu.roll(now, shift, 1)
        else:
            now = zero
        store(t, jnp.where(lane < shift, before, now))
        before = now
    store(tiles, zero)


def unalign_from(load, store, n_local, tiles, shift):
    lane = lane_ids()
    local_tiles = -(-n_local // LANES)
    back = lax.rem(LANES - shift, LANES)
    now = pltpu.roll(load(0), back, 1)
    for t in range(local_tiles):
        later = pltpu.roll(load(t + 1), back, 1) if t + 1 < tiles else now
        store(t, jnp.where(lane < LANES - shift, now, later))
        now = later


def tile_lanes(t):
    return slice(t * LANES, (t + 1) * LANES)


def rows_at(unit, part=0, parts=1):
    return pl.ds(pl.multiple_of((unit * parts + part) * UNIT, UNIT), UNIT)


def both_at(unit):
    return pl.ds(pl.multiple_of(unit * 2 * UNIT, UNIT), 2 * UNIT)


def of_half(half, unit=0):
    return pl.ds(unit * 2 * UNIT + half, UNIT, stride=2)


def align_cot(cot_ref, unit, held, plan, shift):
    for part in range(2):
        align_into(
            lambda t: cot_ref[rows_at(unit, part, 2), tile_lanes(t)],
            lambda t, v: held.__setitem__((t, slice(part * UNIT, (part + 1) * UNIT)), v),
            plan.n_out,
            plan.out_tiles,
            shift,
        )


def tap_weights(w_ref, unit, half, lanes):
    rows = w_ref[of_half(half, unit), :]
    return [jnp.broadcast_to(rows[:, t : t + 1], (UNIT, LANES)) for t in lanes]


def in_turn(count, size, make, keep):
    for first in range(0, count, size):
        some = range(first, min(first + size, count))
        for j, v in [(j, make(j)) for j in some]:
            keep(j, v)


def over_units(ref, rows, body):
    lax.fori_loop(0, ref.shape[0] // rows, lambda u, c: (body(u), c)[1], 0)


def add_up(items):
    items = list(items)
    while len(items) > 1:
        items = [
            items[i] + items[i + 1] if i + 1 < len(items) else items[i]
            for i in range(0, len(items), 2)
        ]
    return items[0]


BIAS_LANE = 48
HEAD_BIAS_LANE = 72
HEAD_LANE = 96


def small_kernel(per_dev, me, cw, cb, fw, fb, sw, sb, hb, hw, ci, cc, row, out, row_out, square):
    row_out[...] = row[...]
    square[...] = jnp.zeros_like(square)
    for part, (w, b) in enumerate(((cw, cb), (fw, fb), (sw, sb))):
        square[2 * SUBL * part : 2 * SUBL * part + TAPS, :per_dev] = w[...]
        square[BIAS_LANE + SUBL * part : BIAS_LANE + SUBL * part + 1, :per_dev] = b[...]
    square[HEAD_BIAS_LANE : HEAD_BIAS_LANE + 1, :per_dev] = hb[...]
    turned = square[...].T
    rows = hw.shape[0]
    lane = lax.broadcasted_iota(jnp.int32, (rows, LANES), 1)
    rest = pltpu.roll(jnp.where(lane < 2 * SUBL, hw[:, LANES:], 0.0), HEAD_LANE, 1)
    out[0:rows] = jnp.where(lane < HEAD_LANE, turned[0:rows], rest)
    out[rows : 2 * rows] = hw[:, :LANES]
    at, n = 2 * rows, ci.shape[0]
    out[at : at + n] = ci[:, :LANES]
    out[at + n : at + 2 * n] = cc[:, :LANES]
    out[at + 2 * n : at + 3 * n] = cc[:, LANES : 2 * LANES]
    lane = lax.broadcasted_iota(jnp.int32, (n, LANES), 1)
    left = jnp.where(lane < 2 * SUBL, ci[:, LANES:], 0.0)
    right = pltpu.roll(jnp.where(lane < 4 * SUBL, cc[:, 2 * LANES :], 0.0), 4 * SUBL, 1)
    out[at + 3 * n : at + 4 * n] = jnp.where(lane < 4 * SUBL, left, right)


def align_patches_kernel(plan, tab, x_ref, after, x_out):
    def body(unit):
        align_into(
            lambda t: x_ref[rows_at(unit), tile_lanes(t)],
            lambda t, v: x_out.__setitem__((t, rows_at(unit)), v),
            plan.n_in,
            plan.in_tiles,
            tab[0],
        )

    over_units(x_ref, UNIT, body)


def align_cot_kernel(plan, tab, cot_ref, after, cot_out, held):
    def body(unit):
        align_cot(cot_ref, unit, held, plan, tab[1])
        for j in range(plan.out_tiles):
            for half in range(2):
                cot_out[j, half, rows_at(unit)] = held[j, of_half(half)]

    over_units(cot_ref, 2 * UNIT, body)


def pack_kernel(plan, tab, cot_ref, after, *refs):
    outs, held = refs[:-1], refs[-1]

    def body(unit):
        align_cot(cot_ref, unit, held, plan, tab[1])
        at = 0
        for op, out in zip(plan.ops, outs):
            send_tiles(
                op,
                lambda j, at=at: [
                    held[tab[plan.at.own_slot + at + j], of_half(half)] for half in range(2)
                ],
                lambda j, at=at: tab[plan.at.upper[0] + at + j],
                out,
                unit,
            )
            at += op.size

    over_units(cot_ref, 2 * UNIT, body)


def tap_sums(tab, at, held, weights):
    totals = [None, None]
    for t in range(TAPS):
        tile = held(tab[at + t])
        for half in range(2):
            term = tile * weights[half][t]
            totals[half] = term if t == 0 else totals[half] + term
    return totals


def keep_halves(ref, j, unit, values):
    for half, v in enumerate(values):
        ref[j, of_half(half, unit)] = v


def send_tiles(op, load, upper, out, unit):
    def store(j, pair):
        for half, v in enumerate(pair):
            out[2 * j + half, rows_at(unit)] = v

    in_turn(op.full, 6, load, store)
    low = lane_ids() < LANES // 2
    for j in range(op.full, op.size):
        even, odd = load(j)
        high = upper(j) > 0
        left = jnp.where(high, pltpu.roll(even, LANES // 2, 1), even)
        right = jnp.where(high, odd, pltpu.roll(odd, LANES // 2, 1))
        out[op.full + j, rows_at(unit)] = jnp.where(low, left, right)


def received_tiles(op, ref, upper, keep, unit):
    in_turn(
        op.full,
        5,
        lambda j: [ref[2 * j + half, rows_at(unit)] for half in range(2)],
        keep,
    )
    low = lane_ids() < LANES // 2
    for j in range(op.full, op.size):
        plane = ref[op.full + j, rows_at(unit)]
        turned = pltpu.roll(plane, LANES // 2, 1)
        high = upper(j) > 0
        even = jnp.where(high, jnp.where(low, 0.0, turned), jnp.where(low, plane, 0.0))
        odd = jnp.where(high, jnp.where(low, 0.0, plane), jnp.where(low, turned, 0.0))
        keep(j, [even, odd])


def partial_kernel(plan, tab, x_ref, w_ref, *refs):
    outs, done = refs[:-1], refs[-1]

    def body(unit):
        def held(slot):
            return x_ref[slot, rows_at(unit)]

        weights = [tap_weights(w_ref, unit, half, range(TAPS)) for half in range(2)]
        in_turn(
            plan.most,
            4,
            lambda n: tap_sums(tab, plan.at.got_taps + (1 + TAPS) * n + 1, held, weights),
            lambda n, totals: keep_split_all(done, n, totals),
        )
        done[plan.most] = jnp.zeros(done.shape[1:], jnp.float32)
        at = 0
        for op, out in zip(plan.back_ops, outs):
            send_tiles(
                op,
                lambda j, at=at: [
                    done[tab[plan.at.from_got + at + j], half] for half in range(2)
                ],
                lambda j, at=at: tab[plan.at.upper[2] + at + j],
                out,
                unit,
            )
            at += op.size

    over_units(w_ref, 2 * UNIT, body)


def forward_kernel(plan, tab, x_ref, w_ref, after, out):
    def body(unit):
        def held(slot):
            return x_ref[slot, rows_at(unit)]

        weights = [
            tap_weights(w_ref, unit, half, [*range(TAPS), BIAS_LANE]) for half in range(2)
        ]
        in_turn(
            plan.out_tiles,
            4,
            lambda j: tap_sums(tab, plan.at.own_taps + TAPS * j, held, weights),
            lambda j, totals: keep_halves(
                out, j, unit, [totals[half] + weights[half][TAPS] for half in range(2)]
            ),
        )

    over_units(w_ref, 2 * UNIT, body)


def take_cots(plan, tab, unit, cot_ref, halos, cots):
    own = plan.out_tiles
    in_turn(
        own,
        5,
        lambda j: [cot_ref[j, half, rows_at(unit)] for half in range(2)],
        lambda j, v: keep_split_all(cots, j, v),
    )
    at = 0
    for op, ref in zip(plan.ops, halos):
        received_tiles(
            op,
            ref,
            lambda j, at=at: tab[plan.at.upper[1] + at + j],
            lambda j, v, at=at: keep_split_all(cots, own + at + j, v),
            unit,
        )
        at += op.size
    cots[own + at] = jnp.zeros(cots.shape[1:], jnp.float32)


def keep_split_all(ref, j, values):
    for half, v in enumerate(values):
        ref[j, half] = v


def merge_cots(plan, tab, cots):
    for n in range(plan.n_merges):
        at = plan.at.merges + 2 * n
        for half in range(2):
            cots[tab[at], half] = cots[tab[at], half] + cots[tab[at + 1], half]


def weights_kernel(plan, tab, x_ref, cot_ref, *refs):
    halos = refs[: len(plan.sizes)]
    sums_ref, cots, rows = refs[len(plan.sizes) :]
    step = pl.program_id(0)
    per = x_ref.shape[1] // UNIT
    zero = jnp.zeros((UNIT, LANES), jnp.float32)

    @pl.when(step == 0)
    def _():
        rows[...] = jnp.zeros_like(rows)

    def body(unit):
        take_cots(plan, tab, unit, cot_ref, halos, cots)
        here = step * per + unit
        for half in range(2):
            bias = cots[0, half]
            for j in range(1, plan.out_tiles):
                bias = bias + cots[j, half]
            rows[TAPS, of_half(half, here), :] = bias
        merge_cots(plan, tab, cots)
        for q, (kind, size) in enumerate(zip(plan.kinds, plan.kind_sizes)):
            width = 1 + len(kind)
            total = [[zero] * len(kind) for _ in range(2)]
            for j in range(size):
                at = plan.at.kinds[q] + width * j
                tile = x_ref[tab[at], rows_at(unit)]
                for n in range(len(kind)):
                    slot = tab[at + 1 + n]
                    for half in range(2):
                        total[half][n] = total[half][n] + cots[slot, half] * tile
            for n, t in enumerate(kind):
                for half in range(2):
                    rows[t, of_half(half, here), :] = total[half][n]

    lax.fori_loop(0, per, lambda u, c: (body(u), c)[1], 0)

    @pl.when(step == pl.num_programs(0) - 1)
    def _():
        lane = lax.broadcasted_iota(jnp.int32, (LANES, LANES), 1)

        def block(b, carry):
            here = pl.ds(pl.multiple_of(b * LANES, LANES), LANES)
            total = jnp.zeros((LANES, LANES), jnp.float32)
            for t in range(TAPS + 1):
                one = jnp.sum(rows[t, here, :], axis=1, keepdims=True)
                total = jnp.where(lane == t, one, total)
            sums_ref[:, here] = total.T[: 2 * SUBL]
            return carry

        lax.fori_loop(0, rows.shape[1] // LANES, block, 0)


def patches_kernel(plan, tab, cot_ref, w_ref, after, *refs):
    halos = refs[: len(plan.sizes)]
    grad_ref, cots, back = refs[len(plan.sizes) :]

    def body(unit):
        take_cots(plan, tab, unit, cot_ref, halos, cots)
        merge_cots(plan, tab, cots)
        for q, (kind, size) in enumerate(zip(plan.kinds, plan.kind_sizes)):
            weights = [tap_weights(w_ref, unit, half, kind) for half in range(2)]
            width = 1 + len(kind)

            def one(j, q=q, kind=kind, weights=weights, width=width):
                at = plan.at.kinds[q] + width * j
                items = []
                for n in range(len(kind)):
                    slot = tab[at + 1 + n]
                    items += [cots[slot, half] * weights[half][n] for half in range(2)]
                return at, add_up(items)

            in_turn(size, 4, one, lambda j, v: back.__setitem__(tab[v[0]], v[1]))
        unalign_from(
            lambda t: back[t],
            lambda t, v: grad_ref.__setitem__((rows_at(unit), tile_lanes(t)), v),
            plan.n_in,
            plan.in_tiles,
            tab[0],
        )

    over_units(w_ref, 2 * UNIT, body)


def finish_kernel(plan, tab, own_ref, *refs):
    n_ops = len(plan.back_sizes)
    halos = refs[:n_ops]
    out_ref, held, got = refs[n_ops:]
    tiles = plan.out_tiles

    def body(unit):
        at = 0
        for op, halo in zip(plan.back_ops, halos):
            received_tiles(
                op,
                halo,
                lambda j, at=at: tab[plan.at.upper[3] + at + j],
                lambda j, v, at=at: keep_halves(got, at + j, 0, v),
                unit,
            )
            at += op.size
        got[at] = jnp.zeros(got.shape[1:], jnp.float32)

        def whole_sum(j):
            total = own_ref[j, both_at(unit)]
            for n in range(plan.n_adds):
                total = total + got[tab[plan.at.adds + plan.n_adds * j + n]]
            return total

        in_turn(tiles, 5, whole_sum, held.__setitem__)
        for part in range(2):
            unalign_from(
                lambda t: held[t, part * UNIT : (part + 1) * UNIT],
                lambda t, v: out_ref.__setitem__((rows_at(unit, part, 2), tile_lanes(t)), v),
                plan.n_out,
                tiles,
                tab[1],
            )

    over_units(out_ref, 2 * UNIT, body)


def spread_kernel(groups, per_dev, rounds, me, parts, ci, cc, after, wide_out, turned_out, class_out, class_grad, grad_out, norms_out, wide, head, cots, classes):
    rows = round_up(per_dev, SUBL)
    n = ci.shape[0]
    channels = groups * per_dev
    wide[...] = jnp.zeros_like(wide)
    head[...] = jnp.zeros_like(head)
    lane = lax.broadcasted_iota(jnp.int32, (n, LANES), 1)
    at = 2 * rows
    for dev in range(groups):
        apart = jnp.bitwise_xor(me[0], dev)
        part = 0
        for place, bit in enumerate(rounds):
            part = part + jnp.bitwise_and(lax.div(apart, bit), 1) * 2**place
        wide[dev * per_dev : (dev + 1) * per_dev, :] = parts[part, :per_dev]
        head[dev * per_dev : (dev + 1) * per_dev, :LANES] = parts[part, rows : rows + per_dev]
        here = slice(dev * n, (dev + 1) * n)
        classes[here, :LANES] = parts[part, at : at + n]
        cots[here, :LANES] = parts[part, at + n : at + 2 * n]
        cots[here, LANES : 2 * LANES] = parts[part, at + 2 * n : at + 3 * n]
        rest = parts[part, at + 3 * n : at + 4 * n]
        ones = jnp.where(lane == 2 * SUBL, 1.0, 0.0)
        classes[here, LANES:] = jnp.where(lane < 2 * SUBL, rest, ones)
        rest = pltpu.roll(rest, LANES - 4 * SUBL, 1)
        cots[here, 2 * LANES :] = jnp.where(lane < 4 * SUBL, rest, 0.0)
    table = wide[...]
    wide_out[...] = table[:channels]
    for b in range(table.shape[0] // LANES):
        turned_out[:, tile_lanes(b)] = table[tile_lanes(b)].T
    lane = lax.broadcasted_iota(jnp.int32, table.shape, 1)
    rest = jnp.where(lane < 2 * SUBL, pltpu.roll(table, LANES - HEAD_LANE, 1), 0.0)
    bias = pltpu.roll(table, LANES - HEAD_BIAS_LANE + 2 * SUBL, 1)
    main = head[:, :LANES]
    norm_b = jnp.sum(jnp.where(lane == 2 * SUBL, bias * bias, 0.0))
    norm_w = jnp.sum(main * main) + jnp.sum(rest * rest)
    head[:, LANES:] = jnp.where(lane == 2 * SUBL, bias, rest)
    conv = jnp.sum(jnp.where(lane < TAPS, table * table, 0.0))
    conv_b = jnp.sum(jnp.where(lane == BIAS_LANE, table * table, 0.0))
    n_lane = lax.broadcasted_iota(jnp.int32, (SUBL, LANES), 1)
    norms = jnp.zeros((SUBL, LANES), jnp.float32)
    for k, v in enumerate((conv, conv_b, norm_w, norm_b)):
        norms = jnp.where(n_lane == k, v, norms)
    norms_out[...] = norms
    lane = lax.broadcasted_iota(jnp.int32, (n, 2 * LANES), 1)
    edge = LANES + 2 * SUBL
    mine = jnp.where(lane < edge, ci[...], jnp.where(lane == edge, 1.0, 0.0))
    last = (((1,), (1,)), ((), ()))
    first = (((0,), (0,)), ((), ()))
    plain = (((1,), (0,)), ((), ()))

    def dot(a, b, dims):
        return lax.dot_general(
            a, b, dims, precision=highest, preferred_element_type=jnp.float32
        )

    class_out[...] = dot(mine, head[:channels, :], last)
    lane = lax.broadcasted_iota(jnp.int32, (n, 3 * LANES), 1)
    my_cot = jnp.where(lane < channels, cc[...], 0.0)
    class_grad[...] = dot(my_cot, head[...], plain)[:, : class_grad.shape[1]]
    pick = pick_rows(channels, per_dev, me[0], cots.shape[1])
    picked = dot(cots[...], pick, plain)
    grad_out[...] = dot(picked, classes[...], first)[:rows]


def pick_rows(channels, per_dev, me, padded):
    shape = (padded, LANES)
    channel = lax.broadcasted_iota(jnp.int32, shape, 0) - me * per_dev
    column = lax.broadcasted_iota(jnp.int32, shape, 1)
    return jnp.where((channel == column) & (column < per_dev), 1.0, 0.0)


def update_kernel(channels, per_dev, me, sums, table, norms, cw, cb, fw, fb, sw, sb, aw, ab, hw, hu, ha, hb, hub, hab,
                  fw_out, sw_out, w_out, a_out, hw_out, ha_out, fb_out, sb_out, b_out, ab_out, hb_out, hab_out, ratio_out):
    padded = sums.shape[1]
    real = lax.broadcasted_iota(jnp.int32, (1, padded), 1) < channels
    wide = moments(
        table[0:TAPS], sums[0:TAPS], table[16 : 16 + TAPS], table[32 : 32 + TAPS], 0.05
    )[2]
    wide_b = moments(table[48:49], sums[TAPS : TAPS + 1], table[56:57], table[64:65], 0.0)[2]
    lane = lax.broadcasted_iota(jnp.int32, (1, LANES), 1)
    update_sq = sums[TAPS + 1 : TAPS + 2, :LANES]
    update_sq = pltpu.roll(update_sq, 2, 1)
    update_sq = jnp.where(lane == 0, jnp.sum(jnp.where(real, wide * wide, 0.0)), update_sq)
    update_sq = jnp.where(lane == 1, jnp.sum(jnp.where(real, wide_b * wide_b, 0.0)), update_sq)
    ratios = jnp.sqrt(norms[0:1, :]) / jnp.sqrt(update_sq)
    rates = [
        learn_rate * jnp.sum(jnp.where(lane == k, ratios, 0.0), axis=1, keepdims=True)
        for k in range(4)
    ]
    mine = lax.dot_general(
        sums[...],
        pick_rows(channels, per_dev, me[0], padded),
        (((1,), (0,)), ((), ())),
        precision=highest,
        preferred_element_type=jnp.float32,
    )
    first, second, update = moments(cw[...], mine[0:TAPS, :per_dev], fw[...], sw[...], 0.05)
    fw_out[...] = first
    sw_out[...] = second
    w_new = cw[...] - rates[0] * update
    w_out[...] = w_new
    a_out[...] = keep_rate * aw[...] + (1.0 - keep_rate) * w_new
    first, second, update = moments(
        cb[...], mine[TAPS : TAPS + 1, :per_dev], fb[...], sb[...], 0.0
    )
    w_new = cb[...] - rates[1] * update
    fb_out[...] = first.reshape(per_dev)
    sb_out[...] = second.reshape(per_dev)
    b_out[...] = w_new.reshape(per_dev)
    ab_out[...] = (keep_rate * ab[...] + (1.0 - keep_rate) * w_new).reshape(per_dev)
    w_new = hb[...] - rates[3] * hub[...]
    hb_out[...] = w_new.reshape(per_dev)
    hab_out[...] = (keep_rate * hab[...] + (1.0 - keep_rate) * w_new).reshape(per_dev)
    ratio_out[...] = ratios[:, :4].reshape(4)
    w_new = hw[...] - rates[2] * hu[...]
    hw_out[...] = w_new
    ha_out[...] = keep_rate * ha[...] + (1.0 - keep_rate) * w_new


def last_kernel(plan, channels, per_dev, count, tab, me, own_ref, *refs):
    n_ops = len(plan.back_sizes)
    halos, refs = refs[:n_ops], refs[n_ops:]
    small, refs = refs[:count], refs[count:]
    out_ref, new, scratch = refs[0], refs[1:-2], refs[-2:]

    @pl.when(pl.program_id(0) == 0)
    def _():
        update_kernel(channels, per_dev, me, *small, *new)

    finish_kernel(plan, tab, own_ref, *halos, out_ref, *scratch)


class Row:
    def __init__(self, ref):
        self.ref = ref

    def __getitem__(self, place):
        return self.ref[0, place]


def call(kernel, tables, operands, in_specs, outs, out_specs, scratch, steps, fills=False, tight=False):
    moved = sum(4 * int(np.prod(a.shape)) for a in operands) + sum(
        4 * int(np.prod(o.shape)) for o in outs
    )
    if tables[0].ndim == 2:
        by_place, kernel = kernel, lambda tab, *refs: by_place(Row(tab), *refs)
    limit = 60
    if tight:
        blocks = [s.block_shape for s in [*in_specs, *out_specs] if s.block_shape]
        need = 8 * sum(int(np.prod(b)) for b in blocks)
        need += 4 * sum(int(np.prod(v.shape)) for v in scratch)
        limit = min(limit, max(24, need * 5 // 2**22 + 4))
    return pl.pallas_call(
        kernel,
        grid_spec=pltpu.PrefetchScalarGridSpec(
            num_scalar_prefetch=len(tables),
            grid=(steps,),
            in_specs=in_specs,
            out_specs=out_specs,
            scratch_shapes=scratch,
        ),
        out_shape=outs,
        compiler_params=pltpu.CompilerParams(
            dimension_semantics=("arbitrary",), vmem_limit_bytes=limit * 1024 * 1024
        ),
        cost_estimate=pl.CostEstimate(
            flops=1, bytes_accessed=moved if fills else 1, transcendentals=0
        ),
    )(*tables, *operands)


def whole(*shape):
    return pl.BlockSpec(shape, lambda g, *tab: (0,) * len(shape))


def round_up(n, m):
    return -(-n // m) * m


def f32(*shape):
    return jax.ShapeDtypeStruct(shape, jnp.float32)


def swap(x, axis, bit):
    size = lax.axis_size(axis)
    return lax.ppermute(x, axis, [(k, k ^ bit) for k in range(size)])


def bits_of(axis):
    size = lax.axis_size(axis)
    assert size & (size - 1) == 0
    bits, b = [], 1
    while b < size:
        bits.append(b)
        b *= 2
    return bits


def sum_over(x, axis):
    for bit in reversed(bits_of(axis)):
        x = x + swap(x, axis, bit)
    return x


def tied(one, many):
    one, many = lax.optimization_barrier((one, list(many)))
    return one, many


def moments(weight, grad, first, second, decay):
    first_new = beta_one * first + (1.0 - beta_one) * grad
    second_new = beta_two * second + (1.0 - beta_two) * grad * grad
    update = (
        first_new / fix_first / (jnp.sqrt(second_new / fix_second) + small_eps) + decay * weight
    )
    return (first_new, second_new, update)


def per_device(
    patches,
    class_in,
    conv_weight,
    conv_bias,
    head_weight,
    head_bias,
    first_conv_w,
    first_conv_b,
    first_head_w,
    first_head_b,
    second_conv_w,
    second_conv_b,
    second_head_w,
    second_head_b,
    average_conv_w,
    average_conv_b,
    average_head_w,
    average_head_b,
    pooled_cot,
    class_cot,
):
    groups = lax.axis_size(CHAN)
    me = lax.axis_index(CHAN)
    my_id = me.astype(jnp.int32)[None]
    per_dev = conv_weight.shape[0]
    n_in, channels_in = patches.shape[1:]
    n_out, channels = pooled_cot.shape[1:]
    local_images = class_in.shape[1]
    images = local_images * groups
    plan = make_plan(groups, images, n_in, n_out)
    tiles, in_tiles = plan.out_tiles, plan.in_tiles
    width = plan.table.shape[1]
    per = 3
    steps = channels_in // (UNIT * per)
    x = patches[0].T
    cot = pooled_cot[0].T
    in_lanes, out_lanes = round_up(n_in, LANES), round_up(n_out, LANES)
    rows, wide_rows = UNIT * per, 2 * UNIT * per
    x_spec = pl.BlockSpec((rows, in_lanes), lambda g, *tab: (g, 0))
    cot_spec = pl.BlockSpec((wide_rows, out_lanes), lambda g, *tab: (g, 0))
    planes = [2 * op.full + op.half for op in plan.ops]
    halo_specs = [pl.BlockSpec((n, rows, LANES), lambda g, *tab: (0, g, 0)) for n in planes]
    halo_outs = [f32(n, channels_in, LANES) for n in planes]
    planes = [2 * op.full + op.half for op in plan.back_ops]
    back_specs = [pl.BlockSpec((n, rows, LANES), lambda g, *tab: (0, g, 0)) for n in planes]
    back_outs = [f32(n, channels_in, LANES) for n in planes]
    held_spec = pl.BlockSpec((in_tiles + 1, rows, LANES), lambda g, *tab: (0, g, 0))
    split_spec = pl.BlockSpec((tiles, 2, rows, LANES), lambda g, *tab: (0, 0, g, 0))
    own_spec = pl.BlockSpec((tiles, wide_rows, LANES), lambda g, *tab: (0, g, 0))
    w_spec = pl.BlockSpec((wide_rows, LANES), lambda g, *tab: (g, 0))
    anywhere = pl.BlockSpec(memory_space=pl.ANY)
    cot_held = pltpu.VMEM((tiles + 1, 2 * UNIT, LANES), jnp.float32)

    pd_rows = round_up(per_dev, SUBL)
    small_rows = 2 * pd_rows + 4 * local_images
    pieces = [
        conv_weight.T,
        conv_bias[None],
        first_conv_w.T,
        first_conv_b[None],
        second_conv_w.T,
        second_conv_b[None],
        head_bias[None],
        head_weight.T,
        class_in[0],
        class_cot[0],
    ]
    own_specs = [
        *(whole(*p.shape) for p in pieces[:7]),
        whole(pd_rows, 2 * LANES),
        whole(local_images, 2 * LANES),
        whole(local_images, 3 * LANES),
    ]
    small, table = call(
        functools.partial(small_kernel, per_dev),
        [my_id],
        [*pieces, jnp.asarray(plan.table)[:, None]],
        [*own_specs, pl.BlockSpec((None, 1, width), lambda g, tab: (tab[0], 0, 0))],
        [f32(small_rows, LANES), jax.ShapeDtypeStruct((1, width), jnp.int32)],
        [whole(small_rows, LANES), whole(1, width)],
        [pltpu.VMEM((LANES, LANES), jnp.float32)],
        1,
    )

    sends = call(
        functools.partial(pack_kernel, plan),
        [table],
        [cot, small],
        [cot_spec, anywhere],
        halo_outs,
        halo_specs,
        [cot_held],
        steps,
    )
    cot_split = call(
        functools.partial(align_cot_kernel, plan),
        [table],
        [cot, sends[0]],
        [cot_spec, anywhere],
        [f32(tiles, 2, channels_in, LANES)],
        [split_spec],
        [cot_held],
        steps,
    )[0]
    x_held = call(
        functools.partial(align_patches_kernel, plan),
        [table],
        [x, cot_split],
        [x_spec, anywhere],
        [f32(in_tiles + 1, channels_in, LANES)],
        [held_spec],
        [],
        steps,
    )[0]

    sends = list(sends)
    cot_halo = [None] * len(sends)
    parts = small[None]
    rounds = bits_of(CHAN)
    rounds = rounds[:1] + rounds[:0:-1]
    for bit in rounds:
        got = swap(parts, CHAN, bit)
        if bit == 1:
            got, sends = tied(got, sends)
        elif bit == rounds[-1]:
            got, (x_held,) = tied(got, [x_held])
        elif bit == rounds[1]:
            got, (cot_split,) = tied(got, [cot_split])
        parts = jnp.concatenate([parts, got], axis=0)
        if bit == 1:
            parts, sends = tied(parts, sends)
            for n, op in enumerate(plan.ops):
                if op.near:
                    cot_halo[n] = lax.ppermute(sends[n], CHAN, op.pairs)
    parts, sends = tied(parts, sends)
    near = [n for n, op in enumerate(plan.ops) if op.near]
    if near:
        cot_halo[near[0]], sends = tied(cot_halo[near[0]], sends)
    for n, op in enumerate(plan.ops):
        if not op.near:
            cot_halo[n] = lax.ppermute(sends[n], CHAN, op.pairs)
    padded = round_up(channels, LANES)
    wide, turned, class_out, class_grad, grad_h, weight_norms = call(
        functools.partial(spread_kernel, groups, per_dev, rounds),
        [my_id],
        [parts, class_in[0], class_cot[0], x_held],
        [whole(*parts.shape), own_specs[8], own_specs[9], anywhere],
        [
            f32(channels, LANES),
            f32(LANES, padded),
            f32(local_images, channels),
            f32(local_images, channels_in),
            f32(pd_rows, 2 * LANES),
            f32(SUBL, LANES),
        ],
        [
            whole(channels, LANES),
            whole(LANES, padded),
            whole(local_images, channels),
            whole(local_images, channels_in),
            whole(pd_rows, 2 * LANES),
            whole(SUBL, LANES),
        ],
        [
            pltpu.VMEM((padded, LANES), jnp.float32),
            pltpu.VMEM((padded, 2 * LANES), jnp.float32),
            pltpu.VMEM((images, 3 * LANES), jnp.float32),
            pltpu.VMEM((images, 2 * LANES), jnp.float32),
        ],
        1,
    )

    partials = call(
        functools.partial(partial_kernel, plan),
        [table],
        [x_held, wide],
        [held_spec, w_spec],
        back_outs,
        back_specs,
        [pltpu.VMEM((plan.most + 1, 2, UNIT, LANES), jnp.float32)],
        steps,
        tight=True,
    )
    partials, late = list(partials), []
    pooled_halo = [None] * len(partials)
    for n, op in enumerate(plan.back_ops):
        if op.early:
            pooled_halo[n] = lax.ppermute(partials[n], CHAN, op.pairs)
        else:
            late.append(n)
    grad_h = sum_over(grad_h, "dp")
    head_t = head_weight.T
    head_first, head_second, head_update = moments(
        head_t, grad_h[:per_dev, :channels_in], first_head_w.T, second_head_w.T, 0.05
    )
    bias_first, bias_second, bias_update = moments(
        head_bias, grad_h[:per_dev, channels_in], first_head_b, second_head_b, 0.0
    )
    norms = [jnp.sum(head_update**2), jnp.sum(bias_update**2)]

    pooled_own = call(
        functools.partial(forward_kernel, plan),
        [table],
        [x_held, wide, head_update],
        [held_spec, w_spec, anywhere],
        [f32(tiles, channels, LANES)],
        [own_spec],
        [],
        steps,
        tight=True,
    )[0]

    waiting = [partials[n] for n in late]
    waiting, cot_halo, pooled_own, norms = lax.optimization_barrier(
        (waiting, cot_halo, pooled_own, norms)
    )
    for n, v in zip(late, waiting):
        pooled_halo[n] = lax.ppermute(v, CHAN, plan.back_ops[n].pairs)
    cots_held = pltpu.VMEM((tiles + plan.halo + 1, 2, UNIT, LANES), jnp.float32)
    sums = call(
        functools.partial(weights_kernel, plan),
        [table],
        [x_held, cot_split, *cot_halo],
        [held_spec, split_spec, *halo_specs],
        [f32(2 * SUBL, padded)],
        [whole(2 * SUBL, padded)],
        [cots_held, pltpu.VMEM((TAPS + 1, padded, LANES), jnp.float32)],
        steps,
        tight=True,
    )[0]
    x_grad = call(
        functools.partial(patches_kernel, plan),
        [table],
        [cot_split, wide, sums, *cot_halo],
        [split_spec, w_spec, anywhere, *halo_specs],
        [f32(channels_in, n_in)],
        [x_spec],
        [cots_held, pltpu.VMEM((in_tiles + 1, UNIT, LANES), jnp.float32)],
        steps,
        tight=True,
    )[0]
    sums = sum_over(sums, "dp")
    row = lax.broadcasted_iota(jnp.int32, sums.shape, 0)
    lane = lax.broadcasted_iota(jnp.int32, sums.shape, 1)
    for k, v in enumerate(norms):
        sums = jnp.where((row == TAPS + 1) & (lane == k), v, sums)
    for bit in bits_of(CHAN)[::-1]:
        got = swap(sums, CHAN, bit)
        if bit == bits_of(CHAN)[-1]:
            got, (x_grad,) = tied(got, [x_grad])
        sums = sums + got
    conv_shapes = [f32(TAPS, per_dev)] * 4
    head_shapes = [f32(per_dev, channels_in)] * 2
    operands = [
        sums,
        turned,
        weight_norms,
        *pieces[:6],
        average_conv_w.T,
        average_conv_b[None],
        head_t,
        head_update,
        average_head_w.T,
        head_bias[None],
        bias_update[None],
        average_head_b[None],
    ]
    specs = [whole(*v.shape) for v in operands]
    out_shapes = [*conv_shapes, *head_shapes, *[f32(per_dev)] * 6, f32(4)]
    pooled, *new, trust = call(
        functools.partial(last_kernel, plan, channels, per_dev, len(operands)),
        [table, my_id],
        [pooled_own, *pooled_halo, *operands],
        [own_spec, *back_specs, *specs],
        [f32(channels, n_out), *out_shapes],
        [cot_spec, *[whole(*v.shape) for v in out_shapes]],
        [cot_held, pltpu.VMEM((plan.back_halo + 1, 2 * UNIT, LANES), jnp.float32)],
        steps,
        tight=True,
    )
    conv_new, (head_new, head_average), bias_new = new[:4], new[4:6], new[6:]
    return (
        pooled.T[None],
        class_out[None],
        x_grad.T[None],
        class_grad[None],
        *(v.T for v in conv_new),
        *bias_new[:4],
        head_first.T,
        head_second.T,
        head_new.T,
        head_average.T,
        bias_first,
        bias_second,
        *bias_new[4:],
        trust,
    )


def solution(mesh):
    by_row, by_column = P("dp", CHAN, None), P(None, CHAN)
    by_channel, by_name = P(CHAN, None), P(CHAN)
    return jax.shard_map(
        per_device,
        mesh=mesh,
        in_specs=(
            by_row,
            by_row,
            by_channel,
            by_name,
            by_column,
            by_name,
            by_channel,
            by_name,
            by_column,
            by_name,
            by_channel,
            by_name,
            by_column,
            by_name,
            by_channel,
            by_name,
            by_column,
            by_name,
            by_row,
            by_row,
        ),
        out_specs=(
            by_row,
            by_row,
            by_row,
            by_row,
            by_channel,
            by_channel,
            by_channel,
            by_channel,
            by_name,
            by_name,
            by_name,
            by_name,
            by_column,
            by_column,
            by_column,
            by_column,
            by_name,
            by_name,
            by_name,
            by_name,
            P(),
        ),
        check_vma=False,
    )
```
